32 devices in a mesh: ctx: 16 (over z, x, core), shard: 2 (over y).
Axes of the slice: x: 2, y: 2, z: 4, core: 2. Of those that a mesh axis runs over, the one named last changes fastest.
Arguments:
- tokens: bfloat16 [2, 16384, 512], P('shard', 'ctx'), may hold values from -6 to 6
- expert_index: int32 [2, 16384, 8], P('shard', 'ctx'), may hold values from 0 to 23, all different within a row
- first_gain: bfloat16 [512], P('shard'), may hold values from 0.5 to 1.5
- first_shift: bfloat16 [512], P('shard'), may hold values from -0.625 to 0.625
- router_weight: bfloat16 [512, 24], P('shard'), may hold values from -0.125 to 0.125
- query_weight: bfloat16 [512, 1536], P('shard'), may hold values from -0.5 to 0.5
- key_weight: bfloat16 [512, 64], P('shard'), may hold values from -0.25 to 0.25
- value_weight: bfloat16 [512, 64], P('shard'), may hold values from -0.25 to 0.25
- output_weight: bfloat16 [1536, 512], P('shard'), may hold values from -24 to 24
- second_gain: bfloat16 [512], P('shard'), may hold values from 0.5 to 1.5
- second_shift: bfloat16 [512], P('shard'), may hold values from -0.625 to 0.625
- up_weight: bfloat16 [512, 2048], P('shard'), may hold values from -0.25 to 0.25
- up_bias: bfloat16 [2048], P('shard'), may hold values from -0.625 to 0.625
- down_weight: bfloat16 [2048, 512], P('shard'), may hold values from -0.1875 to 0.1875
- down_bias: bfloat16 [512], P('shard'), may hold values from -1.75 to 1.75
- out_grad: bfloat16 [2, 16384, 512], P('shard', 'ctx'), may hold values from -6 to 6
Outputs:
- layer_out: bfloat16 [2, 16384, 512], P('shard', 'ctx')
- tokens_grad: bfloat16 [2, 16384, 512], P('shard', 'ctx')
- first_gain_grad: float32 [512], P('shard')
- first_shift_grad: float32 [512], P('shard')
- router_weight_grad: float32 [512, 24], P('shard')
- query_weight_grad: float32 [512, 1536], P('shard')
- key_weight_grad: float32 [512, 64], P('shard')
- value_weight_grad: float32 [512, 64], P('shard')
- output_weight_grad: float32 [1536, 512], P('shard')
- second_gain_grad: float32 [512], P('shard')
- second_shift_grad: float32 [512], P('shard')
- up_weight_grad: float32 [512, 2048], P('shard')
- up_bias_grad: float32 [2048], P('shard')
- down_weight_grad: float32 [2048, 512], P('shard')
- down_bias_grad: float32 [512], P('shard')
The draws below stay inside these ranges and needn't reach their ends.
Inputs may be any that keep to these rules, and one draw needn't show every extreme that they name: `expert_index`: each token names 8 different experts.
All inputs are finite; a program needn't handle non-finite values.
Results may differ from the reference program's by a relative error of at most 0.017.
Values may be sent and summed in bfloat16 or wider, within the bound.
No kernel may reach another device: no remote copies, remote signals or barrier semaphores. Data moves between devices by JAX's collectives and lax.ppermute only.
A program may use at most 256 MiB of HBM per device.

```python
import math
import jax
import jax.numpy as jnp
from jax import lax

D = 512
HEAD = 64
EXPERTS = 24
TOPK = 8
FF = 2048
PROMPT = 8192
CLEN = 1024
GROUPS = 2
GROUP_TOK = 16384


def block_scale(stream_key, extent, split, low, top_value):
    factor_of = 1.0
    for dim, shards_of in split:
        heights = jax.random.uniform(jax.random.fold_in(jax.random.fold_in(stream_key, 6), dim), (shards_of,), jnp.float32, low / len(split), top_value / len(split))
        factor_of = factor_of * jnp.repeat(jnp.exp(heights), extent[dim] // shards_of).reshape((-1,) + (1,) * (len(extent) - 1 - dim))
    return factor_of


def picks_of(rng, rows, count, top, lift):
    sequence = jax.random.permutation(jax.random.fold_in(rng, 1), count)
    favour = sequence
    for power in range(3):
        favour = favour * favour // count
    favour = favour * lift // count
    lots = jax.random.randint(jax.random.fold_in(rng, 2), (rows, count), 0, 4096) + favour
    fixed_rows = jax.random.permutation(jax.random.fold_in(rng, 3), rows)[jnp.arange(count) % rows]
    lots = jnp.where(jnp.arange(rows)[:, None] == fixed_rows[None, :], 1 << 14, lots)
    score = lots * count + jnp.arange(count)
    return lax.top_k(score.astype(jnp.int32), top)[1].astype(jnp.int32)


def gaussian(own_key, extent, scale, most, cuts=(), held_as=jnp.bfloat16):
    level = block_scale(own_key, extent, cuts, -0.22, 0.18) if cuts else 1.0
    array = jax.random.normal(own_key, extent, jnp.float32) * scale * level
    return jnp.minimum(jnp.maximum(array, -most), most).astype(held_as)


def setup_inputs(seed: int = 0) -> dict:
    splits = jax.random.split(jax.random.key(seed), 17)
    return {
        "tokens": gaussian(splits[0], (GROUPS, GROUP_TOK, D), 1.0, 6.0, ((0, 2), (1, 16))),
        "expert_index": picks_of(splits[1], GROUPS * GROUP_TOK, EXPERTS, TOPK, 0).reshape((GROUPS, GROUP_TOK, TOPK)),
        "first_gain": jnp.clip(1.0 + 0.1 * jax.random.normal(splits[2], (D,), jnp.float32), 0.5, 1.5).astype(jnp.bfloat16),
        "first_shift": gaussian(splits[3], (D,), 0.1, 0.625, ((0, 2),)),
        "router_weight": gaussian(splits[4], (D, EXPERTS), (4 * D) ** -0.5, 0.125, ((0, 2),)),
        "query_weight": gaussian(splits[5], (D, EXPERTS * HEAD), (D // 4) ** -0.5, 0.5, ((0, 2),)),
        "key_weight": gaussian(splits[6], (D, HEAD), D ** -0.5, 0.25, ((0, 2),)),
        "value_weight": gaussian(splits[7], (D, HEAD), D ** -0.5, 0.25, ((0, 2),)),
        "output_weight": gaussian(splits[8], (EXPERTS * HEAD, D), 4.0, 24.0, ((0, 2),)),
        "second_gain": jnp.clip(1.0 + 0.1 * jax.random.normal(splits[9], (D,), jnp.float32), 0.5, 1.5).astype(jnp.bfloat16),
        "second_shift": gaussian(splits[10], (D,), 0.1, 0.625, ((0, 2),)),
        "up_weight": gaussian(splits[11], (D, FF), D ** -0.5, 0.25, ((0, 2),)),
        "up_bias": gaussian(splits[12], (FF,), 0.1, 0.625, ((0, 2),)),
        "down_weight": gaussian(splits[13], (FF, D), (FF // 2) ** -0.5, 0.1875, ((0, 2),)),
        "down_bias": gaussian(splits[14], (D,), 0.3, 1.75, ((0, 2),)),
        "out_grad": gaussian(splits[15], (GROUPS, GROUP_TOK, D), 1.0, 6.0, ((0, 2), (1, 16))),
    }


@jax.custom_vjp
def low(v):
    return lax.optimization_barrier(v.astype(jnp.bfloat16)).astype(jnp.float32)

@jax.custom_vjp
def low_back(v):
    return v

def low_keep(v):
    return (low(v), None)

def low_pass(kept, grad):
    return (grad,)

def back_keep(v):
    return (v, None)

def back_low(kept, grad):
    return (low(grad),)
low.defvjp(low_keep, low_pass)
low_back.defvjp(back_keep, back_low)
norm_eps = 1e-05
mask_fill = -1e+30
highest = lax.Precision.HIGHEST

def layer_norm(values, gain, shift):
    center = lax.optimization_barrier(jnp.mean(values, axis=-1, keepdims=True))
    centred = values - center
    spread = lax.optimization_barrier(jnp.mean(centred * centred, axis=-1, keepdims=True))
    return centred * lax.rsqrt(spread + norm_eps) * gain + shift

def segment_of(position):
    return jnp.where(position < PROMPT, 0, 1 + (position - PROMPT) // CLEN)

def visible(query_pos, key_pos):
    query_seg = segment_of(query_pos)[:, None]
    key_seg = segment_of(key_pos)[None, :]
    return (key_pos[None, :] <= query_pos[:, None]) & ((key_seg == 0) | (key_seg == query_seg))

def attend_group(queries, keys, values):
    rows = math.gcd(GROUP_TOK, 512)
    count = GROUP_TOK // rows
    blocks = queries.reshape(count, rows, TOPK, HEAD)
    starts = jnp.arange(count, dtype=jnp.int32) * rows
    key_pos = jnp.arange(GROUP_TOK, dtype=jnp.int32)
    scale = HEAD ** (-0.5)

    def one_block(operand):
        block, start = operand
        query_pos = start + jnp.arange(rows, dtype=jnp.int32)
        allowed = visible(query_pos, key_pos)[:, None, :]
        raw = jnp.einsum('bhd,kd->bhk', block, keys, precision=highest) * scale
        scores = jnp.where(allowed, low_back(raw), mask_fill)
        probs = low(jax.nn.softmax(scores, axis=-1))
        return jnp.einsum('bhk,kd->bhd', probs, values, precision=highest)
    return lax.map(jax.checkpoint(one_block), (blocks, starts)).reshape(GROUP_TOK, TOPK, HEAD)

def forward(tokens, first_gain, first_shift, router_weight, query_weight, key_weight, value_weight, output_weight, second_gain, second_shift, up_weight, up_bias, down_weight, down_bias, expert_index):
    flat = tokens.reshape(-1, D)
    chosen = expert_index.reshape(-1, TOPK)
    first = low(layer_norm(flat, first_gain, first_shift))
    logits = low_back(jnp.dot(first, router_weight, precision=highest))
    gate = jax.nn.softmax(jnp.take_along_axis(logits, chosen, axis=1), axis=-1)
    projected = jnp.dot(first, query_weight, precision=highest).reshape(-1, EXPERTS, HEAD)
    queries = low_back(low(jnp.take_along_axis(projected, chosen[:, :, None], axis=1)))
    keys = low_back(low(jnp.dot(first, key_weight, precision=highest)))
    values = low_back(low(jnp.dot(first, value_weight, precision=highest)))
    pieces = []
    for group in range(GROUPS):
        begin = group * GROUP_TOK
        pieces.append(attend_group(queries[begin:begin + GROUP_TOK], keys[begin:begin + GROUP_TOK], values[begin:begin + GROUP_TOK]))
    attended = low_back(jnp.concatenate(pieces, axis=0))
    weighted = low(gate[:, :, None] * attended)
    onehot = (chosen[:, :, None] == jnp.arange(EXPERTS, dtype=jnp.int32)[None, None, :]).astype(jnp.float32)
    spread_out = jnp.einsum('tje,tjd->ted', onehot, weighted, precision=highest).reshape(-1, EXPERTS * HEAD)
    middle = flat + low_back(jnp.dot(spread_out, output_weight, precision=highest))
    second = low(layer_norm(middle, second_gain, second_shift))
    hidden = low(jax.nn.gelu(low_back(jnp.dot(second, up_weight, precision=highest) + up_bias), approximate=True))
    result = middle + low_back(jnp.dot(hidden, down_weight, precision=highest) + down_bias)
    return result.reshape(tokens.shape)

def reference(tokens, expert_index, first_gain, first_shift, router_weight, query_weight, key_weight, value_weight, output_weight, second_gain, second_shift, up_weight, up_bias, down_weight, down_bias, out_grad):
    operands = [item.astype(jnp.float32) for item in (tokens, first_gain, first_shift, router_weight, query_weight, key_weight, value_weight, output_weight, second_gain, second_shift, up_weight, up_bias, down_weight, down_bias)]

    def wrapped(*inputs):
        return forward(*inputs, expert_index)
    result, pull = jax.vjp(wrapped, *operands)
    grads = pull(out_grad.astype(jnp.float32))
    return (result.astype(jnp.bfloat16), grads[0].astype(jnp.bfloat16), grads[1], grads[2], grads[3], grads[4], grads[5], grads[6], grads[7], grads[8], grads[9], grads[10], grads[11], grads[12], grads[13])
```

```python
import functools
import math

import jax
import jax.numpy as jnp
from jax import lax
from jax.experimental import pallas as pl
from jax.experimental.pallas import tpu as pltpu
from jax.sharding import PartitionSpec as P

PROMPT = 8192
CLEN = 1024
ROWS = 128
TILE = 256
FULL = 1024
PART = 256
VMEM = 60 << 20

norm_eps = 1e-05
mask_fill = -1e30
LOG2E = math.log2(math.e)
bf16 = jnp.bfloat16
f32 = jnp.float32


def dot(a, b):
    return lax.dot_general(a, b, (((1,), (0,)), ((), ())), preferred_element_type=f32)


def dot_tn(a, b):
    return lax.dot_general(a, b, (((0,), (0,)), ((), ())), preferred_element_type=f32)


def dot_nt(a, b):
    return lax.dot_general(a, b, (((1,), (1,)), ((), ())), preferred_element_type=f32)


def params(**kw):
    return pltpu.CompilerParams(vmem_limit_bytes=VMEM, **kw)


def whole(shape):
    return pl.BlockSpec(shape, lambda i: tuple(0 for _ in shape))


def column_norm(values):
    center = jnp.mean(values, axis=0, keepdims=True)
    centred = values - center
    spread = jnp.mean(centred * centred, axis=0, keepdims=True)
    inverse = lax.rsqrt(spread + norm_eps)
    return centred * inverse, inverse


def column_norm_back(grad, unit, inverse, gain):
    scaled = grad * gain
    inner = (
        scaled
        - jnp.mean(scaled, axis=0, keepdims=True)
        - unit * jnp.mean(scaled * unit, axis=0, keepdims=True)
    )
    return inner * inverse


def fold_lanes(values):
    width = values.shape[1]
    total = values[:, :128]
    for start in range(128, width, 128):
        total = total + values[:, start : start + 128]
    return total


def first_kernel(tokens_ref, gain_ref, shift_ref, kv_weight_ref, first_ref, kv_ref):
    unit, _ = column_norm(tokens_ref[...].astype(f32).T)
    first = (unit * gain_ref[...] + shift_ref[...]).astype(bf16)
    first_ref[...] = first
    kv_ref[...] = dot_tn(kv_weight_ref[...], first).T.astype(bf16)


def first_call(tokens, gain, shift, kv_weight):
    count, width = tokens.shape
    pair = kv_weight.shape[1]
    return pl.pallas_call(
        first_kernel,
        grid=(count // TILE,),
        in_specs=[
            pl.BlockSpec((TILE, width), lambda i: (i, 0)),
            whole((width, 1)),
            whole((width, 1)),
            whole((width, pair)),
        ],
        out_specs=[
            pl.BlockSpec((width, TILE), lambda i: (0, i)),
            pl.BlockSpec((TILE, pair), lambda i: (i, 0)),
        ],
        out_shape=[
            jax.ShapeDtypeStruct((width, count), bf16),
            jax.ShapeDtypeStruct((count, pair), bf16),
        ],
        compiler_params=params(),
        name="first_norm",
    )(tokens, gain, shift, kv_weight)


def query_kernel(first_ref, query_weight_ref, router_ref, index_ref, qt_ref, q_ref, gate_ref):
    topk = index_ref.shape[0]
    head = qt_ref.shape[1]
    experts = query_weight_ref.shape[1] // head
    first = first_ref[...]
    projected = dot_tn(query_weight_ref[...], first)
    logits = dot_tn(router_ref[...], first)
    index = index_ref[...]
    picked = jnp.zeros(index.shape, f32)
    for expert in range(experts):
        picked = jnp.where(index == expert, logits[expert : expert + 1, :], picked)
    picked = jnp.exp(picked - jnp.max(picked, axis=0, keepdims=True))
    gate_ref[...] = picked / jnp.sum(picked, axis=0, keepdims=True)
    for part in range(TILE // ROWS):
        lanes = slice(part * ROWS, (part + 1) * ROWS)
        for j in range(topk):
            row = index[j : j + 1, lanes]
            chosen = jnp.zeros((head, ROWS), f32)
            for expert in range(experts):
                chosen = jnp.where(
                    row == expert, projected[expert * head : (expert + 1) * head, lanes], chosen
                )
            qt_ref[part, :, j * ROWS : (j + 1) * ROWS] = chosen.astype(bf16)
            q_ref[part, j * ROWS : (j + 1) * ROWS, :] = chosen.T.astype(bf16)


def query_call(first, query_weight, router, index, head):
    width, count = first.shape
    topk = index.shape[0]
    tiles = count // ROWS
    per = TILE // ROWS
    return pl.pallas_call(
        query_kernel,
        grid=(count // TILE,),
        in_specs=[
            pl.BlockSpec((width, TILE), lambda i: (0, i)),
            whole(query_weight.shape),
            whole(router.shape),
            pl.BlockSpec((topk, TILE), lambda i: (0, i)),
        ],
        out_specs=[
            pl.BlockSpec((per, head, topk * ROWS), lambda i: (i, 0, 0)),
            pl.BlockSpec((per, topk * ROWS, head), lambda i: (i, 0, 0)),
            pl.BlockSpec((topk, TILE), lambda i: (0, i)),
        ],
        out_shape=[
            jax.ShapeDtypeStruct((tiles, head, topk * ROWS), bf16),
            jax.ShapeDtypeStruct((tiles, topk * ROWS, head), bf16),
            jax.ShapeDtypeStruct((topk, count), f32),
        ],
        compiler_params=params(),
        name="queries",
    )(first, query_weight, router, index)


def tile_ranges(base):
    prompt = base < PROMPT
    steps = jnp.where(prompt, base // FULL, PROMPT // FULL)
    begin = steps * FULL
    position = jnp.where(prompt, begin, PROMPT + (base - PROMPT) // CLEN * CLEN)
    parts = (base + ROWS - position + PART - 1) // PART
    return steps, begin, position, parts


def allowed_mask(position, base, width):
    key_pos = position + lax.broadcasted_iota(jnp.int32, (PART, width), 0)
    query_pos = base + lax.rem(lax.broadcasted_iota(jnp.int32, (PART, width), 1), ROWS)
    return key_pos <= query_pos


def attend_kernel(base_ref, kv_ref, qt_ref, out_ref, lse_ref, vt_ref, knorm_ref, acc_ref, max_ref):
    tile = pl.program_id(0)
    head, width = qt_ref.shape[1:]
    total_keys = kv_ref.shape[0]
    factor = LOG2E * head ** (-0.5)

    @pl.when(tile == 0)
    def _():
        knorm_ref[0] = 0.0

        def turn(i, carry):
            span = pl.ds(pl.multiple_of(i * FULL, FULL), FULL)
            both = kv_ref[span, :].T
            vt_ref[:head, span] = both[head:, :]
            vt_ref[head:, span] = jnp.ones((vt_ref.shape[0] - head, FULL), bf16)
            keys = both[:head, :].astype(f32)
            most = jnp.max(jnp.sum(keys * keys, axis=0, keepdims=True))
            knorm_ref[0] = jnp.maximum(knorm_ref[0], most)
            return carry

        lax.fori_loop(0, total_keys // FULL, turn, 0)

    base = base_ref[tile]
    steps, begin, position, parts = tile_ranges(base)
    query = qt_ref[0].astype(f32)
    qnorm = jnp.max(jnp.sum(query * query, axis=0, keepdims=True))
    narrow = qnorm * knorm_ref[0] * (factor * factor) < 100.0 * 100.0
    acc_ref[...] = jnp.zeros(acc_ref.shape, f32)
    max_ref[...] = jnp.zeros(max_ref.shape, f32)

    def plain(offset, size, mask):
        span = pl.ds(pl.multiple_of(offset, size), size)
        scores = dot(kv_ref[span, :head], qt_ref[0]) * factor
        if mask is not None:
            scores = jnp.where(mask, scores, mask_fill)
        probs = jnp.exp2(scores).astype(bf16)
        acc_ref[...] += dot(vt_ref[:, span], probs)

    @pl.when(narrow)
    def _():
        def step(i, carry):
            plain(i * FULL, FULL, None)
            return carry

        def part(i, carry):
            plain(begin + i * PART, PART, allowed_mask(position + i * PART, base, width))
            return carry

        lax.fori_loop(0, steps, step, 0)
        lax.fori_loop(0, parts, part, 0)

    @pl.when(jnp.logical_not(narrow))
    def _():
        max_ref[...] = jnp.full(max_ref.shape, mask_fill, f32)

        def part(i, carry):
            before = i < steps * (FULL // PART)
            offset = i * PART
            span = pl.ds(pl.multiple_of(offset, PART), PART)
            shifted = jnp.where(before, -(1 << 24), position + offset - begin)
            mask = allowed_mask(shifted, base, width)
            scores = dot(kv_ref[span, :head], qt_ref[0]) * factor
            scores = jnp.where(mask, scores, mask_fill)
            old = max_ref[...]
            new = jnp.maximum(old, jnp.max(scores, axis=0, keepdims=True))
            probs = jnp.where(mask, jnp.exp2(scores - new), 0.0).astype(bf16)
            acc_ref[...] = acc_ref[...] * jnp.exp2(old - new) + dot(vt_ref[:, span], probs)
            max_ref[...] = new
            return carry

        lax.fori_loop(0, steps * (FULL // PART) + parts, part, 0)

    total = acc_ref[head : head + 1, :]
    out_ref[0] = acc_ref[:head, :] / total
    lse_ref[0] = max_ref[...] + jnp.log2(total)


def attend_call(bases, kv, qt):
    tiles, head, width = qt.shape
    total_keys, pair = kv.shape
    return pl.pallas_call(
        attend_kernel,
        grid_spec=pltpu.PrefetchScalarGridSpec(
            num_scalar_prefetch=1,
            grid=(tiles,),
            in_specs=[
                pl.BlockSpec((total_keys, pair), lambda i, b: (0, 0)),
                pl.BlockSpec((1, head, width), lambda i, b: (i, 0, 0)),
            ],
            out_specs=[
                pl.BlockSpec((1, head, width), lambda i, b: (i, 0, 0)),
                pl.BlockSpec((1, 1, width), lambda i, b: (i, 0, 0)),
            ],
            scratch_shapes=[
                pltpu.VMEM((head + 16, total_keys), bf16),
                pltpu.SMEM((1,), f32),
                pltpu.VMEM((head + 16, width), f32),
                pltpu.VMEM((1, width), f32),
            ],
        ),
        out_shape=[
            jax.ShapeDtypeStruct((tiles, head, width), f32),
            jax.ShapeDtypeStruct((tiles, 1, width), f32),
        ],
        compiler_params=params(),
        name="attend",
    )(bases, kv, qt)


def attend_back_kernel(
    base_ref, kv_ref, qt_ref, q_ref, dot_ref, do_ref, lse_ref, delta_ref, dq_ref, dkv_ref, kt_ref
):
    tile = pl.program_id(0)
    head, width = qt_ref.shape[1:]
    total_keys = kv_ref.shape[0]
    scale = head ** (-0.5)

    @pl.when(tile == 0)
    def _():
        def turn(i, carry):
            span = pl.ds(pl.multiple_of(i * FULL, FULL), FULL)
            kt_ref[:, span] = kv_ref[span, :].T[:head, :]
            dkv_ref[span, :] = jnp.zeros((FULL, 2 * head), f32)
            return carry

        lax.fori_loop(0, total_keys // FULL, turn, 0)

    base = base_ref[tile]
    steps, begin, position, parts = tile_ranges(base)
    dq_ref[...] = jnp.zeros(dq_ref.shape, f32)

    def block(offset, size, mask):
        span = pl.ds(pl.multiple_of(offset, size), size)
        scores = dot(kv_ref[span, :head], qt_ref[0]) * (LOG2E * scale) - lse_ref[0]
        probs = jnp.exp2(scores)
        if mask is not None:
            probs = jnp.where(mask, probs, 0.0)
        prob_grad = dot(kv_ref[span, head:], dot_ref[0])
        score_grad = (probs * (prob_grad - delta_ref[0])).astype(bf16)
        dq_ref[0] += dot(kt_ref[:, span], score_grad)
        dkv_ref[span, :head] += dot(score_grad, q_ref[0])
        dkv_ref[span, head:] += dot(probs.astype(bf16), do_ref[0])

    def step(i, carry):
        block(i * FULL, FULL, None)
        return carry

    def part(i, carry):
        block(begin + i * PART, PART, allowed_mask(position + i * PART, base, width))
        return carry

    lax.fori_loop(0, steps, step, 0)
    lax.fori_loop(0, parts, part, 0)
    dq_ref[...] = dq_ref[...] * scale

    @pl.when(tile == pl.num_programs(0) - 1)
    def _():
        def finish(i, carry):
            span = pl.ds(pl.multiple_of(i * FULL, FULL), FULL)
            dkv_ref[span, :head] = dkv_ref[span, :head] * scale
            return carry

        lax.fori_loop(0, total_keys // FULL, finish, 0)


def attend_back_call(bases, kv, qt, q, grad_t, grad, lse, delta):
    tiles, head, width = qt.shape
    total_keys, pair = kv.shape
    one = lambda shape: pl.BlockSpec((1,) + shape, lambda i, b: (i, 0, 0))
    return pl.pallas_call(
        attend_back_kernel,
        grid_spec=pltpu.PrefetchScalarGridSpec(
            num_scalar_prefetch=1,
            grid=(tiles,),
            in_specs=[
                pl.BlockSpec((total_keys, pair), lambda i, b: (0, 0)),
                one((head, width)),
                one((width, head)),
                one((head, width)),
                one((width, head)),
                one((1, width)),
                one((1, width)),
            ],
            out_specs=[
                one((head, width)),
                pl.BlockSpec((total_keys, pair), lambda i, b: (0, 0)),
            ],
            scratch_shapes=[pltpu.VMEM((head, total_keys), bf16)],
        ),
        out_shape=[
            jax.ShapeDtypeStruct((tiles, head, width), f32),
            jax.ShapeDtypeStruct((total_keys, pair), f32),
        ],
        compiler_params=params(),
        name="attend_back",
    )(bases, kv, qt, q, grad_t, grad, lse, delta)


def place(index, pieces, expert):
    total = jnp.zeros(pieces[0].shape, f32)
    for j, piece in enumerate(pieces):
        total = jnp.where(index[j : j + 1, :] == expert, piece, total)
    return total


def middle_kernel(
    tokens_ref,
    grad_ref,
    index_ref,
    gate_ref,
    attended_ref,
    output_weight_ref,
    up_weight_ref,
    down_weight_ref,
    gain_ref,
    shift_ref,
    up_bias_ref,
    down_bias_ref,
    layer_out_ref,
    middle_grad_ref,
    grad_t_ref,
    grad_rows_ref,
    delta_ref,
    logit_grad_ref,
    output_weight_grad_ref,
    up_weight_grad_ref,
    down_weight_grad_ref,
    gain_grad_ref,
    shift_grad_ref,
    up_bias_grad_ref,
    down_bias_grad_ref,
    spread_ref,
    chosen_ref,
    dwo_ref,
    dup_ref,
    ddown_ref,
):
    step = pl.program_id(0)
    topk = index_ref.shape[0]
    head = attended_ref.shape[1]
    experts = output_weight_ref.shape[0] // head
    per = TILE // ROWS

    @pl.when(step == 0)
    def _():
        for ref in (
            dwo_ref,
            dup_ref,
            ddown_ref,
            gain_grad_ref,
            shift_grad_ref,
            up_bias_grad_ref,
            down_bias_grad_ref,
        ):
            ref[...] = jnp.zeros(ref.shape, ref.dtype)

    index = index_ref[...]
    gate = gate_ref[...]
    for part in range(per):
        lanes = slice(part * ROWS, (part + 1) * ROWS)
        pieces = [
            attended_ref[part, :, j * ROWS : (j + 1) * ROWS] * gate[j : j + 1, lanes]
            for j in range(topk)
        ]
        for expert in range(experts):
            spread_ref[expert * head : (expert + 1) * head, lanes] = place(
                index[:, lanes], pieces, expert
            ).astype(bf16)

    middle = tokens_ref[...].astype(f32).T + dot_tn(output_weight_ref[...], spread_ref[...])
    unit, inverse = column_norm(middle)
    second = (unit * gain_ref[...] + shift_ref[...]).astype(bf16)
    pre = dot_tn(up_weight_ref[...], second) + up_bias_ref[...]
    coeff = math.sqrt(2.0 / math.pi)
    square = pre * pre
    wave = jnp.tanh(coeff * pre * (1.0 + 0.044715 * square))
    half = 0.5 * (1.0 + wave)
    hidden = (pre * half).astype(bf16)
    slope = half + 0.5 * pre * (1.0 - wave * wave) * (coeff * (1.0 + 3 * 0.044715 * square))
    result = middle + dot_tn(down_weight_ref[...], hidden) + down_bias_ref[...]
    layer_out_ref[...] = result.T.astype(bf16)

    grad_rows = grad_ref[...]
    grad_wide = grad_rows.astype(f32)
    grad_t = grad_wide.T
    ddown_ref[...] += dot(hidden, grad_rows)
    down_bias_grad_ref[...] += jnp.sum(grad_wide, axis=0, keepdims=True)
    pre_grad = (dot(down_weight_ref[...], grad_t.astype(bf16)) * slope).astype(bf16)
    dup_ref[...] += dot_nt(second, pre_grad)
    up_bias_grad_ref[...] += fold_lanes(pre_grad.astype(f32))
    second_grad = dot(up_weight_ref[...], pre_grad)
    gain_grad_ref[...] += fold_lanes(second_grad * unit)
    shift_grad_ref[...] += fold_lanes(second_grad)
    middle_grad = grad_t + column_norm_back(second_grad, unit, inverse, gain_ref[...])
    middle_grad_ref[...] = middle_grad
    middle_low = middle_grad.astype(bf16)
    dwo_ref[...] += dot_nt(spread_ref[...], middle_low)
    chosen_ref[...] = dot(output_weight_ref[...], middle_low)

    for part in range(per):
        lanes = slice(part * ROWS, (part + 1) * ROWS)
        picks = []
        for j in range(topk):
            span = slice(j * ROWS, (j + 1) * ROWS)
            row = index[j : j + 1, lanes]
            chosen = jnp.zeros((head, ROWS), f32)
            for expert in range(experts):
                chosen = jnp.where(
                    row == expert, chosen_ref[expert * head : (expert + 1) * head, lanes], chosen
                )
            attended = attended_ref[part, :, span]
            picks.append(jnp.sum(chosen * attended, axis=0, keepdims=True))
            back = (chosen * gate[j : j + 1, lanes]).astype(bf16)
            grad_t_ref[part, :, span] = back
            back = back.astype(f32)
            grad_rows_ref[part, span, :] = back.T.astype(bf16)
            delta_ref[part, :, span] = jnp.sum(back * attended, axis=0, keepdims=True)
        gates = [gate[j : j + 1, lanes] for j in range(topk)]
        mean = sum(g * p for g, p in zip(gates, picks))
        rows = [g * (p - mean) for g, p in zip(gates, picks)]
        spare = logit_grad_ref.shape[0] - experts
        logit = [place(index[:, lanes], rows, expert) for expert in range(experts)]
        logit.append(jnp.zeros((spare, ROWS), f32))
        logit_grad_ref[:, lanes] = jnp.concatenate(logit, axis=0).astype(bf16)

    @pl.when(step == pl.num_programs(0) - 1)
    def _():
        output_weight_grad_ref[...] = dwo_ref[...].astype(bf16)
        up_weight_grad_ref[...] = dup_ref[...].astype(bf16)
        down_weight_grad_ref[...] = ddown_ref[...].astype(bf16)


def middle_call(
    tokens, grad, index, gate, attended, output_weight, up_weight, down_weight,
    gain, shift, up_bias, down_bias, padded,
):
    count, width = tokens.shape
    topk = index.shape[0]
    tiles, head, wide = attended.shape
    per = TILE // ROWS
    hidden = up_weight.shape[1]
    spread = output_weight.shape[0]
    rows = pl.BlockSpec((TILE, width), lambda i: (i, 0))
    columns = lambda n: pl.BlockSpec((n, TILE), lambda i: (0, i))
    tile = lambda shape: pl.BlockSpec((per,) + shape, lambda i: (i, 0, 0))
    shape = jax.ShapeDtypeStruct
    return pl.pallas_call(
        middle_kernel,
        grid=(count // TILE,),
        in_specs=[
            rows,
            rows,
            columns(topk),
            columns(topk),
            tile((head, wide)),
            whole(output_weight.shape),
            whole(up_weight.shape),
            whole(down_weight.shape),
            whole((width, 1)),
            whole((width, 1)),
            whole((hidden, 1)),
            whole((width, 1)),
        ],
        out_specs=[
            rows,
            columns(width),
            tile((head, wide)),
            tile((wide, head)),
            tile((1, wide)),
            columns(padded),
            whole(output_weight.shape),
            whole(up_weight.shape),
            whole(down_weight.shape),
            whole((width, 128)),
            whole((width, 128)),
            whole((hidden, 128)),
            whole((1, width)),
        ],
        out_shape=[
            shape((count, width), bf16),
            shape((width, count), f32),
            shape((tiles, head, wide), bf16),
            shape((tiles, wide, head), bf16),
            shape((tiles, 1, wide), f32),
            shape((padded, count), bf16),
            shape(output_weight.shape, bf16),
            shape(up_weight.shape, bf16),
            shape(down_weight.shape, bf16),
            shape((width, 128), f32),
            shape((width, 128), f32),
            shape((hidden, 128), f32),
            shape((1, width), f32),
        ],
        scratch_shapes=[
            pltpu.VMEM((spread, TILE), bf16),
            pltpu.VMEM((spread, TILE), f32),
            pltpu.VMEM(output_weight.shape, f32),
            pltpu.VMEM(up_weight.shape, f32),
            pltpu.VMEM(down_weight.shape, f32),
        ],
        compiler_params=params(),
        name="middle",
    )(tokens, grad, index, gate, attended, output_weight, up_weight, down_weight,
      gain, shift, up_bias, down_bias)


def query_back_kernel(
    first_ref,
    index_ref,
    dq_ref,
    query_weight_ref,
    logit_grad_ref,
    router_ref,
    partial_ref,
    query_weight_grad_ref,
    router_grad_ref,
    placed_ref,
    dwq_ref,
    dr_ref,
):
    step = pl.program_id(0)
    topk = index_ref.shape[0]
    head = dq_ref.shape[1]
    experts = query_weight_ref.shape[1] // head

    @pl.when(step == 0)
    def _():
        dwq_ref[...] = jnp.zeros(dwq_ref.shape, f32)
        dr_ref[...] = jnp.zeros(dr_ref.shape, f32)

    index = index_ref[...]
    for part in range(TILE // ROWS):
        lanes = slice(part * ROWS, (part + 1) * ROWS)
        pieces = [dq_ref[part, :, j * ROWS : (j + 1) * ROWS] for j in range(topk)]
        for expert in range(experts):
            placed_ref[expert * head : (expert + 1) * head, lanes] = place(
                index[:, lanes], pieces, expert
            ).astype(bf16)
    first = first_ref[...]
    dwq_ref[...] += dot_nt(first, placed_ref[...])
    dr_ref[...] += dot_nt(first, logit_grad_ref[...])
    partial_ref[...] = dot(query_weight_ref[...], placed_ref[...]) + dot(
        router_ref[...], logit_grad_ref[...]
    )

    @pl.when(step == pl.num_programs(0) - 1)
    def _():
        query_weight_grad_ref[...] = dwq_ref[...].astype(bf16)
        router_grad_ref[...] = dr_ref[...]


def query_back_call(first, index, dq, query_weight, logit_grad, router):
    width, count = first.shape
    topk = index.shape[0]
    tiles, head, wide = dq.shape
    padded = router.shape[1]
    columns = lambda n: pl.BlockSpec((n, TILE), lambda i: (0, i))
    shape = jax.ShapeDtypeStruct
    return pl.pallas_call(
        query_back_kernel,
        grid=(count // TILE,),
        in_specs=[
            columns(width),
            columns(topk),
            pl.BlockSpec((TILE // ROWS, head, wide), lambda i: (i, 0, 0)),
            whole(query_weight.shape),
            columns(padded),
            whole(router.shape),
        ],
        out_specs=[columns(width), whole(query_weight.shape), whole(router.shape)],
        out_shape=[
            shape((width, count), f32),
            shape(query_weight.shape, bf16),
            shape(router.shape, f32),
        ],
        scratch_shapes=[
            pltpu.VMEM((query_weight.shape[1], TILE), bf16),
            pltpu.VMEM(query_weight.shape, f32),
            pltpu.VMEM(router.shape, f32),
        ],
        compiler_params=params(),
        name="query_back",
    )(first, index, dq, query_weight, logit_grad, router)


def first_back_kernel(
    tokens_ref,
    first_ref,
    partial_ref,
    middle_grad_ref,
    dkv_ref,
    kv_weight_ref,
    gain_ref,
    tokens_grad_ref,
    kv_weight_grad_ref,
    gain_grad_ref,
    shift_grad_ref,
):
    step = pl.program_id(0)

    @pl.when(step == 0)
    def _():
        for ref in (kv_weight_grad_ref, gain_grad_ref, shift_grad_ref):
            ref[...] = jnp.zeros(ref.shape, ref.dtype)

    unit, inverse = column_norm(tokens_ref[...].astype(f32).T)
    dkv = dkv_ref[...]
    kv_weight_grad_ref[...] += dot(first_ref[...], dkv)
    first_grad = partial_ref[...] + dot_nt(kv_weight_ref[...], dkv)
    gain_grad_ref[...] += fold_lanes(first_grad * unit)
    shift_grad_ref[...] += fold_lanes(first_grad)
    total = middle_grad_ref[...] + column_norm_back(first_grad, unit, inverse, gain_ref[...])
    tokens_grad_ref[...] = total.T.astype(bf16)


def first_back_call(tokens, first, partial, middle_grad, dkv, kv_weight, gain):
    count, width = tokens.shape
    pair = kv_weight.shape[1]
    columns = lambda n: pl.BlockSpec((n, TILE), lambda i: (0, i))
    rows = lambda n: pl.BlockSpec((TILE, n), lambda i: (i, 0))
    shape = jax.ShapeDtypeStruct
    return pl.pallas_call(
        first_back_kernel,
        grid=(count // TILE,),
        in_specs=[
            rows(width),
            columns(width),
            columns(width),
            columns(width),
            rows(pair),
            whole(kv_weight.shape),
            whole((width, 1)),
        ],
        out_specs=[rows(width), whole(kv_weight.shape), whole((width, 128)), whole((width, 128))],
        out_shape=[
            shape((count, width), bf16),
            shape(kv_weight.shape, f32),
            shape((width, 128), f32),
            shape((width, 128), f32),
        ],
        compiler_params=params(),
        name="first_back",
    )(tokens, first, partial, middle_grad, dkv, kv_weight, gain)


def join(value):
    count = lax.axis_size("shard")
    if count != 2:
        return lax.all_gather(value, "shard", axis=0, tiled=True)
    other = lax.ppermute(value, "shard", [(0, 1), (1, 0)])
    low = lax.axis_index("shard") == 0
    return jnp.concatenate([jnp.where(low, value, other), jnp.where(low, other, value)], axis=0)


def reduce_parameter(grad):
    part = lax.psum_scatter(grad.astype(bf16), "shard", scatter_dimension=0, tiled=True)
    return lax.psum(part, "ctx").astype(f32)


def per_device(
    tokens,
    expert_index,
    first_gain,
    first_shift,
    router_weight,
    query_weight,
    key_weight,
    value_weight,
    output_weight,
    second_gain,
    second_shift,
    up_weight,
    up_bias,
    down_weight,
    down_bias,
    out_grad,
):
    groups, block, width = tokens.shape
    assert groups == 1
    topk = expert_index.shape[-1]
    experts = router_weight.shape[1]
    head = key_weight.shape[1]
    padded = 32
    spare = jnp.zeros((key_weight.shape[0], padded - experts), bf16)
    vectors = [first_gain, first_shift, second_gain, second_shift, down_bias]
    small = jnp.concatenate(
        [key_weight, value_weight, router_weight, spare] + [v[:, None] for v in vectors], axis=1
    )
    small = join(small)
    kv_weight = small[:, : 2 * head]
    router = small[:, 2 * head : 2 * head + padded]
    columns = [
        small[:, 2 * head + padded + i : 2 * head + padded + i + 1].astype(f32)
        for i in range(len(vectors))
    ]
    gain_one, shift_one, gain_two, shift_two, down_bias_all = columns
    query_all = join(query_weight)
    output_all = join(output_weight)
    up_all = join(up_weight)
    down_all = join(down_weight)
    up_bias_all = join(up_bias).astype(f32)[:, None]

    flat = tokens[0]
    grad = out_grad[0]
    index = expert_index[0].T
    first, kv = first_call(flat, gain_one, shift_one, kv_weight)
    gathered = lax.all_gather(kv, "ctx", axis=0, tiled=True)
    qt, q, gate = query_call(first, query_all, router, index, head)
    base = lax.axis_index("ctx") * block
    bases = base + jnp.arange(block // ROWS, dtype=jnp.int32) * ROWS
    segment = jnp.maximum(base, PROMPT) // CLEN * CLEN
    keys = jnp.concatenate(
        [gathered[:PROMPT], lax.dynamic_slice_in_dim(gathered, segment, CLEN, 0)], axis=0
    )
    attended, lse = attend_call(bases, keys, qt)
    (
        layer_out, middle_grad, grad_t, grad_rows, delta, logit_grad,
        output_weight_grad, up_weight_grad, down_weight_grad,
        second_gain_grad, second_shift_grad, up_bias_grad, down_bias_grad,
    ) = middle_call(
        flat, grad, index, gate, attended, output_all, up_all, down_all,
        gain_two, shift_two, up_bias_all, down_bias_all, padded,
    )
    output_weight_grad = reduce_parameter(output_weight_grad)
    up_weight_grad = reduce_parameter(up_weight_grad)
    down_weight_grad = reduce_parameter(down_weight_grad)
    dq, dkeys = attend_back_call(bases, keys, qt, q, grad_t, grad_rows, lse, delta)
    dall = jnp.concatenate(
        [dkeys[:PROMPT], jnp.zeros((gathered.shape[0] - PROMPT, 2 * head), f32)], axis=0
    )
    dall = lax.dynamic_update_slice_in_dim(
        dall, jnp.where(base >= PROMPT, dkeys[PROMPT:], 0.0), segment, 0
    )
    dkv = lax.psum_scatter(dall.astype(bf16), "ctx", scatter_dimension=0, tiled=True)
    partial, query_weight_grad, router_grad = query_back_call(
        first, index, dq, query_all, logit_grad, router
    )
    query_weight_grad = reduce_parameter(query_weight_grad)
    tokens_grad, kv_weight_grad, first_gain_grad, first_shift_grad = first_back_call(
        flat, first, partial, middle_grad, dkv, kv_weight, gain_one
    )
    vector_grads = [
        jnp.sum(first_gain_grad, axis=1),
        jnp.sum(first_shift_grad, axis=1),
        jnp.sum(second_gain_grad, axis=1),
        jnp.sum(second_shift_grad, axis=1),
        down_bias_grad[0],
    ]
    small_grad = jnp.concatenate(
        [kv_weight_grad, router_grad] + [v[:, None] for v in vector_grads], axis=1
    )
    small_grad = reduce_parameter(small_grad)
    up_bias_grad = reduce_parameter(jnp.sum(up_bias_grad, axis=1))
    at = 2 * head + padded
    return (
        layer_out[None],
        tokens_grad[None],
        small_grad[:, at],
        small_grad[:, at + 1],
        small_grad[:, 2 * head : 2 * head + experts],
        query_weight_grad,
        small_grad[:, :head],
        small_grad[:, head : 2 * head],
        output_weight_grad,
        small_grad[:, at + 2],
        small_grad[:, at + 3],
        up_weight_grad,
        up_bias_grad,
        down_weight_grad,
        small_grad[:, at + 4],
    )


def solution(mesh):
    split = P("shard", "ctx", None)
    vector = P("shard")
    matrix = P("shard", None)
    in_specs = (
        split, split, vector, vector, matrix, matrix, matrix, matrix, matrix,
        vector, vector, matrix, vector, matrix, vector, split,
    )
    out_specs = (
        split, split, vector, vector, matrix, matrix, matrix, matrix, matrix,
        vector, vector, matrix, vector, matrix, vector,
    )
    return jax.shard_map(
        per_device, mesh=mesh, in_specs=in_specs, out_specs=out_specs, check_vma=False
    )
```

```python
import functools
import math

import jax
import jax.numpy as jnp
from jax import lax
from jax.experimental import pallas as pl
from jax.experimental.pallas import tpu as pltpu
from jax.sharding import PartitionSpec as P

PROMPT = 8192
CLEN = 1024
ROWS = 128
TILE = 256
FULL = 1024
PART = 256
HALF = PROMPT // 2
VMEM = 60 << 20

norm_eps = 1e-05
mask_fill = -1e30
LOG2E = math.log2(math.e)
bf16 = jnp.bfloat16
f32 = jnp.float32


def dot(a, b):
    return lax.dot_general(a, b, (((1,), (0,)), ((), ())), preferred_element_type=f32)


def dot_tn(a, b):
    return lax.dot_general(a, b, (((0,), (0,)), ((), ())), preferred_element_type=f32)


def dot_nt(a, b):
    return lax.dot_general(a, b, (((1,), (1,)), ((), ())), preferred_element_type=f32)


def params(**kw):
    return pltpu.CompilerParams(vmem_limit_bytes=VMEM, **kw)


def cost(us):
    return pl.CostEstimate(flops=int(us * 1.15e9), transcendentals=0, bytes_accessed=0)


def whole(shape):
    return pl.BlockSpec(shape, lambda i: tuple(0 for _ in shape))


def column_norm(values):
    center = jnp.mean(values, axis=0, keepdims=True)
    centred = values - center
    spread = jnp.mean(centred * centred, axis=0, keepdims=True)
    inverse = lax.rsqrt(spread + norm_eps)
    return centred * inverse, inverse


def column_norm_back(grad, unit, inverse, gain):
    scaled = grad * gain
    inner = (
        scaled
        - jnp.mean(scaled, axis=0, keepdims=True)
        - unit * jnp.mean(scaled * unit, axis=0, keepdims=True)
    )
    return inner * inverse


def fold_lanes(values):
    width = values.shape[1]
    total = values[:, :128]
    for start in range(128, width, 128):
        total = total + values[:, start : start + 128]
    return total


def first_kernel(tokens_ref, gain_ref, shift_ref, kv_weight_ref, first_ref, kv_ref):
    unit, _ = column_norm(tokens_ref[...].astype(f32).T)
    first = (unit * gain_ref[...] + shift_ref[...]).astype(bf16)
    first_ref[...] = first
    kv_ref[...] = dot_tn(kv_weight_ref[...], first).T.astype(bf16)


def first_call(tokens, gain, shift, kv_weight):
    count, width = tokens.shape
    pair = kv_weight.shape[1]
    return pl.pallas_call(
        first_kernel,
        grid=(count // TILE,),
        in_specs=[
            pl.BlockSpec((TILE, width), lambda i: (i, 0)),
            whole((width, 1)),
            whole((width, 1)),
            whole((width, pair)),
        ],
        out_specs=[
            pl.BlockSpec((width, TILE), lambda i: (0, i)),
            pl.BlockSpec((TILE, pair), lambda i: (i, 0)),
        ],
        out_shape=[
            jax.ShapeDtypeStruct((width, count), bf16),
            jax.ShapeDtypeStruct((count, pair), bf16),
        ],
        compiler_params=params(),
        cost_estimate=cost(5),
        name="first_norm",
    )(tokens, gain, shift, kv_weight)


def join_rows(shard, own_ref, other_ref, all_ref):
    half = own_ref.shape[0]
    all_ref[pl.ds(pl.multiple_of(shard * half, half), half), :] = own_ref[...]
    all_ref[pl.ds(pl.multiple_of((1 - shard) * half, half), half), :] = other_ref[...]


def query_kernel(
    shard_ref, first_ref, own_ref, other_ref, router_ref, index_ref,
    qt_ref, q_ref, gate_ref, query_weight_ref,
):
    topk = index_ref.shape[0]

    @pl.when(pl.program_id(0) == 0)
    def _():
        join_rows(shard_ref[0], own_ref, other_ref, query_weight_ref)

    head = qt_ref.shape[1]
    experts = query_weight_ref.shape[1] // head
    first = first_ref[...]
    projected = dot_tn(query_weight_ref[...], first)
    logits = dot_tn(router_ref[...], first)
    index = index_ref[...]
    picked = jnp.zeros(index.shape, f32)
    for expert in range(experts):
        picked = jnp.where(index == expert, logits[expert : expert + 1, :], picked)
    picked = jnp.exp(picked - jnp.max(picked, axis=0, keepdims=True))
    gate_ref[...] = picked / jnp.sum(picked, axis=0, keepdims=True)
    for part in range(TILE // ROWS):
        lanes = slice(part * ROWS, (part + 1) * ROWS)
        for j in range(topk):
            row = index[j : j + 1, lanes]
            chosen = jnp.zeros((head, ROWS), f32)
            for expert in range(experts):
                chosen = jnp.where(
                    row == expert, projected[expert * head : (expert + 1) * head, lanes], chosen
                )
            qt_ref[part, :, j * ROWS : (j + 1) * ROWS] = chosen.astype(bf16)
            q_ref[part, j * ROWS : (j + 1) * ROWS, :] = chosen.T.astype(bf16)


def query_call(shard, first, own, other, router, index, head):
    width, count = first.shape
    topk = index.shape[0]
    tiles = count // ROWS
    per = TILE // ROWS
    keep = lambda shape: pl.BlockSpec(shape, lambda i, s: (0, 0))
    return pl.pallas_call(
        query_kernel,
        grid_spec=pltpu.PrefetchScalarGridSpec(
            num_scalar_prefetch=1,
            grid=(count // TILE,),
            in_specs=[
                pl.BlockSpec((width, TILE), lambda i, s: (0, i)),
                keep(own.shape),
                keep(other.shape),
                keep(router.shape),
                pl.BlockSpec((topk, TILE), lambda i, s: (0, i)),
            ],
            out_specs=[
                pl.BlockSpec((per, head, topk * ROWS), lambda i, s: (i, 0, 0)),
                pl.BlockSpec((per, topk * ROWS, head), lambda i, s: (i, 0, 0)),
                pl.BlockSpec((topk, TILE), lambda i, s: (0, i)),
            ],
            scratch_shapes=[pltpu.VMEM((width, own.shape[1]), bf16)],
        ),
        out_shape=[
            jax.ShapeDtypeStruct((tiles, head, topk * ROWS), bf16),
            jax.ShapeDtypeStruct((tiles, topk * ROWS, head), bf16),
            jax.ShapeDtypeStruct((topk, count), f32),
        ],
        compiler_params=params(),
        cost_estimate=cost(10),
        name="queries",
    )(shard, first, own, other, router, index)


def tile_ranges(base, origin, segment):
    prompt = base < PROMPT
    seen = jnp.clip(base // FULL * FULL - origin, 0, HALF)
    begin = jnp.where(prompt, seen, HALF)
    position = jnp.where(prompt, origin + seen, PROMPT + (base - PROMPT) // CLEN * CLEN)
    inside = prompt & (base >= origin) & (base < origin + HALF)
    if segment:
        inside = inside | jnp.logical_not(prompt)
    parts = jnp.where(inside, (base + ROWS - position + PART - 1) // PART, 0)
    return begin // FULL, begin, position, parts


def allowed_mask(position, base, width):
    key_pos = position + lax.broadcasted_iota(jnp.int32, (PART, width), 0)
    query_pos = base + lax.rem(lax.broadcasted_iota(jnp.int32, (PART, width), 1), ROWS)
    return key_pos <= query_pos


def for_slots(refs, table_ref, visit):
    slot = 0
    for ref in refs:
        for row in range(0, ref.shape[0], PART):
            place_of = pl.multiple_of(table_ref[slot] * PART, PART)
            visit(ref, row, pl.ds(place_of, PART))
            slot += 1


def attend_kernel(origin, buffers, first, last, base_ref, table_ref, *refs):
    sources = refs[:buffers]
    qt_ref = refs[buffers]
    refs = refs[buffers + 1 :]
    if not first:
        acc_in_ref, max_in_ref = refs[:2]
        refs = refs[2:]
    out_ref, lse_ref, kv_ref, vt_ref, knorm_ref, acc_ref, max_ref = refs
    tile = pl.program_id(0)
    head, width = qt_ref.shape[1:]
    factor = LOG2E * head ** (-0.5)

    @pl.when(tile == 0)
    def _():
        knorm_ref[0] = 0.0

        def turn(ref, row, span):
            rows = ref[row : row + PART, :]
            kv_ref[span, :] = rows
            both = rows.T
            vt_ref[:head, span] = both[head:, :]
            vt_ref[head:, span] = jnp.ones((vt_ref.shape[0] - head, PART), bf16)
            keys = both[:head, :].astype(f32)
            most = jnp.max(jnp.sum(keys * keys, axis=0, keepdims=True))
            knorm_ref[0] = jnp.maximum(knorm_ref[0], most)

        for_slots(sources, table_ref, turn)

    base = base_ref[tile]
    steps, begin, position, parts = tile_ranges(base, origin, buffers > 2)
    query = qt_ref[0].astype(f32)
    qnorm = jnp.max(jnp.sum(query * query, axis=0, keepdims=True))
    narrow = qnorm * knorm_ref[0] * (factor * factor) < 100.0 * 100.0
    if first:
        acc_ref[...] = jnp.zeros(acc_ref.shape, f32)
        max_ref[...] = jnp.full(max_ref.shape, jnp.where(narrow, 0.0, mask_fill), f32)
    else:
        acc_ref[...] = acc_in_ref[0]
        max_ref[...] = max_in_ref[0]
        narrow = narrow & (jnp.max(jnp.abs(max_in_ref[0])) == 0.0)

    def plain(offset, size, mask):
        span = pl.ds(pl.multiple_of(offset, size), size)
        scores = dot(kv_ref[span, :head], qt_ref[0]) * factor
        if mask is not None:
            scores = jnp.where(mask, scores, mask_fill)
        probs = jnp.exp2(scores).astype(bf16)
        acc_ref[...] += dot(vt_ref[:, span], probs)

    @pl.when(narrow)
    def _():
        def step(i, carry):
            plain(i * FULL, FULL, None)
            return carry

        def part(i, carry):
            plain(begin + i * PART, PART, allowed_mask(position + i * PART, base, width))
            return carry

        lax.fori_loop(0, steps, step, 0)
        lax.fori_loop(0, parts, part, 0)

    @pl.when(jnp.logical_not(narrow))
    def _():
        def part(i, carry):
            before = i < steps * (FULL // PART)
            offset = i * PART
            span = pl.ds(pl.multiple_of(offset, PART), PART)
            shifted = jnp.where(before, -(1 << 24), position + offset - begin)
            mask = allowed_mask(shifted, base, width)
            scores = dot(kv_ref[span, :head], qt_ref[0]) * factor
            scores = jnp.where(mask, scores, mask_fill)
            old = max_ref[...]
            new = jnp.maximum(old, jnp.max(scores, axis=0, keepdims=True))
            probs = jnp.where(mask, jnp.exp2(scores - new), 0.0).astype(bf16)
            acc_ref[...] = acc_ref[...] * jnp.exp2(old - new) + dot(vt_ref[:, span], probs)
            max_ref[...] = new
            return carry

        lax.fori_loop(0, steps * (FULL // PART) + parts, part, 0)

    if last:
        total = acc_ref[head : head + 1, :]
        out_ref[0] = acc_ref[:head, :] / total
        lse_ref[0] = max_ref[...] + jnp.log2(total)
    else:
        out_ref[0] = acc_ref[...]
        lse_ref[0] = max_ref[...]


def attend_call(origin, sources, table, bases, qt, state=None, last=False):
    tiles, head, width = qt.shape
    total_keys = sum(x.shape[0] for x in sources)
    pair = sources[0].shape[1]
    rows = head if last else head + 16
    one = lambda shape: pl.BlockSpec((1,) + shape, lambda i, b, t: (i, 0, 0))
    keep = lambda x: pl.BlockSpec(x.shape, lambda i, b, t: (0, 0))
    state = () if state is None else tuple(state)
    body = functools.partial(attend_kernel, origin, len(sources), not state, last)
    return pl.pallas_call(
        body,
        grid_spec=pltpu.PrefetchScalarGridSpec(
            num_scalar_prefetch=2,
            grid=(tiles,),
            in_specs=[keep(x) for x in sources]
            + [one((head, width))]
            + ([one((head + 16, width)), one((1, width))] if state else []),
            out_specs=[one((rows, width)), one((1, width))],
            scratch_shapes=[
                pltpu.VMEM((total_keys, pair), bf16),
                pltpu.VMEM((head + 16, total_keys), bf16),
                pltpu.SMEM((1,), f32),
                pltpu.VMEM((head + 16, width), f32),
                pltpu.VMEM((1, width), f32),
            ],
        ),
        out_shape=[
            jax.ShapeDtypeStruct((tiles, rows, width), f32),
            jax.ShapeDtypeStruct((tiles, 1, width), f32),
        ],
        compiler_params=params(),
        cost_estimate=cost(33),
        name="attend",
    )(bases, table, *sources, qt, *state)


def attend_back_kernel(origin, buffers, first, base_ref, table_ref, *refs):
    sources = refs[:buffers]
    qt_ref, q_ref, dot_ref, do_ref, lse_ref, delta_ref = refs[buffers : buffers + 6]
    refs = refs[buffers + 6 :]
    if not first:
        dq_in_ref = refs[0]
        refs = refs[1:]
    dq_ref = refs[0]
    outs = refs[1 : 1 + buffers]
    kv_ref, kt_ref, dkv_ref = refs[1 + buffers :]
    tile = pl.program_id(0)
    head, width = qt_ref.shape[1:]
    scale = head ** (-0.5)

    @pl.when(tile == 0)
    def _():
        def turn(ref, row, span):
            rows = ref[row : row + PART, :]
            kv_ref[span, :] = rows
            kt_ref[:, span] = rows.T[:head, :]
            dkv_ref[span, :] = jnp.zeros((PART, 2 * head), f32)

        for_slots(sources, table_ref, turn)

    base = base_ref[tile]
    steps, begin, position, parts = tile_ranges(base, origin, buffers > 2)
    dq_ref[...] = jnp.zeros(dq_ref.shape, f32) if first else dq_in_ref[...]

    def block(offset, size, mask):
        span = pl.ds(pl.multiple_of(offset, size), size)
        scores = dot(kv_ref[span, :head], qt_ref[0]) * (LOG2E * scale) - lse_ref[0]
        probs = jnp.exp2(scores)
        if mask is not None:
            probs = jnp.where(mask, probs, 0.0)
        prob_grad = dot(kv_ref[span, head:], dot_ref[0])
        score_grad = (probs * (prob_grad - delta_ref[0])).astype(bf16)
        dq_ref[0] += dot(kt_ref[:, span], score_grad) * scale
        dkv_ref[span, :head] += dot(score_grad, q_ref[0])
        dkv_ref[span, head:] += dot(probs.astype(bf16), do_ref[0])

    def step(i, carry):
        block(i * FULL, FULL, None)
        return carry

    def part(i, carry):
        block(begin + i * PART, PART, allowed_mask(position + i * PART, base, width))
        return carry

    lax.fori_loop(0, steps, step, 0)
    lax.fori_loop(0, parts, part, 0)

    @pl.when(tile == pl.num_programs(0) - 1)
    def _():
        lane = lax.broadcasted_iota(jnp.int32, (PART, 2 * head), 1)
        both = jnp.where(lane < head, scale, 1.0)

        def finish(ref, row, span):
            ref[row : row + PART, :] = (dkv_ref[span, :] * both).astype(ref.dtype)

        for_slots(outs, table_ref, finish)


def attend_back_call(origin, sources, kinds, table, bases, qt, q, grad_t, grad, lse, delta, dq=None):
    tiles, head, width = qt.shape
    total_keys = sum(x.shape[0] for x in sources)
    pair = sources[0].shape[1]
    one = lambda shape: pl.BlockSpec((1,) + shape, lambda i, b, t: (i, 0, 0))
    keep = lambda x: pl.BlockSpec(x.shape, lambda i, b, t: (0, 0))
    extra = () if dq is None else (dq,)
    return pl.pallas_call(
        functools.partial(attend_back_kernel, origin, len(sources), dq is None),
        grid_spec=pltpu.PrefetchScalarGridSpec(
            num_scalar_prefetch=2,
            grid=(tiles,),
            in_specs=[keep(x) for x in sources]
            + [
                one((head, width)),
                one((width, head)),
                one((head, width)),
                one((width, head)),
                one((1, width)),
                one((1, width)),
            ]
            + [one((head, width)) for _ in extra],
            out_specs=[one((head, width))] + [keep(x) for x in sources],
            scratch_shapes=[
                pltpu.VMEM((total_keys, pair), bf16),
                pltpu.VMEM((head, total_keys), bf16),
                pltpu.VMEM((total_keys, pair), f32),
            ],
        ),
        out_shape=[jax.ShapeDtypeStruct((tiles, head, width), f32)]
        + [jax.ShapeDtypeStruct(x.shape, kind) for x, kind in zip(sources, kinds)],
        compiler_params=params(),
        cost_estimate=cost(80),
        name="attend_back",
    )(bases, table, *sources, qt, q, grad_t, grad, lse, delta, *extra)


def place(index, pieces, expert):
    total = jnp.zeros(pieces[0].shape, f32)
    for j, piece in enumerate(pieces):
        total = jnp.where(index[j : j + 1, :] == expert, piece, total)
    return total


def middle_kernel(
    shard_ref,
    tokens_ref,
    grad_ref,
    index_ref,
    gate_ref,
    attended_ref,
    output_own_ref,
    output_other_ref,
    up_own_ref,
    up_other_ref,
    down_own_ref,
    down_other_ref,
    gain_ref,
    shift_ref,
    up_bias_ref,
    down_bias_ref,
    layer_out_ref,
    middle_grad_ref,
    grad_t_ref,
    grad_rows_ref,
    delta_ref,
    logit_grad_ref,
    keep_ref,
    send_ref,
    gain_grad_ref,
    shift_grad_ref,
    up_bias_grad_ref,
    down_bias_grad_ref,
    output_weight_ref,
    up_weight_ref,
    down_weight_ref,
    spread_ref,
    chosen_ref,
    dwo_ref,
    dup_ref,
    ddown_ref,
):
    step = pl.program_id(0)
    topk = index_ref.shape[0]
    head = attended_ref.shape[1]
    experts = output_weight_ref.shape[0] // head
    per = TILE // ROWS

    @pl.when(step == 0)
    def _():
        shard = shard_ref[0]
        join_rows(shard, output_own_ref, output_other_ref, output_weight_ref)
        join_rows(shard, up_own_ref, up_other_ref, up_weight_ref)
        join_rows(shard, down_own_ref, down_other_ref, down_weight_ref)
        for ref in (
            dwo_ref,
            dup_ref,
            ddown_ref,
            gain_grad_ref,
            shift_grad_ref,
            up_bias_grad_ref,
            down_bias_grad_ref,
        ):
            ref[...] = jnp.zeros(ref.shape, ref.dtype)

    index = index_ref[...]
    gate = gate_ref[...]
    for part in range(per):
        lanes = slice(part * ROWS, (part + 1) * ROWS)
        pieces = [
            attended_ref[part, :, j * ROWS : (j + 1) * ROWS] * gate[j : j + 1, lanes]
            for j in range(topk)
        ]
        for expert in range(experts):
            spread_ref[expert * head : (expert + 1) * head, lanes] = place(
                index[:, lanes], pieces, expert
            ).astype(bf16)

    middle = tokens_ref[...].astype(f32).T + dot_tn(output_weight_ref[...], spread_ref[...])
    unit, inverse = column_norm(middle)
    second = (unit * gain_ref[...] + shift_ref[...]).astype(bf16)
    pre = dot_tn(up_weight_ref[...], second) + up_bias_ref[...]
    coeff = math.sqrt(2.0 / math.pi)
    square = pre * pre
    wave = jnp.tanh(coeff * pre * (1.0 + 0.044715 * square))
    half = 0.5 * (1.0 + wave)
    hidden = (pre * half).astype(bf16)
    slope = half + 0.5 * pre * (1.0 - wave * wave) * (coeff * (1.0 + 3 * 0.044715 * square))
    result = middle + dot_tn(down_weight_ref[...], hidden) + down_bias_ref[...]
    layer_out_ref[...] = result.T.astype(bf16)

    grad_rows = grad_ref[...]
    grad_wide = grad_rows.astype(f32)
    grad_t = grad_wide.T
    ddown_ref[...] += dot(hidden, grad_rows)
    down_bias_grad_ref[...] += jnp.sum(grad_wide, axis=0, keepdims=True)
    pre_grad = (dot(down_weight_ref[...], grad_t.astype(bf16)) * slope).astype(bf16)
    dup_ref[...] += dot_nt(second, pre_grad)
    up_bias_grad_ref[...] += fold_lanes(pre_grad.astype(f32))
    second_grad = dot(up_weight_ref[...], pre_grad)
    gain_grad_ref[...] += fold_lanes(second_grad * unit)
    shift_grad_ref[...] += fold_lanes(second_grad)
    middle_grad = grad_t + column_norm_back(second_grad, unit, inverse, gain_ref[...])
    middle_grad_ref[...] = middle_grad
    middle_low = middle_grad.astype(bf16)
    dwo_ref[...] += dot_nt(spread_ref[...], middle_low)
    chosen_ref[...] = dot(output_weight_ref[...], middle_low)

    for part in range(per):
        lanes = slice(part * ROWS, (part + 1) * ROWS)
        picks = []
        for j in range(topk):
            span = slice(j * ROWS, (j + 1) * ROWS)
            row = index[j : j + 1, lanes]
            chosen = jnp.zeros((head, ROWS), f32)
            for expert in range(experts):
                chosen = jnp.where(
                    row == expert, chosen_ref[expert * head : (expert + 1) * head, lanes], chosen
                )
            attended = attended_ref[part, :, span]
            picks.append(jnp.sum(chosen * attended, axis=0, keepdims=True))
            back = (chosen * gate[j : j + 1, lanes]).astype(bf16)
            grad_t_ref[part, :, span] = back
            back = back.astype(f32)
            grad_rows_ref[part, span, :] = back.T.astype(bf16)
            delta_ref[part, :, span] = jnp.sum(back * attended, axis=0, keepdims=True)
        gates = [gate[j : j + 1, lanes] for j in range(topk)]
        mean = sum(g * p for g, p in zip(gates, picks))
        rows = [g * (p - mean) for g, p in zip(gates, picks)]
        spare = logit_grad_ref.shape[0] - experts
        logit = [place(index[:, lanes], rows, expert) for expert in range(experts)]
        logit.append(jnp.zeros((spare, ROWS), f32))
        logit_grad_ref[:, lanes] = jnp.concatenate(logit, axis=0).astype(bf16)

    @pl.when(step == pl.num_programs(0) - 1)
    def _():
        for target, part in ((keep_ref, shard_ref[0]), (send_ref, 1 - shard_ref[0])):
            place_of = 0
            for ref in (dwo_ref, ddown_ref, dup_ref):
                half = ref.shape[0] // 2
                rows = pl.ds(pl.multiple_of(part * half, half), half)
                for column in range(0, ref.shape[1], target.shape[1]):
                    span = slice(column, column + target.shape[1])
                    target[place_of : place_of + half, :] = ref[rows, span].astype(bf16)
                    place_of += half


def middle_call(
    shard, tokens, grad, index, gate, attended, weights, gain, shift, up_bias, down_bias, padded
):
    count, width = tokens.shape
    topk = index.shape[0]
    tiles, head, wide = attended.shape
    per = TILE // ROWS
    spread = 2 * weights[0].shape[0]
    hidden = weights[2].shape[1]
    sent = spread // 2 + hidden
    keep = lambda shape: pl.BlockSpec(shape, lambda i, s: tuple(0 for _ in shape))
    rows = pl.BlockSpec((TILE, width), lambda i, s: (i, 0))
    columns = lambda n: pl.BlockSpec((n, TILE), lambda i, s: (0, i))
    tile = lambda shape: pl.BlockSpec((per,) + shape, lambda i, s: (i, 0, 0))
    shape = jax.ShapeDtypeStruct
    return pl.pallas_call(
        middle_kernel,
        grid_spec=pltpu.PrefetchScalarGridSpec(
            num_scalar_prefetch=1,
            grid=(count // TILE,),
            in_specs=[rows, rows, columns(topk), columns(topk), tile((head, wide))]
            + [keep(w.shape) for w in weights]
            + [keep((width, 1)), keep((width, 1)), keep((hidden, 1)), keep((width, 1))],
            out_specs=[
                rows,
                columns(width),
                tile((head, wide)),
                tile((wide, head)),
                tile((1, wide)),
                columns(padded),
                keep((sent, width)),
                keep((sent, width)),
                keep((width, 128)),
                keep((width, 128)),
                keep((hidden, 128)),
                keep((1, width)),
            ],
            scratch_shapes=[
                pltpu.VMEM((spread, width), bf16),
                pltpu.VMEM((width, hidden), bf16),
                pltpu.VMEM((hidden, width), bf16),
                pltpu.VMEM((spread, TILE), bf16),
                pltpu.VMEM((spread, TILE), f32),
                pltpu.VMEM((spread, width), f32),
                pltpu.VMEM((width, hidden), f32),
                pltpu.VMEM((hidden, width), f32),
            ],
        ),
        out_shape=[
            shape((count, width), bf16),
            shape((width, count), f32),
            shape((tiles, head, wide), bf16),
            shape((tiles, wide, head), bf16),
            shape((tiles, 1, wide), f32),
            shape((padded, count), bf16),
            shape((sent, width), bf16),
            shape((sent, width), bf16),
            shape((width, 128), f32),
            shape((width, 128), f32),
            shape((hidden, 128), f32),
            shape((1, width), f32),
        ],
        compiler_params=params(),
        cost_estimate=cost(44),
        name="middle",
    )(shard, tokens, grad, index, gate, attended, *weights, gain, shift, up_bias, down_bias)


def query_back_kernel(
    place_ref,
    first_ref,
    index_ref,
    dq_ref,
    own_ref,
    other_ref,
    logit_grad_ref,
    router_ref,
    partial_ref,
    keep_ref,
    send_ref,
    router_grad_ref,
    query_weight_ref,
    placed_ref,
    dwq_ref,
    dr_ref,
):
    step = pl.program_id(0)
    topk = index_ref.shape[0]
    head = dq_ref.shape[1]
    experts = query_weight_ref.shape[1] // head

    @pl.when(step == 0)
    def _():
        join_rows(place_ref[0], own_ref, other_ref, query_weight_ref)
        dwq_ref[...] = jnp.zeros(dwq_ref.shape, f32)
        dr_ref[...] = jnp.zeros(dr_ref.shape, f32)

    index = index_ref[...]
    for part in range(TILE // ROWS):
        lanes = slice(part * ROWS, (part + 1) * ROWS)
        pieces = [dq_ref[part, :, j * ROWS : (j + 1) * ROWS] for j in range(topk)]
        for expert in range(experts):
            placed_ref[expert * head : (expert + 1) * head, lanes] = place(
                index[:, lanes], pieces, expert
            ).astype(bf16)
    first = first_ref[...]
    dwq_ref[...] += dot_nt(first, placed_ref[...])
    dr_ref[...] += dot_nt(first, logit_grad_ref[...])
    partial_ref[...] = dot(query_weight_ref[...], placed_ref[...]) + dot(
        router_ref[...], logit_grad_ref[...]
    )

    @pl.when(step == pl.num_programs(0) - 1)
    def _():
        router_grad_ref[...] = dr_ref[...]
        size = keep_ref.shape[1]
        for target, core in ((keep_ref, place_ref[1]), (send_ref, 1 - place_ref[1])):
            for half in range(2):
                rows = pl.ds(pl.multiple_of((2 * half + core) * size, size), size)
                target[half] = dwq_ref[rows, :].astype(bf16)


def query_back_call(place_of, first, index, dq, own, other, logit_grad, router):
    width, count = first.shape
    topk = index.shape[0]
    tiles, head, wide = dq.shape
    padded = router.shape[1]
    spread = own.shape[1]
    keep = lambda shape: pl.BlockSpec(shape, lambda i, s: tuple(0 for _ in shape))
    columns = lambda n: pl.BlockSpec((n, TILE), lambda i, s: (0, i))
    shape = jax.ShapeDtypeStruct
    quarters = (2, width // 4, spread)
    return pl.pallas_call(
        query_back_kernel,
        grid_spec=pltpu.PrefetchScalarGridSpec(
            num_scalar_prefetch=1,
            grid=(count // TILE,),
            in_specs=[
                columns(width),
                columns(topk),
                pl.BlockSpec((TILE // ROWS, head, wide), lambda i, s: (i, 0, 0)),
                keep(own.shape),
                keep(other.shape),
                columns(padded),
                keep(router.shape),
            ],
            out_specs=[columns(width), keep(quarters), keep(quarters), keep(router.shape)],
            scratch_shapes=[
                pltpu.VMEM((width, spread), bf16),
                pltpu.VMEM((spread, TILE), bf16),
                pltpu.VMEM((width, spread), f32),
                pltpu.VMEM(router.shape, f32),
            ],
        ),
        out_shape=[
            shape((width, count), f32),
            shape(quarters, bf16),
            shape(quarters, bf16),
            shape(router.shape, f32),
        ],
        compiler_params=params(),
        cost_estimate=cost(10),
        name="query_back",
    )(place_of, first, index, dq, own, other, logit_grad, router)


def first_back_kernel(
    tokens_ref,
    first_ref,
    partial_ref,
    middle_grad_ref,
    dkv_ref,
    kv_weight_ref,
    gain_ref,
    tokens_grad_ref,
    kv_weight_grad_ref,
    gain_grad_ref,
    shift_grad_ref,
):
    step = pl.program_id(0)

    @pl.when(step == 0)
    def _():
        for ref in (kv_weight_grad_ref, gain_grad_ref, shift_grad_ref):
            ref[...] = jnp.zeros(ref.shape, ref.dtype)

    unit, inverse = column_norm(tokens_ref[...].astype(f32).T)
    dkv = dkv_ref[...]
    kv_weight_grad_ref[...] += dot(first_ref[...], dkv)
    first_grad = partial_ref[...] + dot_nt(kv_weight_ref[...], dkv)
    gain_grad_ref[...] += fold_lanes(first_grad * unit)
    shift_grad_ref[...] += fold_lanes(first_grad)
    total = middle_grad_ref[...] + column_norm_back(first_grad, unit, inverse, gain_ref[...])
    tokens_grad_ref[...] = total.T.astype(bf16)


def first_back_call(tokens, first, partial, middle_grad, dkv, kv_weight, gain):
    count, width = tokens.shape
    pair = kv_weight.shape[1]
    columns = lambda n: pl.BlockSpec((n, TILE), lambda i: (0, i))
    rows = lambda n: pl.BlockSpec((TILE, n), lambda i: (i, 0))
    shape = jax.ShapeDtypeStruct
    return pl.pallas_call(
        first_back_kernel,
        grid=(count // TILE,),
        in_specs=[
            rows(width),
            columns(width),
            columns(width),
            columns(width),
            rows(pair),
            whole(kv_weight.shape),
            whole((width, 1)),
        ],
        out_specs=[rows(width), whole(kv_weight.shape), whole((width, 128)), whole((width, 128))],
        out_shape=[
            shape((count, width), bf16),
            shape(kv_weight.shape, f32),
            shape((width, 128), f32),
            shape((width, 128), f32),
        ],
        compiler_params=params(),
        cost_estimate=cost(7),
        name="first_back",
    )(tokens, first, partial, middle_grad, dkv, kv_weight, gain)


def after(value, *others):
    return lax.optimization_barrier((value,) + others)[0]


def other_half(value):
    return lax.ppermute(value, "shard", [(0, 1), (1, 0)])


def join(value, other):
    low = lax.axis_index("shard") == 0
    return jnp.concatenate([jnp.where(low, value, other), jnp.where(low, other, value)], axis=0)


def swap(value, mask):
    count = lax.axis_size("ctx")
    return lax.ppermute(value, "ctx", [(i, i ^ mask) for i in range(count)])


def bit_masks():
    count = lax.axis_size("ctx")
    return [1 << k for k in reversed(range(count.bit_length() - 1))]


def gather_keys(mine):
    masks = bit_masks()
    held = mine
    for mask in masks[:-1]:
        held = jnp.concatenate([held, swap(held, mask)], axis=1)
    return held, swap(held, masks[-1])


def scatter_keys(total):
    for mask in reversed(bit_masks()[:-1]):
        half = total.shape[1] // 2
        total = total[:, :half] + swap(total[:, half:].astype(bf16), mask).astype(f32)
    return total


def add_low(a, b):
    return (a.astype(f32) + b.astype(f32)).astype(bf16)


def halves(value, bit):
    half = value.shape[0] // 2
    keep = lax.dynamic_slice_in_dim(value, bit * half, half, 0)
    send = lax.dynamic_slice_in_dim(value, (1 - bit) * half, half, 0)
    return keep, send


def reduce_quarters(keep, send, halvings):
    me = lax.axis_index("ctx")
    bit = lambda mask: (me // mask) % 2
    _, rows, width = keep.shape
    total = add_low(keep, swap(send, 1)).reshape(2 * rows, width)
    keep, send = halves(total, lax.axis_index("shard"))
    total = add_low(keep, other_half(send))
    masks = bit_masks()[:-1][::-1]
    for mask in masks[:halvings]:
        keep, send = halves(total, bit(mask))
        total = add_low(keep, swap(send, mask))
    for mask in masks[halvings:]:
        total = add_low(total, swap(total, mask))
    for mask in masks[:halvings][::-1] + [1]:
        other = swap(total, mask)
        low = bit(mask) == 0
        total = jnp.concatenate(
            [jnp.where(low, total, other), jnp.where(low, other, total)], axis=0
        )
    return total.astype(f32)


def home_plan(count, block):
    half = count // 2
    if block != 4 * PART or block * half != PROMPT or block != CLEN or half % 2:
        return None
    sends = [None] * count
    hops = [[], [], []]
    for a in range(half // 2):
        b = half - 1 - a
        p, q = a + half, b + half
        sends[a], sends[b] = (0, 1, 2, 3), (2, 3, 0, 1)
        sends[p] = sends[q] = (0, 3, 1, 2)
        hops[0] += [(a, b), (b, a)]
        hops[1] += [(a, p), (p, a), (b, q), (q, b)]
        hops[2] += [(a, q), (b, p), (p, a), (q, b)]
    places = [[(i, sends[i][0]), (i, sends[i][1]), None, None] for i in range(count)]
    for k, hop in enumerate(hops):
        for source, target in hop:
            places[target][k + 1] = (source, sends[source][k + 1])
    return sends, hops, places


def exchange(value, plan, extra=None):
    sends, hops, _ = plan
    me = lax.axis_index("ctx")
    rows, width = value.shape
    size = rows // 4
    starts = jnp.array(sends, jnp.int32)[me] * size
    pieces = [lax.dynamic_slice_in_dim(value, starts[k], size, 0) for k in range(4)]
    if extra is not None:
        count = extra.shape[0]
        tail = count * size // width
        blank = jnp.zeros((-tail % 16, width), value.dtype)
        for k in range(4):
            part = lax.dynamic_slice_in_dim(extra, starts[k], size, 1).reshape(tail, width)
            pieces[k] = jnp.concatenate([pieces[k], part, blank], axis=0)
    got = [lax.ppermute(pieces[k + 1], "ctx", hops[k]) for k in range(3)]
    got[0] = jnp.where(me < lax.axis_size("ctx") // 2, got[0], pieces[1])
    got = [pieces[0]] + got
    main = jnp.concatenate([x[:size] for x in got], axis=0)
    if extra is None:
        return main
    parts = [x[size : size + tail].reshape(count, size) for x in got]
    return main, jnp.concatenate(parts, axis=1)


def exchange_back(value, plan):
    sends, hops, _ = plan
    me = lax.axis_index("ctx")
    size = value.shape[0] // 4
    pieces = [value[k * size : (k + 1) * size] for k in range(4)]
    got = [
        lax.ppermute(pieces[k + 1], "ctx", [(t, s) for s, t in hops[k]]) for k in range(3)
    ]
    got[0] = jnp.where(me < lax.axis_size("ctx") // 2, got[0], pieces[1])
    held = jnp.concatenate([pieces[0]] + got, axis=0)
    order = [[send.index(k) for k in range(4)] for send in sends]
    starts = jnp.array(order, jnp.int32)[me] * size
    return jnp.concatenate(
        [lax.dynamic_slice_in_dim(held, starts[k], size, 0) for k in range(4)], axis=0
    )


def per_device(
    tokens,
    expert_index,
    first_gain,
    first_shift,
    router_weight,
    query_weight,
    key_weight,
    value_weight,
    output_weight,
    second_gain,
    second_shift,
    up_weight,
    up_bias,
    down_weight,
    down_bias,
    out_grad,
):
    groups, block, width = tokens.shape
    assert groups == 1 and lax.axis_size("shard") == 2
    count = lax.axis_size("ctx")
    me = lax.axis_index("ctx")
    shard = lax.axis_index("shard").astype(jnp.int32)[None]
    experts = router_weight.shape[1]
    head = key_weight.shape[1]
    pair = 2 * head
    padded = 32
    plan = home_plan(count, block)
    flat = tokens[0]
    index = expert_index[0].T
    if plan:
        flat, index = exchange(flat, plan, index.astype(bf16))
        index = index.astype(jnp.int32)

    spare = jnp.zeros((key_weight.shape[0], padded - experts), bf16)
    vectors = [first_gain, first_shift, second_gain, second_shift, down_bias]
    half_width = width // 2
    small = jnp.concatenate(
        [key_weight, value_weight, router_weight, spare]
        + [v[:, None] for v in vectors]
        + [up_bias.reshape(half_width, -1)],
        axis=1,
    )
    small = join(small, other_half(small))
    query_other = other_half(after(query_weight, small))
    kv_weight = small[:, :pair]
    router = small[:, pair : pair + padded]
    at = pair + padded
    columns = [small[:, at + i : at + i + 1].astype(f32) for i in range(len(vectors))]
    gain_one, shift_one, gain_two, shift_two, down_bias_all = columns
    end = at + len(vectors)
    up_bias_all = small[:, end:].reshape(-1, 1).astype(f32)
    first, kv = first_call(flat, gain_one, shift_one, kv_weight)

    if plan:
        _, _, places = plan
        where = [[source * 4 + quarter for source, quarter in row] for row in places]
        low_slot = [next(k for k in range(4) if row[k] < HALF // PART) for row in where]
        high_slot = [
            next(k for k in range(4) if HALF // PART <= row[k] < PROMPT // PART) for row in where
        ]
        own_slot = [2 if i < count // 2 else 0 for i in range(count)]
        low_at = [row[k] for row, k in zip(where, low_slot)]
        high_at = [row[k] - HALF // PART for row, k in zip(where, high_slot)]
        own_at = [[row[k] % 4, row[k + 1] % 4] for row, k in zip(where, own_slot)]
        masks = bit_masks()
        slots = [sum(m for k, m in enumerate(masks) if j >> k & 1) for j in range(count)]
        low_table = [[low_at[i ^ m] for m in slots] for i in range(count)]
        high_table = [
            [high_at[i ^ m] for m in slots]
            + [HALF // PART + x for x in own_at[i] + own_at[i ^ (count // 2)]]
            for i in range(count)
        ]
        pick = lambda table: jnp.array(table, jnp.int32)[me]
        bases = pick([[x * PART + r for x in row for r in range(0, PART, ROWS)] for row in where])
        low_table, high_table = pick(low_table), pick(high_table)
        low_start, high_start, own_start = (
            pick(x) * PART for x in (low_slot, high_slot, own_slot)
        )
        take = lambda start, rows: lax.dynamic_slice_in_dim(kv, start, rows, 0)
        near, far = gather_keys(jnp.stack([take(low_start, PART), take(high_start, PART)]))
        own = take(own_start, 2 * PART)
        partner = swap(own, count // 2)
        low_keys = (near[0], far[0])
        high_keys = (near[1], far[1], own, partner)
    else:
        base = me * block
        bases = base + jnp.arange(block // ROWS, dtype=jnp.int32) * ROWS
        gathered = lax.all_gather(kv, "ctx", axis=0, tiled=True)
        segment = jnp.maximum(base, PROMPT) // CLEN * CLEN
        own = lax.dynamic_slice_in_dim(gathered, segment, CLEN, 0)
        quarter = HALF // 2
        low_keys = (gathered[:quarter], gathered[quarter:HALF])
        high_keys = (
            gathered[HALF : HALF + quarter], gathered[HALF + quarter : PROMPT],
            own[: CLEN // 2], own[CLEN // 2 :],
        )
        low_table = jnp.arange(HALF // PART, dtype=jnp.int32)
        high_table = jnp.arange((HALF + CLEN) // PART, dtype=jnp.int32)

    qt, q, gate = query_call(shard, first, query_weight, query_other, router, index, head)
    split = output_weight.shape[0]
    stacked = jnp.concatenate([output_weight, down_weight], axis=0)
    stacked_other = other_half(after(stacked, query_other))
    up_other = other_half(after(up_weight, query_other))
    weights = (
        output_weight, stacked_other[:split], up_weight, up_other, down_weight, stacked_other[split:]
    )
    grad = out_grad[0]
    if plan:
        grad = exchange(after(grad, near, far, partner), plan)
    state = attend_call(0, low_keys, low_table, bases, qt)
    attended, lse = attend_call(HALF, high_keys, high_table, bases, qt, state, last=True)
    (
        layer_out, middle_grad, grad_t, grad_rows, delta, logit_grad, keep, send,
        second_gain_grad, second_shift_grad, up_bias_grad, down_bias_grad,
    ) = middle_call(
        shard, flat, grad, index, gate, attended, weights,
        gain_two, shift_two, up_bias_all, down_bias_all, padded,
    )

    arrived = other_half(send)
    kinds = (f32, bf16) if plan else (bf16, bf16)
    shared = (qt, q, grad_t, grad_rows, lse, delta)
    dq, *high_grads = attend_back_call(
        HALF, high_keys, kinds + (f32, bf16), high_table, bases, *shared
    )
    keep, arrived, dq, *high_grads = lax.optimization_barrier((keep, arrived, dq, *high_grads))
    early = add_low(keep, arrived)
    early_sum = lax.psum(early, "ctx")
    if plan:
        layer_out = exchange_back(after(layer_out, arrived), plan)
        own_grad = high_grads[2] + swap(high_grads[3], count // 2).astype(f32)
        high_grad = high_grads[0] + swap(high_grads[1], 1).astype(f32)
    dq, *low_grads = attend_back_call(
        0, low_keys, kinds, low_table, after(bases, early), *shared, dq=dq
    )
    core = me % 2
    partial, keep, send, router_grad = query_back_call(
        jnp.stack([shard[0], core]), first, index, dq, query_weight, query_other, logit_grad, router
    )
    if plan:
        low_grad = low_grads[0] + swap(low_grads[1], 1).astype(f32)
        low_high = scatter_keys(jnp.stack([low_grad, high_grad]))
        dkv = jnp.zeros((block, pair), bf16)
        pieces = ((own_grad, own_start), (low_high[1], high_start), (low_high[0], low_start))
        for piece, start in pieces:
            dkv = lax.dynamic_update_slice_in_dim(dkv, piece.astype(bf16), start, 0)
    else:
        rest = count * block - PROMPT
        dall = jnp.concatenate(
            [x.astype(bf16) for x in low_grads + high_grads[:2]] + [jnp.zeros((rest, pair), bf16)]
        )
        own_grad = jnp.concatenate([x.astype(bf16) for x in high_grads[2:]])
        own_grad = jnp.where(base >= PROMPT, own_grad, jnp.zeros_like(own_grad))
        dall = lax.dynamic_update_slice_in_dim(dall, own_grad, segment, 0)
        dkv = lax.psum_scatter(dall, "ctx", scatter_dimension=0, tiled=True)

    query_weight_grad = reduce_quarters(keep, send, 1)
    tokens_grad, kv_weight_grad, first_gain_grad, first_shift_grad = first_back_call(
        flat, first, partial, middle_grad, dkv, kv_weight, gain_one
    )
    vector_grads = [
        jnp.sum(first_gain_grad, axis=1),
        jnp.sum(first_shift_grad, axis=1),
        jnp.sum(second_gain_grad, axis=1),
        jnp.sum(second_shift_grad, axis=1),
        down_bias_grad[0],
    ]
    small_grad = jnp.concatenate(
        [kv_weight_grad, router_grad]
        + [v[:, None] for v in vector_grads]
        + [jnp.sum(up_bias_grad, axis=1).reshape(width, -1)],
        axis=1,
    ).astype(bf16)
    quarters = small_grad.reshape(2, 2, width // 4, -1)
    keep = lax.dynamic_index_in_dim(quarters, core, 1, keepdims=False)
    send = lax.dynamic_index_in_dim(quarters, 1 - core, 1, keepdims=False)
    small_grad = reduce_quarters(keep, send, 0)
    if plan:
        tokens_grad = exchange_back(tokens_grad, plan)
    early_sum = early_sum.astype(f32)
    cuts = [split, split + down_weight.shape[0]]
    output_weight_grad, down_weight_grad, up_weight_grad = jnp.split(early_sum, cuts)
    up_weight_grad = jnp.concatenate(
        jnp.split(up_weight_grad, up_weight_grad.shape[0] // half_width), axis=1
    )
    return (
        layer_out[None],
        tokens_grad[None],
        small_grad[:, at],
        small_grad[:, at + 1],
        small_grad[:, pair : pair + experts],
        query_weight_grad,
        small_grad[:, :head],
        small_grad[:, head:pair],
        output_weight_grad,
        small_grad[:, at + 2],
        small_grad[:, at + 3],
        up_weight_grad,
        small_grad[:, end:].reshape(-1),
        down_weight_grad,
        small_grad[:, at + 4],
    )


def solution(mesh):
    split = P("shard", "ctx", None)
    vector = P("shard")
    matrix = P("shard", None)
    in_specs = (
        split, split, vector, vector, matrix, matrix, matrix, matrix, matrix,
        vector, vector, matrix, vector, matrix, vector, split,
    )
    out_specs = (
        split, split, vector, vector, matrix, matrix, matrix, matrix, matrix,
        vector, vector, matrix, vector, matrix, vector,
    )
    return jax.shard_map(
        per_device, mesh=mesh, in_specs=in_specs, out_specs=out_specs, check_vma=False
    )
```

```python
import functools
import math

import jax
import jax.numpy as jnp
from jax import lax
from jax.experimental import pallas as pl
from jax.experimental.pallas import tpu as pltpu
from jax.sharding import PartitionSpec as P

PROMPT = 8192
CLEN = 1024
ROWS = 128
TILE = 256
FULL = 1024
PART = 256
HALF = PROMPT // 2
VMEM = 60 << 20

PIECES, IS_PROMPT, LOW_SLOT, HIGH_SLOT, OWN_SLOT, SHARD, CORE, SIDE, BASES = 0, 4, 5, 6, 7, 8, 9, 10, 11
norm_eps = 1e-05
mask_fill = -1e30
LOG2E = math.log2(math.e)
bf16 = jnp.bfloat16
f32 = jnp.float32


def dot(a, b):
    return lax.dot_general(a, b, (((1,), (0,)), ((), ())), preferred_element_type=f32)


def dot_tn(a, b):
    return lax.dot_general(a, b, (((0,), (0,)), ((), ())), preferred_element_type=f32)


def dot_nt(a, b):
    return lax.dot_general(a, b, (((1,), (1,)), ((), ())), preferred_element_type=f32)


def params(**kw):
    return pltpu.CompilerParams(vmem_limit_bytes=VMEM, **kw)


def cost(us):
    return pl.CostEstimate(flops=int(us * 1.15e9), transcendentals=0, bytes_accessed=0)


def whole(shape):
    return pl.BlockSpec(shape, lambda i: tuple(0 for _ in shape))


def column_norm(values):
    center = jnp.mean(values, axis=0, keepdims=True)
    centred = values - center
    spread = jnp.mean(centred * centred, axis=0, keepdims=True)
    inverse = lax.rsqrt(spread + norm_eps)
    return centred * inverse, inverse


def column_norm_back(grad, unit, inverse, gain):
    scaled = grad * gain
    inner = (
        scaled
        - jnp.mean(scaled, axis=0, keepdims=True)
        - unit * jnp.mean(scaled * unit, axis=0, keepdims=True)
    )
    return inner * inverse


def fold_lanes(values):
    width = values.shape[1]
    total = values[:, :128]
    for start in range(128, width, 128):
        total = total + values[:, start : start + 128]
    return total


def pick_piece(step, table_ref, sources, target_ref):
    if len(sources) == 1:
        target_ref[...] = sources[0][...]
        return
    keep, own, *got = sources
    rows = target_ref.shape[0]
    prompt = table_ref[IS_PROMPT] == 1
    which = ((step == 0), (step == 1) & jnp.logical_not(prompt), (step == 1) & prompt)
    for chosen, ref in zip(which + ((step == 2), (step == 3)), (keep, own, *got)):

        @pl.when(chosen)
        def _():
            target_ref[...] = ref[:rows, :]


def store_piece(step, targets, value):
    if len(targets) == 1:
        targets[0][...] = value
        return
    for k, ref in enumerate(targets):

        @pl.when(step == k)
        def _():
            ref[...] = value


def piece_specs(pieces):
    if len(pieces) == 1:
        return [pl.BlockSpec((TILE, pieces[0].shape[1]), lambda i, t: (i, 0))]
    return [pl.BlockSpec(x.shape, lambda i, t: (0, 0)) for x in pieces]


def pack_kernel(table_ref, *refs):
    rows_ref, *refs = refs
    index = refs.pop(0) if len(refs) > 4 else None
    for k, ref in enumerate(refs):
        span = pl.ds(pl.multiple_of(table_ref[PIECES + k] * PART, PART), PART)
        ref[:PART, :] = rows_ref[span, :]
        if index is not None:
            chosen = index[:, span].astype(f32)
            blank = jnp.zeros((16 - index.shape[0], PART), f32)
            ref[PART:, :] = jnp.concatenate(
                [jnp.concatenate([chosen, blank], axis=0)] * (ref.shape[1] // PART), axis=1
            ).astype(bf16)


def pack_call(table, rows, index=None):
    count, width = rows.shape
    out = (count // 4 + (0 if index is None else 16), width)
    inputs = (rows,) if index is None else (rows, index)
    return pl.pallas_call(
        pack_kernel,
        grid_spec=pltpu.PrefetchScalarGridSpec(
            num_scalar_prefetch=1,
            grid=(1,),
            in_specs=[pl.BlockSpec(x.shape, lambda i, t: (0, 0)) for x in inputs],
            out_specs=[pl.BlockSpec(out, lambda i, t: (0, 0))] * 4,
        ),
        out_shape=[jax.ShapeDtypeStruct(out, bf16)] * 4,
        compiler_params=params(),
        cost_estimate=cost(2),
        name="pack",
    )(table, *inputs)


def unpack_kernel(table_ref, keep_ref, own_ref, *refs):
    *got, out_ref = refs
    prompt = table_ref[IS_PROMPT] == 1
    place_of = lambda k: pl.ds(pl.multiple_of(table_ref[PIECES + k] * PART, PART), PART)
    out_ref[place_of(0), :] = keep_ref[...]
    out_ref[place_of(2), :] = got[1][...]
    out_ref[place_of(3), :] = got[2][...]

    @pl.when(prompt)
    def _():
        out_ref[place_of(1), :] = got[0][...]

    @pl.when(jnp.logical_not(prompt))
    def _():
        out_ref[place_of(1), :] = own_ref[...]


def unpack_call(table, pieces):
    rows, width = pieces[0].shape
    return pl.pallas_call(
        unpack_kernel,
        grid_spec=pltpu.PrefetchScalarGridSpec(
            num_scalar_prefetch=1,
            grid=(1,),
            in_specs=[pl.BlockSpec((rows, width), lambda i, t: (0, 0))] * 5,
            out_specs=pl.BlockSpec((4 * rows, width), lambda i, t: (0, 0)),
        ),
        out_shape=jax.ShapeDtypeStruct((4 * rows, width), bf16),
        compiler_params=params(),
        cost_estimate=cost(2),
        name="unpack",
    )(table, *pieces)


def first_kernel(pieces, table_ref, *refs):
    sources = refs[:pieces]
    gain_ref, shift_ref, kv_weight_ref = refs[pieces : pieces + 3]
    refs = refs[pieces + 3 :]
    step = pl.program_id(0)
    first_ref = refs[0]
    tokens_ref = refs[-1]
    pick_piece(step, table_ref, sources, tokens_ref)
    unit, _ = column_norm(tokens_ref[...].astype(f32).T)
    first = (unit * gain_ref[...] + shift_ref[...]).astype(bf16)
    first_ref[...] = first
    kv = dot_tn(kv_weight_ref[...], first).T.astype(bf16)
    if pieces == 1:
        refs[1][...] = kv
        return
    shared_ref, own_ref, index_ref, flat_ref, _ = refs[1:]
    flat_ref[...] = tokens_ref[...]
    topk, rows = index_ref.shape
    keep, own, *got = sources
    prompt = table_ref[IS_PROMPT] == 1
    which = ((step == 0), (step == 1) & jnp.logical_not(prompt), (step == 1) & prompt)
    for chosen, ref in zip(which + ((step == 2), (step == 3)), (keep, own, *got)):

        @pl.when(chosen)
        def _():
            index_ref[...] = ref[PART:, :rows][:topk, :].astype(f32).astype(jnp.int32)

    for slot, half in ((LOW_SLOT, 0), (HIGH_SLOT, 1)):

        @pl.when(step == table_ref[slot])
        def _():
            shared_ref[half * PART : (half + 1) * PART, :] = kv

    for half in range(2):

        @pl.when(step == table_ref[OWN_SLOT] + half)
        def _():
            own_ref[half * PART : (half + 1) * PART, :] = kv


def first_call(table, sources, count, topk, gain, shift, kv_weight):
    width, pair = kv_weight.shape
    keep = lambda shape: pl.BlockSpec(shape, lambda i, t: (0, 0))
    shape = jax.ShapeDtypeStruct
    split = len(sources) > 1
    outs = [(pl.BlockSpec((width, TILE), lambda i, t: (0, i)), shape((width, count), bf16))]
    rows = lambda n: pl.BlockSpec((TILE, n), lambda i, t: (i, 0))
    if split:
        outs += [
            (keep((2 * PART, pair)), shape((2 * PART, pair), bf16)),
            (keep((2 * PART, pair)), shape((2 * PART, pair), bf16)),
            (pl.BlockSpec((topk, TILE), lambda i, t: (0, i)), shape((topk, count), jnp.int32)),
            (rows(width), shape((count, width), bf16)),
        ]
    else:
        outs += [(rows(pair), shape((count, pair), bf16))]
    return pl.pallas_call(
        functools.partial(first_kernel, len(sources)),
        grid_spec=pltpu.PrefetchScalarGridSpec(
            num_scalar_prefetch=1,
            grid=(count // TILE,),
            in_specs=piece_specs(sources)
            + [keep((width, 1)), keep((width, 1)), keep((width, pair))],
            out_specs=[x for x, _ in outs],
            scratch_shapes=[pltpu.VMEM((TILE, width), bf16)],
        ),
        out_shape=[x for _, x in outs],
        compiler_params=params(),
        cost_estimate=cost(5),
        name="first_norm",
    )(table, *sources, gain, shift, kv_weight)


def join_rows(shard, own_ref, other_ref, all_ref, start=0):
    half = own_ref.shape[0]
    all_ref[pl.ds(pl.multiple_of(shard * half, half), half), :] = own_ref[...]
    rows = pl.ds(pl.multiple_of((1 - shard) * half, half), half)
    all_ref[rows, :] = other_ref[start : start + half, :]


def query_kernel(
    table_ref, first_ref, own_ref, other_ref, router_ref, index_ref,
    qt_ref, q_ref, gate_ref, query_weight_ref,
):
    topk = index_ref.shape[0]

    @pl.when(pl.program_id(0) == 0)
    def _():
        join_rows(table_ref[SHARD], own_ref, other_ref, query_weight_ref)

    head = qt_ref.shape[1]
    experts = query_weight_ref.shape[1] // head
    first = first_ref[...]
    projected = dot_tn(query_weight_ref[...], first)
    logits = dot_tn(router_ref[...], first)
    index = index_ref[...]
    picked = jnp.zeros(index.shape, f32)
    for expert in range(experts):
        picked = jnp.where(index == expert, logits[expert : expert + 1, :], picked)
    picked = jnp.exp(picked - jnp.max(picked, axis=0, keepdims=True))
    gate_ref[...] = picked / jnp.sum(picked, axis=0, keepdims=True)
    for part in range(TILE // ROWS):
        lanes = slice(part * ROWS, (part + 1) * ROWS)
        for j in range(topk):
            row = index[j : j + 1, lanes]
            chosen = jnp.zeros((head, ROWS), f32)
            for expert in range(experts):
                chosen = jnp.where(
                    row == expert, projected[expert * head : (expert + 1) * head, lanes], chosen
                )
            qt_ref[part, :, j * ROWS : (j + 1) * ROWS] = chosen.astype(bf16)
            q_ref[part, j * ROWS : (j + 1) * ROWS, :] = chosen.T.astype(bf16)


def query_call(table, first, own, other, router, index, head):
    width, count = first.shape
    topk = index.shape[0]
    tiles = count // ROWS
    per = TILE // ROWS
    keep = lambda shape: pl.BlockSpec(shape, lambda i, s: (0, 0))
    return pl.pallas_call(
        query_kernel,
        grid_spec=pltpu.PrefetchScalarGridSpec(
            num_scalar_prefetch=1,
            grid=(count // TILE,),
            in_specs=[
                pl.BlockSpec((width, TILE), lambda i, s: (0, i)),
                keep(own.shape),
                keep(other.shape),
                keep(router.shape),
                pl.BlockSpec((topk, TILE), lambda i, s: (0, i)),
            ],
            out_specs=[
                pl.BlockSpec((per, head, topk * ROWS), lambda i, s: (i, 0, 0)),
                pl.BlockSpec((per, topk * ROWS, head), lambda i, s: (i, 0, 0)),
                pl.BlockSpec((topk, TILE), lambda i, s: (0, i)),
            ],
            scratch_shapes=[pltpu.VMEM((width, own.shape[1]), bf16)],
        ),
        out_shape=[
            jax.ShapeDtypeStruct((tiles, head, topk * ROWS), bf16),
            jax.ShapeDtypeStruct((tiles, topk * ROWS, head), bf16),
            jax.ShapeDtypeStruct((topk, count), f32),
        ],
        compiler_params=params(),
        cost_estimate=cost(10),
        name="queries",
    )(table, first, own, other, router, index)


def tile_ranges(base):
    prompt = base < PROMPT
    begin = jnp.where(prompt, base // FULL * FULL, PROMPT)
    position = jnp.where(prompt, begin, PROMPT + (base - PROMPT) // CLEN * CLEN)
    parts = (base + ROWS - position + PART - 1) // PART
    return begin // FULL, begin, position, parts


def allowed_mask(position, base, width):
    key_pos = position + lax.broadcasted_iota(jnp.int32, (PART, width), 0)
    query_pos = base + lax.rem(lax.broadcasted_iota(jnp.int32, (PART, width), 1), ROWS)
    return key_pos <= query_pos


def for_slots(refs, table_ref, start, visit):
    slot = 0
    for ref in refs:
        for row in range(0, ref.shape[0], PART):
            place_of = pl.multiple_of(table_ref[start + slot] * PART, PART)
            visit(ref, row, pl.ds(place_of, PART))
            slot += 1


def attend_kernel(start, buffers, table_ref, *refs):
    sources = refs[:buffers]
    qt_ref = refs[buffers]
    refs = refs[buffers + 1 :]
    out_ref, lse_ref, kv_ref, vt_ref, knorm_ref, acc_ref, max_ref = refs
    tile = pl.program_id(0)
    head, width = qt_ref.shape[1:]
    factor = LOG2E * head ** (-0.5)

    @pl.when(tile == 0)
    def _():
        knorm_ref[0] = 0.0

        def turn(ref, row, span):
            rows = ref[row : row + PART, :]
            kv_ref[span, :] = rows
            both = rows.T
            vt_ref[:head, span] = both[head:, :]
            vt_ref[head:, span] = jnp.ones((vt_ref.shape[0] - head, PART), bf16)
            keys = both[:head, :].astype(f32)
            most = jnp.max(jnp.sum(keys * keys, axis=0, keepdims=True))
            knorm_ref[0] = jnp.maximum(knorm_ref[0], most)

        for_slots(sources, table_ref, start, turn)

    base = table_ref[BASES + tile]
    steps, begin, position, parts = tile_ranges(base)
    query = qt_ref[0].astype(f32)
    qnorm = jnp.max(jnp.sum(query * query, axis=0, keepdims=True))
    narrow = qnorm * knorm_ref[0] * (factor * factor) < 100.0 * 100.0
    acc_ref[...] = jnp.zeros(acc_ref.shape, f32)
    max_ref[...] = jnp.full(max_ref.shape, jnp.where(narrow, 0.0, mask_fill), f32)

    def plain(offset, size, mask):
        span = pl.ds(pl.multiple_of(offset, size), size)
        scores = dot(kv_ref[span, :head], qt_ref[0]) * factor
        if mask is not None:
            scores = jnp.where(mask, scores, mask_fill)
        probs = jnp.exp2(scores).astype(bf16)
        acc_ref[...] += dot(vt_ref[:, span], probs)

    @pl.when(narrow)
    def _():
        def step(i, carry):
            plain(i * FULL, FULL, None)
            return carry

        def part(i, carry):
            plain(begin + i * PART, PART, allowed_mask(position + i * PART, base, width))
            return carry

        lax.fori_loop(0, steps, step, 0)
        lax.fori_loop(0, parts, part, 0)

    @pl.when(jnp.logical_not(narrow))
    def _():
        def part(i, carry):
            before = i < steps * (FULL // PART)
            offset = i * PART
            span = pl.ds(pl.multiple_of(offset, PART), PART)
            shifted = jnp.where(before, -(1 << 24), position + offset - begin)
            mask = allowed_mask(shifted, base, width)
            scores = dot(kv_ref[span, :head], qt_ref[0]) * factor
            scores = jnp.where(mask, scores, mask_fill)
            old = max_ref[...]
            new = jnp.maximum(old, jnp.max(scores, axis=0, keepdims=True))
            probs = jnp.where(mask, jnp.exp2(scores - new), 0.0).astype(bf16)
            acc_ref[...] = acc_ref[...] * jnp.exp2(old - new) + dot(vt_ref[:, span], probs)
            max_ref[...] = new
            return carry

        lax.fori_loop(0, steps * (FULL // PART) + parts, part, 0)

    total = acc_ref[head : head + 1, :]
    out_ref[0] = acc_ref[:head, :] / total
    lse_ref[0] = max_ref[...] + jnp.log2(total)


def attend_call(start, sources, table, qt):
    tiles, head, width = qt.shape
    total_keys = sum(x.shape[0] for x in sources)
    pair = sources[0].shape[1]
    one = lambda shape: pl.BlockSpec((1,) + shape, lambda i, t: (i, 0, 0))
    keep = lambda x: pl.BlockSpec(x.shape, lambda i, t: (0, 0))
    return pl.pallas_call(
        functools.partial(attend_kernel, start, len(sources)),
        grid_spec=pltpu.PrefetchScalarGridSpec(
            num_scalar_prefetch=1,
            grid=(tiles,),
            in_specs=[keep(x) for x in sources] + [one((head, width))],
            out_specs=[one((head, width)), one((1, width))],
            scratch_shapes=[
                pltpu.VMEM((total_keys, pair), bf16),
                pltpu.VMEM((head + 16, total_keys), bf16),
                pltpu.SMEM((1,), f32),
                pltpu.VMEM((head + 16, width), f32),
                pltpu.VMEM((1, width), f32),
            ],
        ),
        out_shape=[
            jax.ShapeDtypeStruct((tiles, head, width), f32),
            jax.ShapeDtypeStruct((tiles, 1, width), f32),
        ],
        compiler_params=params(),
        cost_estimate=cost(64),
        name="attend",
    )(table, *sources, qt)


def attend_back_kernel(start, buffers, table_ref, *refs):
    sources = refs[:buffers]
    qt_ref, q_ref, dot_ref, do_ref, lse_ref, delta_ref = refs[buffers : buffers + 6]
    refs = refs[buffers + 6 :]
    dq_ref = refs[0]
    outs = refs[1 : 1 + buffers]
    kv_ref, kt_ref, dkv_ref = refs[1 + buffers :]
    tile = pl.program_id(0)
    head, width = qt_ref.shape[1:]
    scale = head ** (-0.5)

    @pl.when(tile == 0)
    def _():
        def turn(ref, row, span):
            rows = ref[row : row + PART, :]
            kv_ref[span, :] = rows
            kt_ref[:, span] = rows.T[:head, :]
            dkv_ref[span, :] = jnp.zeros((PART, 2 * head), f32)

        for_slots(sources, table_ref, start, turn)

    base = table_ref[BASES + tile]
    steps, begin, position, parts = tile_ranges(base)
    dq_ref[...] = jnp.zeros(dq_ref.shape, f32)

    def block(offset, size, mask):
        span = pl.ds(pl.multiple_of(offset, size), size)
        scores = dot(kv_ref[span, :head], qt_ref[0]) * (LOG2E * scale) - lse_ref[0]
        probs = jnp.exp2(scores)
        if mask is not None:
            probs = jnp.where(mask, probs, 0.0)
        prob_grad = dot(kv_ref[span, head:], dot_ref[0])
        score_grad = (probs * (prob_grad - delta_ref[0])).astype(bf16)
        dq_ref[0] += dot(kt_ref[:, span], score_grad) * scale
        dkv_ref[span, :head] += dot(score_grad, q_ref[0])
        dkv_ref[span, head:] += dot(probs.astype(bf16), do_ref[0])

    def step(i, carry):
        block(i * FULL, FULL, None)
        return carry

    def part(i, carry):
        block(begin + i * PART, PART, allowed_mask(position + i * PART, base, width))
        return carry

    lax.fori_loop(0, steps, step, 0)
    lax.fori_loop(0, parts, part, 0)

    @pl.when(tile == pl.num_programs(0) - 1)
    def _():
        lane = lax.broadcasted_iota(jnp.int32, (PART, 2 * head), 1)
        both = jnp.where(lane < head, scale, 1.0)

        def finish(ref, row, span):
            ref[row : row + PART, :] = (dkv_ref[span, :] * both).astype(ref.dtype)

        for_slots(outs, table_ref, start, finish)


def attend_back_call(start, sources, kinds, table, qt, q, grad_t, grad, lse, delta):
    tiles, head, width = qt.shape
    total_keys = sum(x.shape[0] for x in sources)
    pair = sources[0].shape[1]
    one = lambda shape: pl.BlockSpec((1,) + shape, lambda i, t: (i, 0, 0))
    keep = lambda x: pl.BlockSpec(x.shape, lambda i, t: (0, 0))
    return pl.pallas_call(
        functools.partial(attend_back_kernel, start, len(sources)),
        grid_spec=pltpu.PrefetchScalarGridSpec(
            num_scalar_prefetch=1,
            grid=(tiles,),
            in_specs=[keep(x) for x in sources]
            + [
                one((head, width)),
                one((width, head)),
                one((head, width)),
                one((width, head)),
                one((1, width)),
                one((1, width)),
            ],
            out_specs=[one((head, width))] + [keep(x) for x in sources],
            scratch_shapes=[
                pltpu.VMEM((total_keys, pair), bf16),
                pltpu.VMEM((head, total_keys), bf16),
                pltpu.VMEM((total_keys, pair), f32),
            ],
        ),
        out_shape=[jax.ShapeDtypeStruct((tiles, head, width), f32)]
        + [jax.ShapeDtypeStruct(x.shape, kind) for x, kind in zip(sources, kinds)],
        compiler_params=params(),
        cost_estimate=cost(160),
        name="attend_back",
    )(table, *sources, qt, q, grad_t, grad, lse, delta)


def place(index, pieces, expert):
    total = jnp.zeros(pieces[0].shape, f32)
    for j, piece in enumerate(pieces):
        total = jnp.where(index[j : j + 1, :] == expert, piece, total)
    return total


def middle_kernel(pieces, table_ref, *refs):
    sources = refs[:pieces]
    refs = refs[pieces:]
    outs = 4 if pieces > 1 else 1
    layer_out_refs = refs[MIDDLE_INPUTS : MIDDLE_INPUTS + outs]
    refs = refs[:MIDDLE_INPUTS] + refs[MIDDLE_INPUTS + outs :]
    middle_body(table_ref, sources, layer_out_refs, *refs)


MIDDLE_INPUTS = 13


def middle_body(
    table_ref,
    sources,
    layer_out_refs,
    tokens_ref,
    index_ref,
    gate_ref,
    attended_ref,
    output_own_ref,
    down_own_ref,
    both_other_ref,
    up_own_ref,
    up_other_ref,
    gain_ref,
    shift_ref,
    up_bias_ref,
    down_bias_ref,
    middle_grad_ref,
    grad_t_ref,
    grad_rows_ref,
    delta_ref,
    logit_grad_ref,
    output_weight_grad_ref,
    up_weight_grad_ref,
    down_weight_grad_ref,
    gain_grad_ref,
    shift_grad_ref,
    up_bias_grad_ref,
    down_bias_grad_ref,
    grad_ref,
    output_weight_ref,
    up_weight_ref,
    down_weight_ref,
    spread_ref,
    chosen_ref,
    dwo_ref,
    dup_ref,
    ddown_ref,
):
    step = pl.program_id(0)
    topk = index_ref.shape[0]
    head = attended_ref.shape[1]
    experts = output_weight_ref.shape[0] // head
    per = TILE // ROWS

    @pl.when(step == 0)
    def _():
        shard = table_ref[SHARD]
        join_rows(shard, output_own_ref, both_other_ref, output_weight_ref)
        join_rows(shard, down_own_ref, both_other_ref, down_weight_ref, output_own_ref.shape[0])
        join_rows(shard, up_own_ref, up_other_ref, up_weight_ref)
        for ref in (
            dwo_ref,
            dup_ref,
            ddown_ref,
            gain_grad_ref,
            shift_grad_ref,
            up_bias_grad_ref,
            down_bias_grad_ref,
        ):
            ref[...] = jnp.zeros(ref.shape, ref.dtype)

    pick_piece(step, table_ref, sources, grad_ref)
    index = index_ref[...]
    gate = gate_ref[...]
    for part in range(per):
        lanes = slice(part * ROWS, (part + 1) * ROWS)
        pieces = [
            attended_ref[part, :, j * ROWS : (j + 1) * ROWS] * gate[j : j + 1, lanes]
            for j in range(topk)
        ]
        for expert in range(experts):
            spread_ref[expert * head : (expert + 1) * head, lanes] = place(
                index[:, lanes], pieces, expert
            ).astype(bf16)

    middle = tokens_ref[...].astype(f32).T + dot_tn(output_weight_ref[...], spread_ref[...])
    unit, inverse = column_norm(middle)
    second = (unit * gain_ref[...] + shift_ref[...]).astype(bf16)
    pre = dot_tn(up_weight_ref[...], second) + up_bias_ref[...]
    coeff = math.sqrt(2.0 / math.pi)
    square = pre * pre
    wave = jnp.tanh(coeff * pre * (1.0 + 0.044715 * square))
    half = 0.5 * (1.0 + wave)
    hidden = (pre * half).astype(bf16)
    slope = half + 0.5 * pre * (1.0 - wave * wave) * (coeff * (1.0 + 3 * 0.044715 * square))
    result = middle + dot_tn(down_weight_ref[...], hidden) + down_bias_ref[...]
    store_piece(step, layer_out_refs, result.T.astype(bf16))

    grad_rows = grad_ref[...]
    grad_wide = grad_rows.astype(f32)
    grad_t = grad_wide.T
    ddown_ref[...] += dot(hidden, grad_rows)
    down_bias_grad_ref[...] += jnp.sum(grad_wide, axis=0, keepdims=True)
    pre_grad = (dot(down_weight_ref[...], grad_t.astype(bf16)) * slope).astype(bf16)
    dup_ref[...] += dot_nt(second, pre_grad)
    up_bias_grad_ref[...] += fold_lanes(pre_grad.astype(f32))
    second_grad = dot(up_weight_ref[...], pre_grad)
    gain_grad_ref[...] += fold_lanes(second_grad * unit)
    shift_grad_ref[...] += fold_lanes(second_grad)
    middle_grad = grad_t + column_norm_back(second_grad, unit, inverse, gain_ref[...])
    middle_grad_ref[...] = middle_grad
    middle_low = middle_grad.astype(bf16)
    dwo_ref[...] += dot_nt(spread_ref[...], middle_low)
    chosen_ref[...] = dot(output_weight_ref[...], middle_low)

    for part in range(per):
        lanes = slice(part * ROWS, (part + 1) * ROWS)
        picks = []
        for j in range(topk):
            span = slice(j * ROWS, (j + 1) * ROWS)
            row = index[j : j + 1, lanes]
            chosen = jnp.zeros((head, ROWS), f32)
            for expert in range(experts):
                chosen = jnp.where(
                    row == expert, chosen_ref[expert * head : (expert + 1) * head, lanes], chosen
                )
            attended = attended_ref[part, :, span]
            picks.append(jnp.sum(chosen * attended, axis=0, keepdims=True))
            back = (chosen * gate[j : j + 1, lanes]).astype(bf16)
            grad_t_ref[part, :, span] = back
            back = back.astype(f32)
            grad_rows_ref[part, span, :] = back.T.astype(bf16)
            delta_ref[part, :, span] = jnp.sum(back * attended, axis=0, keepdims=True)
        gates = [gate[j : j + 1, lanes] for j in range(topk)]
        mean = sum(g * p for g, p in zip(gates, picks))
        rows = [g * (p - mean) for g, p in zip(gates, picks)]
        spare = logit_grad_ref.shape[0] - experts
        logit = [place(index[:, lanes], rows, expert) for expert in range(experts)]
        logit.append(jnp.zeros((spare, ROWS), f32))
        logit_grad_ref[:, lanes] = jnp.concatenate(logit, axis=0).astype(bf16)

    @pl.when(step == pl.num_programs(0) - 1)
    def _():
        output_weight_grad_ref[...] = dwo_ref[...].astype(bf16)
        up_weight_grad_ref[...] = dup_ref[...].astype(bf16)
        down_weight_grad_ref[...] = ddown_ref[...].astype(bf16)


def middle_call(
    table, sources, tokens, index, gate, attended, weights, gain, shift, up_bias, down_bias, padded
):
    count, width = tokens.shape
    topk = index.shape[0]
    tiles, head, wide = attended.shape
    per = TILE // ROWS
    spread = 2 * weights[0].shape[0]
    hidden = 2 * weights[1].shape[0]
    keep = lambda shape: pl.BlockSpec(shape, lambda i, s: tuple(0 for _ in shape))
    rows = pl.BlockSpec((TILE, width), lambda i, s: (i, 0))
    columns = lambda n: pl.BlockSpec((n, TILE), lambda i, s: (0, i))
    tile = lambda shape: pl.BlockSpec((per,) + shape, lambda i, s: (i, 0, 0))
    shape = jax.ShapeDtypeStruct
    if len(sources) > 1:
        outs = [(keep((TILE, width)), shape((TILE, width), bf16))] * 4
    else:
        outs = [(rows, shape((count, width), bf16))]
    outs += [
        (columns(width), shape((width, count), f32)),
        (tile((head, wide)), shape((tiles, head, wide), bf16)),
        (tile((wide, head)), shape((tiles, wide, head), bf16)),
        (tile((1, wide)), shape((tiles, 1, wide), f32)),
        (columns(padded), shape((padded, count), bf16)),
        (keep((spread, width)), shape((spread, width), bf16)),
        (keep((width, hidden)), shape((width, hidden), bf16)),
        (keep((hidden, width)), shape((hidden, width), bf16)),
        (keep((width, 128)), shape((width, 128), f32)),
        (keep((width, 128)), shape((width, 128), f32)),
        (keep((hidden, 128)), shape((hidden, 128), f32)),
        (keep((1, width)), shape((1, width), f32)),
    ]
    return pl.pallas_call(
        functools.partial(middle_kernel, len(sources)),
        grid_spec=pltpu.PrefetchScalarGridSpec(
            num_scalar_prefetch=1,
            grid=(count // TILE,),
            in_specs=piece_specs(sources)
            + [rows, columns(topk), columns(topk), tile((head, wide))]
            + [keep(w.shape) for w in weights]
            + [keep((width, 1)), keep((width, 1)), keep((hidden, 1)), keep((width, 1))],
            out_specs=[x for x, _ in outs],
            scratch_shapes=[
                pltpu.VMEM((TILE, width), bf16),
                pltpu.VMEM((spread, width), bf16),
                pltpu.VMEM((width, hidden), bf16),
                pltpu.VMEM((hidden, width), bf16),
                pltpu.VMEM((spread, TILE), bf16),
                pltpu.VMEM((spread, TILE), f32),
                pltpu.VMEM((spread, width), f32),
                pltpu.VMEM((width, hidden), f32),
                pltpu.VMEM((hidden, width), f32),
            ],
        ),
        out_shape=[x for _, x in outs],
        compiler_params=params(),
        cost_estimate=cost(44),
        name="middle",
    )(table, *sources, tokens, index, gate, attended, *weights, gain, shift, up_bias, down_bias)


def query_back_kernel(
    table_ref,
    first_ref,
    index_ref,
    dq_ref,
    own_ref,
    other_ref,
    logit_grad_ref,
    router_ref,
    partial_ref,
    keep_ref,
    send_ref,
    router_grad_ref,
    query_weight_ref,
    placed_ref,
    dwq_ref,
    dr_ref,
):
    step = pl.program_id(0)
    topk = index_ref.shape[0]
    head = dq_ref.shape[1]
    experts = query_weight_ref.shape[1] // head

    @pl.when(step == 0)
    def _():
        join_rows(table_ref[SHARD], own_ref, other_ref, query_weight_ref)
        dwq_ref[...] = jnp.zeros(dwq_ref.shape, f32)
        dr_ref[...] = jnp.zeros(dr_ref.shape, f32)

    index = index_ref[...]
    for part in range(TILE // ROWS):
        lanes = slice(part * ROWS, (part + 1) * ROWS)
        pieces = [dq_ref[part, :, j * ROWS : (j + 1) * ROWS] for j in range(topk)]
        for expert in range(experts):
            placed_ref[expert * head : (expert + 1) * head, lanes] = place(
                index[:, lanes], pieces, expert
            ).astype(bf16)
    first = first_ref[...]
    dwq_ref[...] += dot_nt(first, placed_ref[...])
    dr_ref[...] += dot_nt(first, logit_grad_ref[...])
    partial_ref[...] = dot(query_weight_ref[...], placed_ref[...]) + dot(
        router_ref[...], logit_grad_ref[...]
    )

    @pl.when(step == pl.num_programs(0) - 1)
    def _():
        router_grad_ref[...] = dr_ref[...]
        size = keep_ref.shape[2]
        shard, core, side = table_ref[SHARD], table_ref[CORE], table_ref[SIDE]
        for target, last in ((keep_ref, core), (send_ref, 1 - core)):
            for i, half in enumerate((shard, 1 - shard)):
                for j, part in enumerate((side, 1 - side)):
                    at = ((half * 2 + last) * 2 + part) * size
                    rows = pl.ds(pl.multiple_of(at, size), size)
                    target[i, j] = dwq_ref[rows, :].astype(bf16)


def query_back_call(table, first, index, dq, own, other, logit_grad, router):
    width, count = first.shape
    topk = index.shape[0]
    tiles, head, wide = dq.shape
    padded = router.shape[1]
    spread = own.shape[1]
    keep = lambda shape: pl.BlockSpec(shape, lambda i, s: tuple(0 for _ in shape))
    columns = lambda n: pl.BlockSpec((n, TILE), lambda i, s: (0, i))
    shape = jax.ShapeDtypeStruct
    quarters = (2, 2, width // 8, spread)
    return pl.pallas_call(
        query_back_kernel,
        grid_spec=pltpu.PrefetchScalarGridSpec(
            num_scalar_prefetch=1,
            grid=(count // TILE,),
            in_specs=[
                columns(width),
                columns(topk),
                pl.BlockSpec((TILE // ROWS, head, wide), lambda i, s: (i, 0, 0)),
                keep(own.shape),
                keep(other.shape),
                columns(padded),
                keep(router.shape),
            ],
            out_specs=[columns(width), keep(quarters), keep(quarters), keep(router.shape)],
            scratch_shapes=[
                pltpu.VMEM((width, spread), bf16),
                pltpu.VMEM((spread, TILE), bf16),
                pltpu.VMEM((width, spread), f32),
                pltpu.VMEM(router.shape, f32),
            ],
        ),
        out_shape=[
            shape((width, count), f32),
            shape(quarters, bf16),
            shape(quarters, bf16),
            shape(router.shape, f32),
        ],
        compiler_params=params(),
        cost_estimate=cost(0),
        name="query_back",
    )(table, first, index, dq, own, other, logit_grad, router)


def first_back_kernel(pieces, table_ref, *refs):
    tokens_ref, first_ref, partial_ref, middle_grad_ref = refs[:4]
    sources = refs[4 : 4 + pieces]
    kv_weight_ref, gain_ref, rest_ref = refs[4 + pieces : 7 + pieces]
    refs = refs[7 + pieces :]
    outs = 4 if pieces > 1 else 1
    tokens_grad_refs = refs[:outs]
    keep_ref, send_ref, total_ref, gain_grad_ref, shift_grad_ref, dkv_ref = refs[outs:]
    step = pl.program_id(0)
    pair = kv_weight_ref.shape[1]

    @pl.when(step == 0)
    def _():
        total_ref[:, :pair] = jnp.zeros((total_ref.shape[0], pair), f32)
        for ref in (gain_grad_ref, shift_grad_ref):
            ref[...] = jnp.zeros(ref.shape, ref.dtype)

    unit, inverse = column_norm(tokens_ref[...].astype(f32).T)
    if pieces == 1:
        dkv_ref[...] = sources[0][...]
    else:
        low_ref, high_ref, own_ref = sources
        own = table_ref[OWN_SLOT]
        for chosen, ref, half in (
            (table_ref[LOW_SLOT], low_ref, 0),
            (table_ref[HIGH_SLOT], high_ref, 0),
            (own, own_ref, 0),
            (own + 1, own_ref, 1),
        ):

            @pl.when(step == chosen)
            def _():
                dkv_ref[...] = ref[half * PART : (half + 1) * PART, :]

    dkv = dkv_ref[...]
    total_ref[:, :pair] += dot(first_ref[...], dkv)
    first_grad = partial_ref[...] + dot_nt(kv_weight_ref[...], dkv)
    gain_grad_ref[...] += fold_lanes(first_grad * unit)
    shift_grad_ref[...] += fold_lanes(first_grad)
    total = middle_grad_ref[...] + column_norm_back(first_grad, unit, inverse, gain_ref[...])
    store_piece(step, tokens_grad_refs, total.T.astype(bf16))

    @pl.when(step == pl.num_programs(0) - 1)
    def _():
        lane = lax.broadcasted_iota(jnp.int32, rest_ref.shape, 1)
        gains = jnp.sum(gain_grad_ref[...], axis=1, keepdims=True)
        shifts = jnp.sum(shift_grad_ref[...], axis=1, keepdims=True)
        rest = jnp.where(lane == 0, gains, jnp.where(lane == 1, shifts, rest_ref[...]))
        total_ref[:, pair:] = rest
        size = keep_ref.shape[1]
        shard, core = table_ref[SHARD], table_ref[CORE]
        for target, last in ((keep_ref, core), (send_ref, 1 - core)):
            for i, half in enumerate((shard, 1 - shard)):
                rows = pl.ds(pl.multiple_of((half * 2 + last) * size, size), size)
                target[i] = total_ref[rows, :].astype(bf16)


def first_back_call(table, tokens, first, partial, middle_grad, dkv, kv_weight, gain, rest):
    count, width = tokens.shape
    pair = kv_weight.shape[1]
    wide = pair + rest.shape[1]
    columns = lambda n: pl.BlockSpec((n, TILE), lambda i, t: (0, i))
    rows = lambda n: pl.BlockSpec((TILE, n), lambda i, t: (i, 0))
    keep = lambda shape: pl.BlockSpec(shape, lambda i, t: tuple(0 for _ in shape))
    shape = jax.ShapeDtypeStruct
    quarters = (2, width // 4, wide)
    if len(dkv) > 1:
        outs = [(keep((TILE, width)), shape((TILE, width), bf16))] * 4
    else:
        outs = [(rows(width), shape((count, width), bf16))]
    outs += [(keep(quarters), shape(quarters, bf16))] * 2
    return pl.pallas_call(
        functools.partial(first_back_kernel, len(dkv)),
        grid_spec=pltpu.PrefetchScalarGridSpec(
            num_scalar_prefetch=1,
            grid=(count // TILE,),
            in_specs=[rows(width), columns(width), columns(width), columns(width)]
            + piece_specs(dkv)
            + [keep(kv_weight.shape), keep((width, 1)), keep(rest.shape)],
            out_specs=[x for x, _ in outs],
            scratch_shapes=[
                pltpu.VMEM((width, wide), f32),
                pltpu.VMEM((width, 128), f32),
                pltpu.VMEM((width, 128), f32),
                pltpu.VMEM((TILE, pair), bf16),
            ],
        ),
        out_shape=[x for _, x in outs],
        compiler_params=params(),
        cost_estimate=cost(7),
        name="first_back",
    )(table, tokens, first, partial, middle_grad, *dkv, kv_weight, gain, rest)


def after(value, *others):
    return lax.optimization_barrier((value,) + others)[0]


def other_half(value):
    return lax.ppermute(value, "shard", [(0, 1), (1, 0)])


def join(value, other):
    low = lax.axis_index("shard") == 0
    return jnp.concatenate([jnp.where(low, value, other), jnp.where(low, other, value)], axis=0)


def swap(value, mask):
    count = lax.axis_size("ctx")
    return lax.ppermute(value, "ctx", [(i, i ^ mask) for i in range(count)])


def bit_masks(count):
    return [1 << k for k in reversed(range(count.bit_length() - 1))]


def key_orders(count):
    masks = bit_masks(count)
    return masks, masks[:1] + masks[1:-1][::-1] + masks[-1:]


def slots_of(masks):
    return [sum(m for k, m in enumerate(masks) if j >> k & 1) for j in range(1 << len(masks))]


def gather_keys(shared):
    low_order, high_order = key_orders(lax.axis_size("ctx"))
    got = swap(shared, low_order[0])
    low = jnp.concatenate([shared[:PART], got[:PART]], axis=0)
    high = jnp.concatenate([shared[PART:], got[PART:]], axis=0)
    for low_mask, high_mask in zip(low_order[1:-1], high_order[1:-1]):
        low_got, high_got = swap(low, low_mask), swap(high, high_mask)
        low = jnp.concatenate([low, low_got], axis=0)
        high = jnp.concatenate([high, high_got], axis=0)
    return (low, swap(low, low_order[-1])), (high, swap(high, high_order[-1]))


def add_low(a, b):
    return (a.astype(f32) + b.astype(f32)).astype(bf16)


def step_down(total, mask):
    half = total.shape[0] // 2
    return total[:half], swap(total[half:].astype(bf16), mask)


def double(total, mask):
    other = swap(total, mask)
    low = (lax.axis_index("ctx") // mask) % 2 == 0
    return jnp.concatenate([jnp.where(low, total, other), jnp.where(low, other, total)], axis=0)


def home_plan(count, block):
    half = count // 2
    if block != 4 * PART or block * half != PROMPT or block != CLEN or half % 2:
        return None
    sends = [None] * count
    hops = [[], [], []]
    for a in range(half // 2):
        b = half - 1 - a
        p, q = a + half, b + half
        sends[a], sends[b] = (0, 1, 2, 3), (2, 3, 0, 1)
        sends[p] = sends[q] = (0, 3, 1, 2)
        hops[0] += [(a, b), (b, a)]
        hops[1] += [(a, p), (p, a), (b, q), (q, b)]
        hops[2] += [(a, q), (b, p), (p, a), (q, b)]
    places = [[(i, sends[i][0]), (i, sends[i][1]), None, None] for i in range(count)]
    for k, hop in enumerate(hops):
        for source, target in hop:
            places[target][k + 1] = (source, sends[source][k + 1])
    return sends, hops, places


def plan_rows(plan, count):
    sends, _, places = plan
    lower, prompt = HALF // PART, PROMPT // PART
    where = [[source * 4 + quarter for source, quarter in row] for row in places]
    low_slot = [next(k for k in range(4) if row[k] < lower) for row in where]
    high_slot = [next(k for k in range(4) if lower <= row[k] < prompt) for row in where]
    own_slot = [2 if i < count // 2 else 0 for i in range(count)]
    own_at = [[row[k] % 4, row[k + 1] % 4] for row, k in zip(where, own_slot)]
    low_slots, high_slots = (slots_of(masks) for masks in key_orders(count))
    rows = []
    for i in range(count):
        row = list(sends[i]) + [int(i < count // 2), low_slot[i], high_slot[i], own_slot[i]]
        row += [0, i % 2, i // 2 % 2]
        row += [x * PART + r for x in where[i] for r in range(0, PART, ROWS)]
        row += [where[i ^ m][low_slot[i ^ m]] for m in low_slots]
        row += [where[i ^ m][high_slot[i ^ m]] for m in high_slots]
        row += [prompt + x for x in own_at[i] + own_at[i ^ (count // 2)]]
        rows.append(row)
    return rows


def send_pieces(pieces, plan):
    got = [lax.ppermute(piece, "ctx", hop) for piece, hop in zip(pieces[1:], plan[1])]
    return pieces[0], pieces[1], *got


def send_back(pieces, plan):
    hops = [[(t, s) for s, t in hop] for hop in plan[1]]
    got = [lax.ppermute(piece, "ctx", hop) for piece, hop in zip(pieces[1:], hops)]
    return pieces[0], pieces[1], *got


def per_device(
    tokens,
    expert_index,
    first_gain,
    first_shift,
    router_weight,
    query_weight,
    key_weight,
    value_weight,
    output_weight,
    second_gain,
    second_shift,
    up_weight,
    up_bias,
    down_weight,
    down_bias,
    out_grad,
):
    groups, block, width = tokens.shape
    assert groups == 1 and lax.axis_size("shard") == 2
    count = lax.axis_size("ctx")
    me = lax.axis_index("ctx")
    shard = lax.axis_index("shard")
    experts = router_weight.shape[1]
    topk = expert_index.shape[-1]
    head = key_weight.shape[1]
    pair = 2 * head
    padded = 32
    tiles = block // ROWS
    key_table = BASES + tiles
    plan = home_plan(count, block)
    if plan:
        table = jnp.array(plan_rows(plan, count), jnp.int32)[me]
        table = table + shard * (jnp.arange(table.shape[0], dtype=jnp.int32) == SHARD)
        packed = pack_call(table, tokens[0], expert_index[0].T)
        sources = send_pieces(packed, plan)
        key_weight, packed = lax.optimization_barrier((key_weight, packed))
    else:
        base = me * block
        numbers = [0, 0, 0, 0, 0, 0, 0, 0, shard, me % 2, me // 2 % 2]
        table = jnp.concatenate(
            [
                jnp.stack([jnp.int32(x) for x in numbers]),
                base + jnp.arange(tiles, dtype=jnp.int32) * ROWS,
                jnp.arange((PROMPT + CLEN) // PART, dtype=jnp.int32),
            ]
        )
        sources = (tokens[0],)

    spare = jnp.zeros((key_weight.shape[0], padded - experts), bf16)
    vectors = [first_gain, first_shift, second_gain, second_shift, down_bias]
    half_width = width // 2
    small = jnp.concatenate(
        [key_weight, value_weight, router_weight, spare]
        + [v[:, None] for v in vectors]
        + [up_bias.reshape(half_width, -1)],
        axis=1,
    )
    small = join(small, other_half(small))
    query_other = other_half(after(query_weight, small))
    kv_weight = small[:, :pair]
    router = small[:, pair : pair + padded]
    at = pair + padded
    columns = [small[:, at + i : at + i + 1].astype(f32) for i in range(len(vectors))]
    gain_one, shift_one, gain_two, shift_two, down_bias_all = columns
    up_bias_all = small[:, at + len(vectors) :].reshape(-1, 1).astype(f32)

    both_weights = jnp.concatenate([output_weight, down_weight], axis=0)
    early_work = (both_weights, router, up_bias_all, *columns)
    if plan:
        grads = pack_call(after(table, small), out_grad[0])
        early_work += tuple(grads)
    table, early_work = lax.optimization_barrier((table, early_work))
    both_weights, router, up_bias_all, *rest = early_work
    gain_one, shift_one, gain_two, shift_two, down_bias_all = rest[: len(vectors)]
    grads = rest[len(vectors) :]
    first_out = first_call(table, sources, block, topk, gain_one, shift_one, kv_weight)
    if plan:
        first, shared, own, index, flat = first_out
        low_keys, high_keys = gather_keys(shared)
        partner = swap(own, count // 2)
        high_keys += (own, partner)
    else:
        first, kv = first_out
        flat = tokens[0]
        index = expert_index[0].T
        gathered = lax.all_gather(kv, "ctx", axis=0, tiled=True)
        segment = jnp.maximum(base, PROMPT) // CLEN * CLEN
        own = lax.dynamic_slice_in_dim(gathered, segment, CLEN, 0)
        quarter = HALF // 2
        low_keys = (gathered[:quarter], gathered[quarter:HALF])
        high_keys = (
            gathered[HALF : HALF + quarter], gathered[HALF + quarter : PROMPT],
            own[: CLEN // 2], own[CLEN // 2 :],
        )

    qt, q, gate = query_call(table, first, query_weight, query_other, router, index, head)
    both_other = other_half(after(both_weights, query_other))
    weights = (
        output_weight, down_weight, both_other, up_weight, other_half(after(up_weight, query_other))
    )
    if plan:
        grads = send_pieces(after(tuple(grads), *low_keys, *high_keys), plan)
    else:
        grads = (out_grad[0],)
    keys = low_keys + high_keys
    attended, lse = attend_call(key_table, keys, table, qt)
    outs = 4 if plan else 1
    middle = middle_call(
        table, grads, flat, index, gate, attended, weights,
        gain_two, shift_two, up_bias_all, down_bias_all, padded,
    )
    layer_out = middle[:outs]
    (
        middle_grad, grad_t, grad_rows, delta, logit_grad,
        output_weight_grad, up_weight_grad, down_weight_grad,
        second_gain_grad, second_shift_grad, up_bias_grad, down_bias_grad,
    ) = middle[outs:]

    early = lax.psum((output_weight_grad, up_weight_grad, down_weight_grad), ("ctx", "shard"))
    if plan:
        layer_out = send_back(layer_out, plan)
    kinds = (f32, bf16, f32, bf16, f32, bf16) if plan else (bf16,) * 6
    dq, *key_grads = attend_back_call(
        key_table, keys, kinds, table, qt, q, grad_t, grad_rows, lse, delta
    )
    dq, key_grads, layer_out = lax.optimization_barrier((dq, key_grads, layer_out))
    if plan:
        low_near, low_far, high_near, high_far, own_near, own_far = key_grads
        low_got, high_got = swap(low_far, 1), swap(high_far, 1)
    partial, keep, send, router_grad = query_back_call(
        table, first, index, dq, query_weight, query_other, logit_grad, router
    )
    keep, send, router_grad, partial, *early = lax.optimization_barrier(
        (keep, send, router_grad, partial, *early)
    )
    total = add_low(keep, swap(send, 1))
    if plan:
        low_order, high_order = key_orders(count)
        low_keep, low_got = step_down(low_near + low_got.astype(f32), low_order[2])
        high_keep, high_got = step_down(high_near + high_got.astype(f32), high_order[2])
        query_got = other_half(total[1])
    sums = (second_gain_grad, second_shift_grad, down_bias_grad, up_bias_grad)
    total, layer_out, *sums = lax.optimization_barrier((total, layer_out, *sums))
    second_gain_grad, second_shift_grad, down_bias_grad, up_bias_grad = sums
    rest = jnp.concatenate(
        [
            jnp.zeros((width, 2), f32),
            jnp.sum(second_gain_grad, axis=1)[:, None],
            jnp.sum(second_shift_grad, axis=1)[:, None],
            down_bias_grad[0][:, None],
            jnp.sum(up_bias_grad, axis=1).reshape(width, -1),
        ],
        axis=1,
    )
    bias_columns = rest.shape[1] - 5
    rest = jnp.pad(rest, ((0, 0), (0, padded - rest.shape[1])))
    rest = jnp.concatenate([rest, router_grad, jnp.zeros((width, 128 - 2 * padded), f32)], axis=1)
    if plan:
        low_got, high_got, total, own_far = lax.optimization_barrier(
            (low_got, high_got, total, own_far)
        )
        own_got = swap(own_far, count // 2)
        low_keep, low_got = step_down(low_keep + low_got.astype(f32), low_order[1])
        high_keep, high_got = step_down(high_keep + high_got.astype(f32), high_order[1])
        low_got, high_got = lax.optimization_barrier((low_got, high_got))
        low_sum = low_keep + low_got.astype(f32)
        high_sum = high_keep + high_got.astype(f32)
        both = jnp.concatenate([low_sum[PART:], high_sum[PART:]], axis=0).astype(bf16)
        both = swap(both, low_order[0])
        total = add_low(total[0], query_got)
        query_got = swap(total[1], 2)
        both, total = lax.optimization_barrier((both, total))
        dkv = (
            add_low(low_sum[:PART], both[:PART]),
            add_low(high_sum[:PART], both[PART:]),
            add_low(own_near, own_got),
        )
    else:
        rows = count * block - PROMPT
        dall = jnp.concatenate(key_grads[:4] + [jnp.zeros((rows, pair), bf16)])
        own_grad = jnp.concatenate(key_grads[4:])
        own_grad = jnp.where(base >= PROMPT, own_grad, jnp.zeros_like(own_grad))
        dall = lax.dynamic_update_slice_in_dim(dall, own_grad, segment, 0)
        dkv = (lax.psum_scatter(dall, "ctx", scatter_dimension=0, tiled=True),)
        total = add_low(total[0], other_half(total[1]))
        query_got = swap(total[1], 2)
    done = first_back_call(
        table, flat, first, partial, middle_grad, dkv, kv_weight, gain_one, rest
    )
    tokens_grad = done[:outs]
    keep, send = done[outs:]
    small_sum = add_low(keep, swap(send, 1))
    small_sum = add_low(small_sum[0], other_half(small_sum[1]))
    small_sum = add_low(small_sum, swap(small_sum, 2))
    total = add_low(total[0], query_got)
    for mask in bit_masks(count)[:-2][::-1]:
        got, small_got = swap(total, mask), swap(small_sum, mask)
        total, small_sum = add_low(total, got), add_low(small_sum, small_got)
    if plan:
        tokens_grad = send_back(tokens_grad, plan)
    query_weight_grad = double(double(total, 2), 1).astype(f32)
    small_grad = double(small_sum, 1).astype(f32)
    layer_out = unpack_call(table, layer_out) if plan else layer_out[0]
    tokens_grad = unpack_call(table, tokens_grad) if plan else tokens_grad[0]
    output_weight_grad, up_weight_grad, down_weight_grad = (
        lax.dynamic_slice_in_dim(x, shard * (x.shape[0] // 2), x.shape[0] // 2, 0).astype(f32)
        for x in early
    )
    return (
        layer_out[None],
        tokens_grad[None],
        small_grad[:, pair],
        small_grad[:, pair + 1],
        small_grad[:, pair + padded : pair + padded + experts],
        query_weight_grad,
        small_grad[:, :head],
        small_grad[:, head:pair],
        output_weight_grad,
        small_grad[:, pair + 2],
        small_grad[:, pair + 3],
        up_weight_grad,
        small_grad[:, pair + 5 : pair + 5 + bias_columns].reshape(-1),
        down_weight_grad,
        small_grad[:, pair + 4],
    )


def solution(mesh):
    split = P("shard", "ctx", None)
    vector = P("shard")
    matrix = P("shard", None)
    in_specs = (
        split, split, vector, vector, matrix, matrix, matrix, matrix, matrix,
        vector, vector, matrix, vector, matrix, vector, split,
    )
    out_specs = (
        split, split, vector, vector, matrix, matrix, matrix, matrix, matrix,
        vector, vector, matrix, vector, matrix, vector,
    )
    return jax.shard_map(
        per_device, mesh=mesh, in_specs=in_specs, out_specs=out_specs, check_vma=False
    )
```

```python
import functools
import math

import jax
import jax.numpy as jnp
from jax import lax
from jax.experimental import pallas as pl
from jax.experimental.pallas import tpu as pltpu
from jax.sharding import PartitionSpec as P

PROMPT = 8192
CLEN = 1024
ROWS = 128
TILE = 256
FULL = 1024
PART = 256
HALF = PROMPT // 2
VMEM = 60 << 20

PIECES, IS_PROMPT, LOW_SLOT, HIGH_SLOT, OWN_SLOT, SHARD, CORE, SIDE, BASES = 0, 4, 5, 6, 7, 8, 9, 10, 11
norm_eps = 1e-05
mask_fill = -1e30
LOG2E = math.log2(math.e)
bf16 = jnp.bfloat16
f32 = jnp.float32


def dot(a, b):
    return lax.dot_general(a, b, (((1,), (0,)), ((), ())), preferred_element_type=f32)


def dot_tn(a, b):
    return lax.dot_general(a, b, (((0,), (0,)), ((), ())), preferred_element_type=f32)


def dot_nt(a, b):
    return lax.dot_general(a, b, (((1,), (1,)), ((), ())), preferred_element_type=f32)


def params(**kw):
    return pltpu.CompilerParams(vmem_limit_bytes=VMEM, **kw)


def cost(us):
    return pl.CostEstimate(flops=int(us * 1.15e9), transcendentals=0, bytes_accessed=0)


def whole(shape):
    return pl.BlockSpec(shape, lambda i: tuple(0 for _ in shape))


def column_norm(values):
    center = jnp.mean(values, axis=0, keepdims=True)
    centred = values - center
    spread = jnp.mean(centred * centred, axis=0, keepdims=True)
    inverse = lax.rsqrt(spread + norm_eps)
    return centred * inverse, inverse


def column_norm_back(grad, unit, inverse, gain):
    scaled = grad * gain
    inner = (
        scaled
        - jnp.mean(scaled, axis=0, keepdims=True)
        - unit * jnp.mean(scaled * unit, axis=0, keepdims=True)
    )
    return inner * inverse


def fold_lanes(values):
    width = values.shape[1]
    total = values[:, :128]
    for start in range(128, width, 128):
        total = total + values[:, start : start + 128]
    return total


def pick_piece(step, table_ref, sources, target_ref):
    if len(sources) == 1:
        target_ref[...] = sources[0][...]
        return
    keep, own, *got = sources
    rows = target_ref.shape[0]
    prompt = table_ref[IS_PROMPT] == 1
    which = ((step == 0), (step == 1) & jnp.logical_not(prompt), (step == 1) & prompt)
    for chosen, ref in zip(which + ((step == 2), (step == 3)), (keep, own, *got)):

        @pl.when(chosen)
        def _():
            target_ref[...] = ref[:rows, :]


def store_piece(step, targets, value):
    if len(targets) == 1:
        targets[0][...] = value
        return
    for k, ref in enumerate(targets):

        @pl.when(step == k)
        def _():
            ref[...] = value


def piece_specs(pieces):
    if len(pieces) == 1:
        return [pl.BlockSpec((TILE, pieces[0].shape[1]), lambda i, t: (i, 0))]
    return [pl.BlockSpec(x.shape, lambda i, t: (0, 0)) for x in pieces]


def pack_kernel(table_ref, *refs):
    rows_ref, *refs = refs
    index = refs.pop(0) if len(refs) > 4 else None
    for k, ref in enumerate(refs):
        span = pl.ds(pl.multiple_of(table_ref[PIECES + k] * PART, PART), PART)
        ref[:PART, :] = rows_ref[span, :]
        if index is not None:
            chosen = index[:, span].astype(f32)
            blank = jnp.zeros((16 - index.shape[0], PART), f32)
            ref[PART:, :] = jnp.concatenate(
                [jnp.concatenate([chosen, blank], axis=0)] * (ref.shape[1] // PART), axis=1
            ).astype(bf16)


def pack_call(table, rows, index=None):
    count, width = rows.shape
    out = (count // 4 + (0 if index is None else 16), width)
    inputs = (rows,) if index is None else (rows, index)
    return pl.pallas_call(
        pack_kernel,
        grid_spec=pltpu.PrefetchScalarGridSpec(
            num_scalar_prefetch=1,
            grid=(1,),
            in_specs=[pl.BlockSpec(x.shape, lambda i, t: (0, 0)) for x in inputs],
            out_specs=[pl.BlockSpec(out, lambda i, t: (0, 0))] * 4,
        ),
        out_shape=[jax.ShapeDtypeStruct(out, bf16)] * 4,
        compiler_params=params(),
        cost_estimate=cost(2),
        name="pack",
    )(table, *inputs)


def unpack_kernel(table_ref, keep_ref, own_ref, *refs):
    *got, out_ref = refs
    prompt = table_ref[IS_PROMPT] == 1
    place_of = lambda k: pl.ds(pl.multiple_of(table_ref[PIECES + k] * PART, PART), PART)
    out_ref[place_of(0), :] = keep_ref[...]
    out_ref[place_of(2), :] = got[1][...]
    out_ref[place_of(3), :] = got[2][...]

    @pl.when(prompt)
    def _():
        out_ref[place_of(1), :] = got[0][...]

    @pl.when(jnp.logical_not(prompt))
    def _():
        out_ref[place_of(1), :] = own_ref[...]


def unpack_call(table, pieces):
    rows, width = pieces[0].shape
    return pl.pallas_call(
        unpack_kernel,
        grid_spec=pltpu.PrefetchScalarGridSpec(
            num_scalar_prefetch=1,
            grid=(1,),
            in_specs=[pl.BlockSpec((rows, width), lambda i, t: (0, 0))] * 5,
            out_specs=pl.BlockSpec((4 * rows, width), lambda i, t: (0, 0)),
        ),
        out_shape=jax.ShapeDtypeStruct((4 * rows, width), bf16),
        compiler_params=params(),
        cost_estimate=cost(0),
        name="unpack",
    )(table, *pieces)


def first_kernel(pieces, table_ref, *refs):
    sources = refs[:pieces]
    gain_ref, shift_ref, kv_weight_ref = refs[pieces : pieces + 3]
    refs = refs[pieces + 3 :]
    step = pl.program_id(0)
    first_ref = refs[0]
    tokens_ref = refs[-1]
    pick_piece(step, table_ref, sources, tokens_ref)
    unit, _ = column_norm(tokens_ref[...].astype(f32).T)
    first = (unit * gain_ref[...] + shift_ref[...]).astype(bf16)
    first_ref[...] = first
    kv = dot_tn(kv_weight_ref[...], first).T.astype(bf16)
    if pieces == 1:
        refs[1][...] = kv
        return
    shared_ref, own_ref, index_ref, flat_ref, _ = refs[1:]
    flat_ref[...] = tokens_ref[...]
    topk, rows = index_ref.shape
    keep, own, *got = sources
    prompt = table_ref[IS_PROMPT] == 1
    which = ((step == 0), (step == 1) & jnp.logical_not(prompt), (step == 1) & prompt)
    for chosen, ref in zip(which + ((step == 2), (step == 3)), (keep, own, *got)):

        @pl.when(chosen)
        def _():
            index_ref[...] = ref[PART:, :rows][:topk, :].astype(f32).astype(jnp.int32)

    for slot, half in ((LOW_SLOT, 0), (HIGH_SLOT, 1)):

        @pl.when(step == table_ref[slot])
        def _():
            shared_ref[half * PART : (half + 1) * PART, :] = kv

    for half in range(2):

        @pl.when(step == table_ref[OWN_SLOT] + half)
        def _():
            own_ref[half * PART : (half + 1) * PART, :] = kv


def first_call(table, sources, count, topk, gain, shift, kv_weight):
    width, pair = kv_weight.shape
    keep = lambda shape: pl.BlockSpec(shape, lambda i, t: (0, 0))
    shape = jax.ShapeDtypeStruct
    split = len(sources) > 1
    outs = [(pl.BlockSpec((width, TILE), lambda i, t: (0, i)), shape((width, count), bf16))]
    rows = lambda n: pl.BlockSpec((TILE, n), lambda i, t: (i, 0))
    if split:
        outs += [
            (keep((2 * PART, pair)), shape((2 * PART, pair), bf16)),
            (keep((2 * PART, pair)), shape((2 * PART, pair), bf16)),
            (pl.BlockSpec((topk, TILE), lambda i, t: (0, i)), shape((topk, count), jnp.int32)),
            (rows(width), shape((count, width), bf16)),
        ]
    else:
        outs += [(rows(pair), shape((count, pair), bf16))]
    return pl.pallas_call(
        functools.partial(first_kernel, len(sources)),
        grid_spec=pltpu.PrefetchScalarGridSpec(
            num_scalar_prefetch=1,
            grid=(count // TILE,),
            in_specs=piece_specs(sources)
            + [keep((width, 1)), keep((width, 1)), keep((width, pair))],
            out_specs=[x for x, _ in outs],
            scratch_shapes=[pltpu.VMEM((TILE, width), bf16)],
        ),
        out_shape=[x for _, x in outs],
        compiler_params=params(),
        cost_estimate=cost(5),
        name="first_norm",
    )(table, *sources, gain, shift, kv_weight)


def join_rows(shard, own_ref, other_ref, all_ref, start=0):
    half = own_ref.shape[0]
    all_ref[pl.ds(pl.multiple_of(shard * half, half), half), :] = own_ref[...]
    rows = pl.ds(pl.multiple_of((1 - shard) * half, half), half)
    all_ref[rows, :] = other_ref[start : start + half, :]


def query_kernel(
    table_ref, first_ref, own_ref, other_ref, router_ref, index_ref,
    qt_ref, q_ref, gate_ref, query_weight_ref,
):
    topk = index_ref.shape[0]

    @pl.when(pl.program_id(0) == 0)
    def _():
        join_rows(table_ref[SHARD], own_ref, other_ref, query_weight_ref)

    head = qt_ref.shape[1]
    experts = query_weight_ref.shape[1] // head
    first = first_ref[...]
    projected = dot_tn(query_weight_ref[...], first)
    logits = dot_tn(router_ref[...], first)
    index = index_ref[...]
    picked = jnp.zeros(index.shape, f32)
    for expert in range(experts):
        picked = jnp.where(index == expert, logits[expert : expert + 1, :], picked)
    picked = jnp.exp(picked - jnp.max(picked, axis=0, keepdims=True))
    gate_ref[...] = picked / jnp.sum(picked, axis=0, keepdims=True)
    for part in range(TILE // ROWS):
        lanes = slice(part * ROWS, (part + 1) * ROWS)
        for j in range(topk):
            row = index[j : j + 1, lanes]
            chosen = jnp.zeros((head, ROWS), f32)
            for expert in range(experts):
                chosen = jnp.where(
                    row == expert, projected[expert * head : (expert + 1) * head, lanes], chosen
                )
            qt_ref[part, :, j * ROWS : (j + 1) * ROWS] = chosen.astype(bf16)
            q_ref[part, j * ROWS : (j + 1) * ROWS, :] = chosen.T.astype(bf16)


def query_call(table, first, own, other, router, index, head):
    width, count = first.shape
    topk = index.shape[0]
    tiles = count // ROWS
    per = TILE // ROWS
    keep = lambda shape: pl.BlockSpec(shape, lambda i, s: (0, 0))
    return pl.pallas_call(
        query_kernel,
        grid_spec=pltpu.PrefetchScalarGridSpec(
            num_scalar_prefetch=1,
            grid=(count // TILE,),
            in_specs=[
                pl.BlockSpec((width, TILE), lambda i, s: (0, i)),
                keep(own.shape),
                keep(other.shape),
                keep(router.shape),
                pl.BlockSpec((topk, TILE), lambda i, s: (0, i)),
            ],
            out_specs=[
                pl.BlockSpec((per, head, topk * ROWS), lambda i, s: (i, 0, 0)),
                pl.BlockSpec((per, topk * ROWS, head), lambda i, s: (i, 0, 0)),
                pl.BlockSpec((topk, TILE), lambda i, s: (0, i)),
            ],
            scratch_shapes=[pltpu.VMEM((width, own.shape[1]), bf16)],
        ),
        out_shape=[
            jax.ShapeDtypeStruct((tiles, head, topk * ROWS), bf16),
            jax.ShapeDtypeStruct((tiles, topk * ROWS, head), bf16),
            jax.ShapeDtypeStruct((topk, count), f32),
        ],
        compiler_params=params(),
        cost_estimate=cost(10),
        name="queries",
    )(table, first, own, other, router, index)


def tile_ranges(base):
    prompt = base < PROMPT
    begin = jnp.where(prompt, base // FULL * FULL, PROMPT)
    position = jnp.where(prompt, begin, PROMPT + (base - PROMPT) // CLEN * CLEN)
    parts = (base + ROWS - position + PART - 1) // PART
    return begin // FULL, begin, position, parts


def allowed_mask(position, base, width):
    key_pos = position + lax.broadcasted_iota(jnp.int32, (PART, width), 0)
    query_pos = base + lax.rem(lax.broadcasted_iota(jnp.int32, (PART, width), 1), ROWS)
    return key_pos <= query_pos


def for_slots(refs, table_ref, start, visit):
    slot = 0
    for ref in refs:
        for row in range(0, ref.shape[0], PART):
            place_of = pl.multiple_of(table_ref[start + slot] * PART, PART)
            visit(ref, row, pl.ds(place_of, PART))
            slot += 1


def attend_kernel(start, buffers, table_ref, *refs):
    sources = refs[:buffers]
    qt_ref = refs[buffers]
    out_ref, factor_ref, probs_ref = refs[buffers + 1 : buffers + 4]
    refs = refs[buffers + 4 :]
    kv_ref, vt_ref, knorm_ref, acc_ref, max_ref, full_ref, part_ref, full_sem, part_sem, done_ref = refs
    tile = pl.program_id(0)
    head, width = qt_ref.shape[1:]
    factor = LOG2E * head ** (-0.5)

    @pl.when(tile == 0)
    def _():
        knorm_ref[0] = 0.0
        done_ref[0] = 0
        done_ref[1] = 0

        def turn(ref, row, span):
            rows = ref[row : row + PART, :]
            kv_ref[span, :] = rows
            both = rows.T
            vt_ref[:head, span] = both[head:, :]
            vt_ref[head:, span] = jnp.ones((vt_ref.shape[0] - head, PART), bf16)
            keys = both[:head, :].astype(f32)
            most = jnp.max(jnp.sum(keys * keys, axis=0, keepdims=True))
            knorm_ref[0] = jnp.maximum(knorm_ref[0], most)

        for_slots(sources, table_ref, start, turn)

    base = table_ref[BASES + tile]
    steps, begin, position, parts = tile_ranges(base)
    query = qt_ref[0].astype(f32)
    qnorm = jnp.max(jnp.sum(query * query, axis=0, keepdims=True))
    narrow = qnorm * knorm_ref[0] * (factor * factor) < 60.0 * 60.0
    acc_ref[...] = jnp.zeros(acc_ref.shape, f32)
    max_ref[...] = jnp.zeros(max_ref.shape, f32)

    def writer(kind, buffer_ref, sem, span):
        count = done_ref[kind]
        slot = lax.rem(count, 2)
        copy = pltpu.make_async_copy(
            buffer_ref.at[slot], probs_ref.at[tile, span, :], sem.at[slot]
        )
        done_ref[kind] = count + 1

        @pl.when(count >= 2)
        def _():
            copy.wait()

        def write(probs):
            buffer_ref[slot] = probs
            copy.start()

        return write

    def span_of(offset, size):
        return pl.ds(pl.multiple_of(offset, size), size)

    def scores_of(span):
        return dot(kv_ref[span, :head], qt_ref[0]) * factor

    @pl.when(narrow)
    def _():
        def step(i, carry):
            span = span_of(i * FULL, FULL)
            write = writer(0, full_ref, full_sem, span)
            probs = jnp.exp2(scores_of(span)).astype(bf16)
            write(probs)
            acc_ref[...] += dot(vt_ref[:, span], probs)
            return carry

        def part(i, carry):
            span = span_of(begin + i * PART, PART)
            write = writer(1, part_ref, part_sem, span)
            mask = allowed_mask(position + i * PART, base, width)
            probs = jnp.exp2(jnp.where(mask, scores_of(span), mask_fill)).astype(bf16)
            write(probs)
            acc_ref[...] += dot(vt_ref[:, span], probs)
            return carry

        lax.fori_loop(0, steps, step, 0)
        lax.fori_loop(0, parts, part, 0)
        factor_ref[0] = 1.0 / acc_ref[head : head + 1, :]

    @pl.when(jnp.logical_not(narrow))
    def _():
        max_ref[...] = jnp.full(max_ref.shape, mask_fill, f32)
        count = steps * (FULL // PART) + parts

        def masked(i):
            before = i < steps * (FULL // PART)
            offset = i * PART
            span = span_of(offset, PART)
            shifted = jnp.where(before, -(1 << 24), position + offset - begin)
            mask = allowed_mask(shifted, base, width)
            return span, mask, jnp.where(mask, scores_of(span), mask_fill)

        def part(i, carry):
            span, mask, scores = masked(i)
            old = max_ref[...]
            new = jnp.maximum(old, jnp.max(scores, axis=0, keepdims=True))
            probs = jnp.where(mask, jnp.exp2(scores - new), 0.0).astype(bf16)
            acc_ref[...] = acc_ref[...] * jnp.exp2(old - new) + dot(vt_ref[:, span], probs)
            max_ref[...] = new
            return carry

        lax.fori_loop(0, count, part, 0)
        max_ref[...] = max_ref[...] + jnp.log2(acc_ref[head : head + 1, :])

        def again(i, carry):
            span, mask, scores = masked(i)
            write = writer(1, part_ref, part_sem, span)
            write(jnp.where(mask, jnp.exp2(scores - max_ref[...]), 0.0).astype(bf16))
            return carry

        lax.fori_loop(0, count, again, 0)
        factor_ref[0] = jnp.ones(max_ref.shape, f32)

    out_ref[0] = acc_ref[:head, :] / acc_ref[head : head + 1, :]

    @pl.when(tile == pl.num_programs(0) - 1)
    def _():
        for kind, buffer_ref, sem in ((0, full_ref, full_sem), (1, part_ref, part_sem)):
            for slot in range(2):

                @pl.when(done_ref[kind] > slot)
                def _():
                    rows = pl.ds(0, buffer_ref.shape[1])
                    pltpu.make_async_copy(
                        buffer_ref.at[slot], probs_ref.at[0, rows, :], sem.at[slot]
                    ).wait()


def attend_call(start, sources, table, qt):
    tiles, head, width = qt.shape
    total_keys = sum(x.shape[0] for x in sources)
    pair = sources[0].shape[1]
    one = lambda shape: pl.BlockSpec((1,) + shape, lambda i, t: (i, 0, 0))
    keep = lambda x: pl.BlockSpec(x.shape, lambda i, t: (0, 0))
    return pl.pallas_call(
        functools.partial(attend_kernel, start, len(sources)),
        grid_spec=pltpu.PrefetchScalarGridSpec(
            num_scalar_prefetch=1,
            grid=(tiles,),
            in_specs=[keep(x) for x in sources] + [one((head, width))],
            out_specs=[one((head, width)), one((1, width)), pl.BlockSpec(memory_space=pl.ANY)],
            scratch_shapes=[
                pltpu.VMEM((total_keys, pair), bf16),
                pltpu.VMEM((head + 16, total_keys), bf16),
                pltpu.SMEM((1,), f32),
                pltpu.VMEM((head + 16, width), f32),
                pltpu.VMEM((1, width), f32),
                pltpu.VMEM((2, FULL, width), bf16),
                pltpu.VMEM((2, PART, width), bf16),
                pltpu.SemaphoreType.DMA((2,)),
                pltpu.SemaphoreType.DMA((2,)),
                pltpu.SMEM((2,), jnp.int32),
            ],
        ),
        out_shape=[
            jax.ShapeDtypeStruct((tiles, head, width), f32),
            jax.ShapeDtypeStruct((tiles, 1, width), f32),
            jax.ShapeDtypeStruct((tiles, total_keys, width), bf16),
        ],
        compiler_params=params(),
        cost_estimate=cost(64),
        name="attend",
    )(table, *sources, qt)


def attend_back_kernel(start, buffers, table_ref, *refs):
    sources = refs[:buffers]
    q_ref, dot_ref, do_ref, delta_ref, probs_ref = refs[buffers : buffers + 5]
    refs = refs[buffers + 5 :]
    dq_ref = refs[0]
    outs = refs[1 : 1 + buffers]
    refs = refs[1 + buffers :]
    kv_ref, kt_ref, dkv_ref, rows_ref, full_ref, part_ref, full_sem, part_sem, done_ref = refs
    tile = pl.program_id(0)
    tiles = pl.num_programs(0)
    width, head = q_ref.shape[1:]
    scale = head ** (-0.5)

    @pl.when(tile == 0)
    def _():
        done_ref[0] = 0
        rows_ref[...] = jnp.zeros(rows_ref.shape, bf16)

        def turn(ref, row, span):
            rows = ref[row : row + PART, :]
            kv_ref[span, :] = rows
            kt_ref[:, span] = rows.T[:head, :]
            dkv_ref[span, :] = jnp.zeros((PART, 2 * head), f32)

        for_slots(sources, table_ref, start, turn)

    def steps_of(which):
        return tile_ranges(table_ref[BASES + jnp.clip(which, 0, tiles - 1)])[0]

    steps, begin, _, parts = tile_ranges(table_ref[BASES + tile])

    def full_copy(which, i, slot):
        rows = pl.ds(pl.multiple_of(i * FULL, FULL), FULL)
        return pltpu.make_async_copy(
            probs_ref.at[which, rows, :], full_ref.at[slot], full_sem.at[slot]
        )

    def part_copy(i):
        slot = lax.rem(i, 2)
        rows = pl.ds(pl.multiple_of(begin + i * PART, PART), PART)
        return pltpu.make_async_copy(
            probs_ref.at[tile, rows, :], part_ref.at[slot], part_sem.at[slot]
        )

    done = done_ref[0]

    @pl.when((steps > 0) & ((tile == 0) | (steps_of(tile - 1) == 0)))
    def _():
        full_copy(tile, 0, lax.rem(done, 2)).start()

    for i in range(2):

        @pl.when(i < parts)
        def _():
            part_copy(i).start()

    dq_ref[...] = jnp.zeros(dq_ref.shape, f32)
    rows_ref[:width, :head] = q_ref[0]
    rows_ref[width:, head:] = do_ref[0]

    def block(offset, size, probs):
        span = pl.ds(pl.multiple_of(offset, size), size)
        prob_grad = dot(kv_ref[span, head:], dot_ref[0])
        score_grad = (probs.astype(f32) * (prob_grad - delta_ref[0])).astype(bf16)
        dq_ref[0] += dot(kt_ref[:, span], score_grad)
        dkv_ref[span, :] += dot(jnp.concatenate([score_grad, probs], axis=1), rows_ref[...])

    def step(i, carry):
        slot = lax.rem(done + i, 2)

        @pl.when(i + 1 < steps)
        def _():
            full_copy(tile, i + 1, 1 - slot).start()

        @pl.when((i + 1 == steps) & (tile + 1 < tiles) & (steps_of(tile + 1) > 0))
        def _():
            full_copy(tile + 1, 0, 1 - slot).start()

        full_copy(tile, i, slot).wait()
        block(i * FULL, FULL, full_ref[slot])
        return carry

    def part(i, carry):
        part_copy(i).wait()
        block(begin + i * PART, PART, part_ref[lax.rem(i, 2)])

        @pl.when(i + 2 < parts)
        def _():
            part_copy(i + 2).start()

        return carry

    lax.fori_loop(0, steps, step, 0)
    lax.fori_loop(0, parts, part, 0)
    done_ref[0] = done + steps
    dq_ref[...] = dq_ref[...] * scale

    @pl.when(tile == tiles - 1)
    def _():
        lane = lax.broadcasted_iota(jnp.int32, (PART, 2 * head), 1)
        both = jnp.where(lane < head, scale, 1.0)

        def finish(ref, row, span):
            ref[row : row + PART, :] = (dkv_ref[span, :] * both).astype(ref.dtype)

        for_slots(outs, table_ref, start, finish)


def attend_back_call(start, sources, kinds, table, q, grad_t, grad, delta, probs):
    tiles, width, head = q.shape
    total_keys = sum(x.shape[0] for x in sources)
    pair = sources[0].shape[1]
    one = lambda shape: pl.BlockSpec((1,) + shape, lambda i, t: (i, 0, 0))
    keep = lambda x: pl.BlockSpec(x.shape, lambda i, t: (0, 0))
    return pl.pallas_call(
        functools.partial(attend_back_kernel, start, len(sources)),
        grid_spec=pltpu.PrefetchScalarGridSpec(
            num_scalar_prefetch=1,
            grid=(tiles,),
            in_specs=[keep(x) for x in sources]
            + [
                one((width, head)),
                one((head, width)),
                one((width, head)),
                one((1, width)),
                pl.BlockSpec(memory_space=pl.ANY),
            ],
            out_specs=[one((head, width))] + [keep(x) for x in sources],
            scratch_shapes=[
                pltpu.VMEM((total_keys, pair), bf16),
                pltpu.VMEM((head, total_keys), bf16),
                pltpu.VMEM((total_keys, pair), f32),
                pltpu.VMEM((2 * width, pair), bf16),
                pltpu.VMEM((2, FULL, width), bf16),
                pltpu.VMEM((2, PART, width), bf16),
                pltpu.SemaphoreType.DMA((2,)),
                pltpu.SemaphoreType.DMA((2,)),
                pltpu.SMEM((1,), jnp.int32),
            ],
        ),
        out_shape=[jax.ShapeDtypeStruct((tiles, head, width), f32)]
        + [jax.ShapeDtypeStruct(x.shape, kind) for x, kind in zip(sources, kinds)],
        compiler_params=params(),
        cost_estimate=cost(130),
        name="attend_back",
    )(table, *sources, q, grad_t, grad, delta, probs)


def place(index, pieces, expert):
    total = jnp.zeros(pieces[0].shape, f32)
    for j, piece in enumerate(pieces):
        total = jnp.where(index[j : j + 1, :] == expert, piece, total)
    return total


def middle_kernel(pieces, table_ref, *refs):
    sources = refs[:pieces]
    refs = refs[pieces:]
    outs = 4 if pieces > 1 else 1
    layer_out_refs = refs[MIDDLE_INPUTS : MIDDLE_INPUTS + outs]
    refs = refs[:MIDDLE_INPUTS] + refs[MIDDLE_INPUTS + outs :]
    middle_body(table_ref, sources, layer_out_refs, *refs)


MIDDLE_INPUTS = 14


def middle_body(
    table_ref,
    sources,
    layer_out_refs,
    tokens_ref,
    index_ref,
    gate_ref,
    attended_ref,
    factor_ref,
    output_own_ref,
    down_own_ref,
    both_other_ref,
    up_own_ref,
    up_other_ref,
    gain_ref,
    shift_ref,
    up_bias_ref,
    down_bias_ref,
    middle_grad_ref,
    grad_t_ref,
    grad_rows_ref,
    delta_ref,
    logit_grad_ref,
    output_weight_grad_ref,
    up_weight_grad_ref,
    down_weight_grad_ref,
    gain_grad_ref,
    shift_grad_ref,
    up_bias_grad_ref,
    down_bias_grad_ref,
    grad_ref,
    output_weight_ref,
    up_weight_ref,
    down_weight_ref,
    spread_ref,
    chosen_ref,
    dwo_ref,
    dup_ref,
    ddown_ref,
):
    step = pl.program_id(0)
    topk = index_ref.shape[0]
    head = attended_ref.shape[1]
    experts = output_weight_ref.shape[0] // head
    per = TILE // ROWS

    @pl.when(step == 0)
    def _():
        shard = table_ref[SHARD]
        join_rows(shard, output_own_ref, both_other_ref, output_weight_ref)
        join_rows(shard, down_own_ref, both_other_ref, down_weight_ref, output_own_ref.shape[0])
        join_rows(shard, up_own_ref, up_other_ref, up_weight_ref)
        for ref in (
            dwo_ref,
            dup_ref,
            ddown_ref,
            gain_grad_ref,
            shift_grad_ref,
            up_bias_grad_ref,
            down_bias_grad_ref,
        ):
            ref[...] = jnp.zeros(ref.shape, ref.dtype)

    pick_piece(step, table_ref, sources, grad_ref)
    index = index_ref[...]
    gate = gate_ref[...]
    for part in range(per):
        lanes = slice(part * ROWS, (part + 1) * ROWS)
        pieces = [
            attended_ref[part, :, j * ROWS : (j + 1) * ROWS] * gate[j : j + 1, lanes]
            for j in range(topk)
        ]
        for expert in range(experts):
            spread_ref[expert * head : (expert + 1) * head, lanes] = place(
                index[:, lanes], pieces, expert
            ).astype(bf16)

    middle = tokens_ref[...].astype(f32).T + dot_tn(output_weight_ref[...], spread_ref[...])
    unit, inverse = column_norm(middle)
    second = (unit * gain_ref[...] + shift_ref[...]).astype(bf16)
    pre = dot_tn(up_weight_ref[...], second) + up_bias_ref[...]
    coeff = math.sqrt(2.0 / math.pi)
    square = pre * pre
    wave = jnp.tanh(coeff * pre * (1.0 + 0.044715 * square))
    half = 0.5 * (1.0 + wave)
    hidden = (pre * half).astype(bf16)
    slope = half + 0.5 * pre * (1.0 - wave * wave) * (coeff * (1.0 + 3 * 0.044715 * square))
    result = middle + dot_tn(down_weight_ref[...], hidden) + down_bias_ref[...]
    store_piece(step, layer_out_refs, result.T.astype(bf16))

    grad_rows = grad_ref[...]
    grad_wide = grad_rows.astype(f32)
    grad_t = grad_wide.T
    ddown_ref[...] += dot(hidden, grad_rows)
    down_bias_grad_ref[...] += jnp.sum(grad_wide, axis=0, keepdims=True)
    pre_grad = (dot(down_weight_ref[...], grad_t.astype(bf16)) * slope).astype(bf16)
    dup_ref[...] += dot_nt(second, pre_grad)
    up_bias_grad_ref[...] += fold_lanes(pre_grad.astype(f32))
    second_grad = dot(up_weight_ref[...], pre_grad)
    gain_grad_ref[...] += fold_lanes(second_grad * unit)
    shift_grad_ref[...] += fold_lanes(second_grad)
    middle_grad = grad_t + column_norm_back(second_grad, unit, inverse, gain_ref[...])
    middle_grad_ref[...] = middle_grad
    middle_low = middle_grad.astype(bf16)
    dwo_ref[...] += dot_nt(spread_ref[...], middle_low)
    chosen_ref[...] = dot(output_weight_ref[...], middle_low)

    for part in range(per):
        lanes = slice(part * ROWS, (part + 1) * ROWS)
        picks = []
        for j in range(topk):
            span = slice(j * ROWS, (j + 1) * ROWS)
            row = index[j : j + 1, lanes]
            chosen = jnp.zeros((head, ROWS), f32)
            for expert in range(experts):
                chosen = jnp.where(
                    row == expert, chosen_ref[expert * head : (expert + 1) * head, lanes], chosen
                )
            attended = attended_ref[part, :, span]
            picks.append(jnp.sum(chosen * attended, axis=0, keepdims=True))
            back = (chosen * gate[j : j + 1, lanes]).astype(bf16).astype(f32)
            back = (back * factor_ref[part, :, span]).astype(bf16)
            grad_t_ref[part, :, span] = back
            back = back.astype(f32)
            grad_rows_ref[part, span, :] = back.T.astype(bf16)
            delta_ref[part, :, span] = jnp.sum(back * attended, axis=0, keepdims=True)
        gates = [gate[j : j + 1, lanes] for j in range(topk)]
        mean = sum(g * p for g, p in zip(gates, picks))
        rows = [g * (p - mean) for g, p in zip(gates, picks)]
        spare = logit_grad_ref.shape[0] - experts
        logit = [place(index[:, lanes], rows, expert) for expert in range(experts)]
        logit.append(jnp.zeros((spare, ROWS), f32))
        logit_grad_ref[:, lanes] = jnp.concatenate(logit, axis=0).astype(bf16)

    @pl.when(step == pl.num_programs(0) - 1)
    def _():
        output_weight_grad_ref[...] = dwo_ref[...].astype(bf16)
        up_weight_grad_ref[...] = dup_ref[...].astype(bf16)
        down_weight_grad_ref[...] = ddown_ref[...].astype(bf16)


def middle_call(
    table, sources, tokens, index, gate, attended, factor, weights,
    gain, shift, up_bias, down_bias, padded,
):
    count, width = tokens.shape
    topk = index.shape[0]
    tiles, head, wide = attended.shape
    per = TILE // ROWS
    spread = 2 * weights[0].shape[0]
    hidden = 2 * weights[1].shape[0]
    keep = lambda shape: pl.BlockSpec(shape, lambda i, s: tuple(0 for _ in shape))
    rows = pl.BlockSpec((TILE, width), lambda i, s: (i, 0))
    columns = lambda n: pl.BlockSpec((n, TILE), lambda i, s: (0, i))
    tile = lambda shape: pl.BlockSpec((per,) + shape, lambda i, s: (i, 0, 0))
    shape = jax.ShapeDtypeStruct
    if len(sources) > 1:
        outs = [(keep((TILE, width)), shape((TILE, width), bf16))] * 4
    else:
        outs = [(rows, shape((count, width), bf16))]
    outs += [
        (columns(width), shape((width, count), f32)),
        (tile((head, wide)), shape((tiles, head, wide), bf16)),
        (tile((wide, head)), shape((tiles, wide, head), bf16)),
        (tile((1, wide)), shape((tiles, 1, wide), f32)),
        (columns(padded), shape((padded, count), bf16)),
        (keep((spread, width)), shape((spread, width), bf16)),
        (keep((width, hidden)), shape((width, hidden), bf16)),
        (keep((hidden, width)), shape((hidden, width), bf16)),
        (keep((width, 128)), shape((width, 128), f32)),
        (keep((width, 128)), shape((width, 128), f32)),
        (keep((hidden, 128)), shape((hidden, 128), f32)),
        (keep((1, width)), shape((1, width), f32)),
    ]
    return pl.pallas_call(
        functools.partial(middle_kernel, len(sources)),
        grid_spec=pltpu.PrefetchScalarGridSpec(
            num_scalar_prefetch=1,
            grid=(count // TILE,),
            in_specs=piece_specs(sources)
            + [rows, columns(topk), columns(topk), tile((head, wide)), tile((1, wide))]
            + [keep(w.shape) for w in weights]
            + [keep((width, 1)), keep((width, 1)), keep((hidden, 1)), keep((width, 1))],
            out_specs=[x for x, _ in outs],
            scratch_shapes=[
                pltpu.VMEM((TILE, width), bf16),
                pltpu.VMEM((spread, width), bf16),
                pltpu.VMEM((width, hidden), bf16),
                pltpu.VMEM((hidden, width), bf16),
                pltpu.VMEM((spread, TILE), bf16),
                pltpu.VMEM((spread, TILE), f32),
                pltpu.VMEM((spread, width), f32),
                pltpu.VMEM((width, hidden), f32),
                pltpu.VMEM((hidden, width), f32),
            ],
        ),
        out_shape=[x for _, x in outs],
        compiler_params=params(),
        cost_estimate=cost(44),
        name="middle",
    )(table, *sources, tokens, index, gate, attended, factor, *weights,
      gain, shift, up_bias, down_bias)


def query_back_kernel(
    table_ref,
    first_ref,
    index_ref,
    dq_ref,
    own_ref,
    other_ref,
    logit_grad_ref,
    router_ref,
    partial_ref,
    keep_ref,
    send_ref,
    router_grad_ref,
    query_weight_ref,
    placed_ref,
    dwq_ref,
    dr_ref,
):
    step = pl.program_id(0)
    topk = index_ref.shape[0]
    head = dq_ref.shape[1]
    experts = query_weight_ref.shape[1] // head

    @pl.when(step == 0)
    def _():
        join_rows(table_ref[SHARD], own_ref, other_ref, query_weight_ref)
        dwq_ref[...] = jnp.zeros(dwq_ref.shape, f32)
        dr_ref[...] = jnp.zeros(dr_ref.shape, f32)

    index = index_ref[...]
    for part in range(TILE // ROWS):
        lanes = slice(part * ROWS, (part + 1) * ROWS)
        pieces = [dq_ref[part, :, j * ROWS : (j + 1) * ROWS] for j in range(topk)]
        for expert in range(experts):
            placed_ref[expert * head : (expert + 1) * head, lanes] = place(
                index[:, lanes], pieces, expert
            ).astype(bf16)
    first = first_ref[...]
    dwq_ref[...] += dot_nt(first, placed_ref[...])
    dr_ref[...] += dot_nt(first, logit_grad_ref[...])
    partial_ref[...] = dot(query_weight_ref[...], placed_ref[...]) + dot(
        router_ref[...], logit_grad_ref[...]
    )

    @pl.when(step == pl.num_programs(0) - 1)
    def _():
        router_grad_ref[...] = dr_ref[...]
        size = keep_ref.shape[2]
        shard, core, side = table_ref[SHARD], table_ref[CORE], table_ref[SIDE]
        for target, last in ((keep_ref, core), (send_ref, 1 - core)):
            for i, half in enumerate((shard, 1 - shard)):
                for j, part in enumerate((side, 1 - side)):
                    at = ((half * 2 + last) * 2 + part) * size
                    rows = pl.ds(pl.multiple_of(at, size), size)
                    target[i, j] = dwq_ref[rows, :].astype(bf16)


def query_back_call(table, first, index, dq, own, other, logit_grad, router):
    width, count = first.shape
    topk = index.shape[0]
    tiles, head, wide = dq.shape
    padded = router.shape[1]
    spread = own.shape[1]
    keep = lambda shape: pl.BlockSpec(shape, lambda i, s: tuple(0 for _ in shape))
    columns = lambda n: pl.BlockSpec((n, TILE), lambda i, s: (0, i))
    shape = jax.ShapeDtypeStruct
    quarters = (2, 2, width // 8, spread)
    return pl.pallas_call(
        query_back_kernel,
        grid_spec=pltpu.PrefetchScalarGridSpec(
            num_scalar_prefetch=1,
            grid=(count // TILE,),
            in_specs=[
                columns(width),
                columns(topk),
                pl.BlockSpec((TILE // ROWS, head, wide), lambda i, s: (i, 0, 0)),
                keep(own.shape),
                keep(other.shape),
                columns(padded),
                keep(router.shape),
            ],
            out_specs=[columns(width), keep(quarters), keep(quarters), keep(router.shape)],
            scratch_shapes=[
                pltpu.VMEM((width, spread), bf16),
                pltpu.VMEM((spread, TILE), bf16),
                pltpu.VMEM((width, spread), f32),
                pltpu.VMEM(router.shape, f32),
            ],
        ),
        out_shape=[
            shape((width, count), f32),
            shape(quarters, bf16),
            shape(quarters, bf16),
            shape(router.shape, f32),
        ],
        compiler_params=params(),
        cost_estimate=cost(0),
        name="query_back",
    )(table, first, index, dq, own, other, logit_grad, router)


def first_back_kernel(pieces, table_ref, *refs):
    tokens_ref, first_ref, partial_ref, middle_grad_ref = refs[:4]
    sources = refs[4 : 4 + pieces]
    kv_weight_ref, gain_ref, rest_ref = refs[4 + pieces : 7 + pieces]
    refs = refs[7 + pieces :]
    outs = 4 if pieces > 1 else 1
    tokens_grad_refs = refs[:outs]
    keep_ref, send_ref, total_ref, gain_grad_ref, shift_grad_ref, dkv_ref = refs[outs:]
    step = pl.program_id(0)
    pair = kv_weight_ref.shape[1]

    @pl.when(step == 0)
    def _():
        total_ref[:, :pair] = jnp.zeros((total_ref.shape[0], pair), f32)
        for ref in (gain_grad_ref, shift_grad_ref):
            ref[...] = jnp.zeros(ref.shape, ref.dtype)

    unit, inverse = column_norm(tokens_ref[...].astype(f32).T)
    if pieces == 1:
        dkv_ref[...] = sources[0][...]
    else:
        low_ref, high_ref, own_ref = sources
        own = table_ref[OWN_SLOT]
        for chosen, ref, half in (
            (table_ref[LOW_SLOT], low_ref, 0),
            (table_ref[HIGH_SLOT], high_ref, 0),
            (own, own_ref, 0),
            (own + 1, own_ref, 1),
        ):

            @pl.when(step == chosen)
            def _():
                dkv_ref[...] = ref[half * PART : (half + 1) * PART, :]

    dkv = dkv_ref[...]
    total_ref[:, :pair] += dot(first_ref[...], dkv)
    first_grad = partial_ref[...] + dot_nt(kv_weight_ref[...], dkv)
    gain_grad_ref[...] += fold_lanes(first_grad * unit)
    shift_grad_ref[...] += fold_lanes(first_grad)
    total = middle_grad_ref[...] + column_norm_back(first_grad, unit, inverse, gain_ref[...])
    store_piece(step, tokens_grad_refs, total.T.astype(bf16))

    @pl.when(step == pl.num_programs(0) - 1)
    def _():
        lane = lax.broadcasted_iota(jnp.int32, rest_ref.shape, 1)
        gains = jnp.sum(gain_grad_ref[...], axis=1, keepdims=True)
        shifts = jnp.sum(shift_grad_ref[...], axis=1, keepdims=True)
        rest = jnp.where(lane == 0, gains, jnp.where(lane == 1, shifts, rest_ref[...]))
        total_ref[:, pair:] = rest
        size = keep_ref.shape[1]
        shard, core = table_ref[SHARD], table_ref[CORE]
        for target, last in ((keep_ref, core), (send_ref, 1 - core)):
            for i, half in enumerate((shard, 1 - shard)):
                rows = pl.ds(pl.multiple_of((half * 2 + last) * size, size), size)
                target[i] = total_ref[rows, :].astype(bf16)


def first_back_call(table, tokens, first, partial, middle_grad, dkv, kv_weight, gain, rest):
    count, width = tokens.shape
    pair = kv_weight.shape[1]
    wide = pair + rest.shape[1]
    columns = lambda n: pl.BlockSpec((n, TILE), lambda i, t: (0, i))
    rows = lambda n: pl.BlockSpec((TILE, n), lambda i, t: (i, 0))
    keep = lambda shape: pl.BlockSpec(shape, lambda i, t: tuple(0 for _ in shape))
    shape = jax.ShapeDtypeStruct
    quarters = (2, width // 4, wide)
    if len(dkv) > 1:
        outs = [(keep((TILE, width)), shape((TILE, width), bf16))] * 4
    else:
        outs = [(rows(width), shape((count, width), bf16))]
    outs += [(keep(quarters), shape(quarters, bf16))] * 2
    return pl.pallas_call(
        functools.partial(first_back_kernel, len(dkv)),
        grid_spec=pltpu.PrefetchScalarGridSpec(
            num_scalar_prefetch=1,
            grid=(count // TILE,),
            in_specs=[rows(width), columns(width), columns(width), columns(width)]
            + piece_specs(dkv)
            + [keep(kv_weight.shape), keep((width, 1)), keep(rest.shape)],
            out_specs=[x for x, _ in outs],
            scratch_shapes=[
                pltpu.VMEM((width, wide), f32),
                pltpu.VMEM((width, 128), f32),
                pltpu.VMEM((width, 128), f32),
                pltpu.VMEM((TILE, pair), bf16),
            ],
        ),
        out_shape=[x for _, x in outs],
        compiler_params=params(),
        cost_estimate=cost(7),
        name="first_back",
    )(table, tokens, first, partial, middle_grad, *dkv, kv_weight, gain, rest)


def after(value, *others):
    return lax.optimization_barrier((value,) + others)[0]


def other_half(value):
    return lax.ppermute(value, "shard", [(0, 1), (1, 0)])


def join(value, other):
    low = lax.axis_index("shard") == 0
    return jnp.concatenate([jnp.where(low, value, other), jnp.where(low, other, value)], axis=0)


def swap(value, mask):
    count = lax.axis_size("ctx")
    return lax.ppermute(value, "ctx", [(i, i ^ mask) for i in range(count)])


def bit_masks(count):
    return [1 << k for k in reversed(range(count.bit_length() - 1))]


def key_orders(count):
    masks = bit_masks(count)
    return masks, masks[:1] + masks[1:-1][::-1] + masks[-1:]


def slots_of(masks):
    return [sum(m for k, m in enumerate(masks) if j >> k & 1) for j in range(1 << len(masks))]


def gather_keys(shared):
    low_order, high_order = key_orders(lax.axis_size("ctx"))
    got = swap(shared, low_order[0])
    low = jnp.concatenate([shared[:PART], got[:PART]], axis=0)
    high = jnp.concatenate([shared[PART:], got[PART:]], axis=0)
    for low_mask, high_mask in zip(low_order[1:-1], high_order[1:-1]):
        low_got, high_got = swap(low, low_mask), swap(high, high_mask)
        low = jnp.concatenate([low, low_got], axis=0)
        high = jnp.concatenate([high, high_got], axis=0)
    return (low, swap(low, low_order[-1])), (high, swap(high, high_order[-1]))


def add_low(a, b):
    return (a.astype(f32) + b.astype(f32)).astype(bf16)


def step_down(total, mask):
    half = total.shape[0] // 2
    return total[:half], swap(total[half:].astype(bf16), mask)


def double(total, mask):
    other = swap(total, mask)
    low = (lax.axis_index("ctx") // mask) % 2 == 0
    return jnp.concatenate([jnp.where(low, total, other), jnp.where(low, other, total)], axis=0)


def home_plan(count, block):
    half = count // 2
    if block != 4 * PART or block * half != PROMPT or block != CLEN or half % 2:
        return None
    sends = [None] * count
    hops = [[], [], []]
    for a in range(half // 2):
        b = half - 1 - a
        p, q = a + half, b + half
        sends[a], sends[b] = (0, 1, 2, 3), (2, 3, 0, 1)
        sends[p] = sends[q] = (0, 3, 1, 2)
        hops[0] += [(a, b), (b, a)]
        hops[1] += [(a, p), (p, a), (b, q), (q, b)]
        hops[2] += [(a, q), (b, p), (p, a), (q, b)]
    places = [[(i, sends[i][0]), (i, sends[i][1]), None, None] for i in range(count)]
    for k, hop in enumerate(hops):
        for source, target in hop:
            places[target][k + 1] = (source, sends[source][k + 1])
    return sends, hops, places


def plan_rows(plan, count):
    sends, _, places = plan
    lower, prompt = HALF // PART, PROMPT // PART
    where = [[source * 4 + quarter for source, quarter in row] for row in places]
    low_slot = [next(k for k in range(4) if row[k] < lower) for row in where]
    high_slot = [next(k for k in range(4) if lower <= row[k] < prompt) for row in where]
    own_slot = [2 if i < count // 2 else 0 for i in range(count)]
    own_at = [[row[k] % 4, row[k + 1] % 4] for row, k in zip(where, own_slot)]
    low_slots, high_slots = (slots_of(masks) for masks in key_orders(count))
    rows = []
    for i in range(count):
        row = list(sends[i]) + [int(i < count // 2), low_slot[i], high_slot[i], own_slot[i]]
        row += [0, i % 2, i // 2 % 2]
        row += [x * PART + r for x in where[i] for r in range(0, PART, ROWS)]
        row += [where[i ^ m][low_slot[i ^ m]] for m in low_slots]
        row += [where[i ^ m][high_slot[i ^ m]] for m in high_slots]
        row += [prompt + x for x in own_at[i] + own_at[i ^ (count // 2)]]
        rows.append(row)
    return rows


def send_pieces(pieces, plan):
    got = [lax.ppermute(piece, "ctx", hop) for piece, hop in zip(pieces[1:], plan[1])]
    return pieces[0], pieces[1], *got


def send_back(pieces, plan):
    hops = [[(t, s) for s, t in hop] for hop in plan[1]]
    got = [lax.ppermute(piece, "ctx", hop) for piece, hop in zip(pieces[1:], hops)]
    return pieces[0], pieces[1], *got


def per_device(
    tokens,
    expert_index,
    first_gain,
    first_shift,
    router_weight,
    query_weight,
    key_weight,
    value_weight,
    output_weight,
    second_gain,
    second_shift,
    up_weight,
    up_bias,
    down_weight,
    down_bias,
    out_grad,
):
    groups, block, width = tokens.shape
    assert groups == 1 and lax.axis_size("shard") == 2
    count = lax.axis_size("ctx")
    me = lax.axis_index("ctx")
    shard = lax.axis_index("shard")
    experts = router_weight.shape[1]
    topk = expert_index.shape[-1]
    head = key_weight.shape[1]
    pair = 2 * head
    padded = 32
    tiles = block // ROWS
    key_table = BASES + tiles
    plan = home_plan(count, block)
    if plan:
        table = jnp.array(plan_rows(plan, count), jnp.int32)[me]
        table = table + shard * (jnp.arange(table.shape[0], dtype=jnp.int32) == SHARD)
        packed = pack_call(table, tokens[0], expert_index[0].T)
        sources = send_pieces(packed, plan)
        key_weight, packed = lax.optimization_barrier((key_weight, packed))
    else:
        base = me * block
        numbers = [0, 0, 0, 0, 0, 0, 0, 0, shard, me % 2, me // 2 % 2]
        table = jnp.concatenate(
            [
                jnp.stack([jnp.int32(x) for x in numbers]),
                base + jnp.arange(tiles, dtype=jnp.int32) * ROWS,
                jnp.arange((PROMPT + CLEN) // PART, dtype=jnp.int32),
            ]
        )
        sources = (tokens[0],)

    spare = jnp.zeros((key_weight.shape[0], padded - experts), bf16)
    vectors = [first_gain, first_shift, second_gain, second_shift, down_bias]
    half_width = width // 2
    small = jnp.concatenate(
        [key_weight, value_weight, router_weight, spare]
        + [v[:, None] for v in vectors]
        + [up_bias.reshape(half_width, -1)],
        axis=1,
    )
    small = join(small, other_half(small))
    query_other = other_half(after(query_weight, small))
    kv_weight = small[:, :pair]
    router = small[:, pair : pair + padded]
    at = pair + padded
    columns = [small[:, at + i : at + i + 1].astype(f32) for i in range(len(vectors))]
    gain_one, shift_one, gain_two, shift_two, down_bias_all = columns
    up_bias_all = small[:, at + len(vectors) :].reshape(-1, 1).astype(f32)

    both_weights = jnp.concatenate([output_weight, down_weight], axis=0)
    early_work = (both_weights, router, up_bias_all, *columns)
    if plan:
        grads = pack_call(after(table, small), out_grad[0])
        early_work += tuple(grads)
    table, early_work = lax.optimization_barrier((table, early_work))
    both_weights, router, up_bias_all, *rest = early_work
    gain_one, shift_one, gain_two, shift_two, down_bias_all = rest[: len(vectors)]
    grads = rest[len(vectors) :]
    first_out = first_call(table, sources, block, topk, gain_one, shift_one, kv_weight)
    if plan:
        first, shared, own, index, flat = first_out
        low_keys, high_keys = gather_keys(shared)
        partner = swap(own, count // 2)
        high_keys += (own, partner)
    else:
        first, kv = first_out
        flat = tokens[0]
        index = expert_index[0].T
        gathered = lax.all_gather(kv, "ctx", axis=0, tiled=True)
        segment = jnp.maximum(base, PROMPT) // CLEN * CLEN
        own = lax.dynamic_slice_in_dim(gathered, segment, CLEN, 0)
        quarter = HALF // 2
        low_keys = (gathered[:quarter], gathered[quarter:HALF])
        high_keys = (
            gathered[HALF : HALF + quarter], gathered[HALF + quarter : PROMPT],
            own[: CLEN // 2], own[CLEN // 2 :],
        )

    qt, q, gate = query_call(table, first, query_weight, query_other, router, index, head)
    both_other = other_half(after(both_weights, query_other))
    weights = (
        output_weight, down_weight, both_other, up_weight, other_half(after(up_weight, query_other))
    )
    if plan:
        grads = send_pieces(after(tuple(grads), *low_keys, *high_keys), plan)
    else:
        grads = (out_grad[0],)
    keys = low_keys + high_keys
    attended, factor, probs = attend_call(key_table, keys, table, qt)
    outs = 4 if plan else 1
    middle = middle_call(
        table, grads, flat, index, gate, attended, factor, weights,
        gain_two, shift_two, up_bias_all, down_bias_all, padded,
    )
    layer_out = middle[:outs]
    (
        middle_grad, grad_t, grad_rows, delta, logit_grad,
        output_weight_grad, up_weight_grad, down_weight_grad,
        second_gain_grad, second_shift_grad, up_bias_grad, down_bias_grad,
    ) = middle[outs:]

    early = lax.psum((output_weight_grad, up_weight_grad, down_weight_grad), ("ctx", "shard"))
    if plan:
        layer_out = send_back(layer_out, plan)
    kinds = (f32, bf16, f32, bf16, f32, bf16) if plan else (bf16,) * 6
    dq, *key_grads = attend_back_call(
        key_table, keys, kinds, table, q, grad_t, grad_rows, delta, probs
    )
    dq, key_grads, layer_out = lax.optimization_barrier((dq, key_grads, layer_out))
    if plan:
        low_near, low_far, high_near, high_far, own_near, own_far = key_grads
        low_got, high_got = swap(low_far, 1), swap(high_far, 1)
    partial, keep, send, router_grad = query_back_call(
        table, first, index, dq, query_weight, query_other, logit_grad, router
    )
    sums = (second_gain_grad, second_shift_grad, down_bias_grad, up_bias_grad)
    router_grad, layer_out, *sums = lax.optimization_barrier((router_grad, layer_out, *sums))
    second_gain_grad, second_shift_grad, down_bias_grad, up_bias_grad = sums
    layer_out = unpack_call(table, layer_out) if plan else layer_out[0]
    rest = jnp.concatenate(
        [
            jnp.zeros((width, 2), f32),
            jnp.sum(second_gain_grad, axis=1)[:, None],
            jnp.sum(second_shift_grad, axis=1)[:, None],
            down_bias_grad[0][:, None],
            jnp.sum(up_bias_grad, axis=1).reshape(width, -1),
        ],
        axis=1,
    )
    bias_columns = rest.shape[1] - 5
    rest = jnp.pad(rest, ((0, 0), (0, padded - rest.shape[1])))
    rest = jnp.concatenate([rest, router_grad, jnp.zeros((width, 128 - 2 * padded), f32)], axis=1)
    total = add_low(keep, swap(send, 1))
    if plan:
        low_order, high_order = key_orders(count)
        low_keep, low_got = step_down(low_near + low_got.astype(f32), low_order[2])
        high_keep, high_got = step_down(high_near + high_got.astype(f32), high_order[2])
        total, rest, layer_out, *early = lax.optimization_barrier(
            (total, rest, layer_out, *early)
        )
        query_got = other_half(total[1])
    if plan:
        low_got, high_got, total, own_far = lax.optimization_barrier(
            (low_got, high_got, total, own_far)
        )
        own_got = swap(own_far, count // 2)
        low_keep, low_got = step_down(low_keep + low_got.astype(f32), low_order[1])
        high_keep, high_got = step_down(high_keep + high_got.astype(f32), high_order[1])
        low_got, high_got = lax.optimization_barrier((low_got, high_got))
        low_sum = low_keep + low_got.astype(f32)
        high_sum = high_keep + high_got.astype(f32)
        both = jnp.concatenate([low_sum[PART:], high_sum[PART:]], axis=0).astype(bf16)
        both = swap(both, low_order[0])
        total = add_low(total[0], query_got)
        query_got = swap(total[1], 2)
        both, total = lax.optimization_barrier((both, total))
        dkv = (
            add_low(low_sum[:PART], both[:PART]),
            add_low(high_sum[:PART], both[PART:]),
            add_low(own_near, own_got),
        )
    else:
        rows = count * block - PROMPT
        dall = jnp.concatenate(key_grads[:4] + [jnp.zeros((rows, pair), bf16)])
        own_grad = jnp.concatenate(key_grads[4:])
        own_grad = jnp.where(base >= PROMPT, own_grad, jnp.zeros_like(own_grad))
        dall = lax.dynamic_update_slice_in_dim(dall, own_grad, segment, 0)
        dkv = (lax.psum_scatter(dall, "ctx", scatter_dimension=0, tiled=True),)
        total = add_low(total[0], other_half(total[1]))
        query_got = swap(total[1], 2)
    done = first_back_call(
        table, flat, first, partial, middle_grad, dkv, kv_weight, gain_one, rest
    )
    tokens_grad = done[:outs]
    keep, send, *early = lax.optimization_barrier((*done[outs:], *early))
    small_sum = add_low(keep, swap(send, 1))
    small_sum = add_low(small_sum[0], other_half(small_sum[1]))
    small_sum = add_low(small_sum, swap(small_sum, 2))
    total = add_low(total[0], query_got)
    for mask in bit_masks(count)[:-2][::-1]:
        got, small_got = swap(total, mask), swap(small_sum, mask)
        total, small_sum = add_low(total, got), add_low(small_sum, small_got)
    if plan:
        tokens_grad = send_back(tokens_grad, plan)
    query_weight_grad = double(double(total, 2), 1).astype(f32)
    small_grad = double(small_sum, 1).astype(f32)
    tokens_grad = unpack_call(table, tokens_grad) if plan else tokens_grad[0]
    output_weight_grad, up_weight_grad, down_weight_grad = (
        lax.dynamic_slice_in_dim(x, shard * (x.shape[0] // 2), x.shape[0] // 2, 0).astype(f32)
        for x in early
    )
    return (
        layer_out[None],
        tokens_grad[None],
        small_grad[:, pair],
        small_grad[:, pair + 1],
        small_grad[:, pair + padded : pair + padded + experts],
        query_weight_grad,
        small_grad[:, :head],
        small_grad[:, head:pair],
        output_weight_grad,
        small_grad[:, pair + 2],
        small_grad[:, pair + 3],
        up_weight_grad,
        small_grad[:, pair + 5 : pair + 5 + bias_columns].reshape(-1),
        down_weight_grad,
        small_grad[:, pair + 4],
    )


def solution(mesh):
    split = P("shard", "ctx", None)
    vector = P("shard")
    matrix = P("shard", None)
    in_specs = (
        split, split, vector, vector, matrix, matrix, matrix, matrix, matrix,
        vector, vector, matrix, vector, matrix, vector, split,
    )
    out_specs = (
        split, split, vector, vector, matrix, matrix, matrix, matrix, matrix,
        vector, vector, matrix, vector, matrix, vector,
    )
    return jax.shard_map(
        per_device, mesh=mesh, in_specs=in_specs, out_specs=out_specs, check_vma=False
    )
```

```python
import functools
import math

import jax
import jax.numpy as jnp
from jax import lax
from jax.experimental import pallas as pl
from jax.experimental.pallas import tpu as pltpu
from jax.sharding import PartitionSpec as P

PROMPT = 8192
CLEN = 1024
ROWS = 128
TILE = 256
FULL = 1024
PART = 256
HALF = PROMPT // 2
VMEM = 60 << 20

PIECES, IS_PROMPT, LOW_SLOT, HIGH_SLOT, OWN_SLOT, SHARD, CORE, SIDE, BASES = 0, 4, 5, 6, 7, 8, 9, 10, 11
norm_eps = 1e-05
mask_fill = -1e30
LOG2E = math.log2(math.e)
bf16 = jnp.bfloat16
f32 = jnp.float32


def dot(a, b):
    return lax.dot_general(a, b, (((1,), (0,)), ((), ())), preferred_element_type=f32)


def dot_tn(a, b):
    return lax.dot_general(a, b, (((0,), (0,)), ((), ())), preferred_element_type=f32)


def dot_nt(a, b):
    return lax.dot_general(a, b, (((1,), (1,)), ((), ())), preferred_element_type=f32)


def params(**kw):
    return pltpu.CompilerParams(vmem_limit_bytes=VMEM, **kw)


def cost(us):
    return pl.CostEstimate(flops=int(us * 1.15e9), transcendentals=0, bytes_accessed=0)


def whole(shape):
    return pl.BlockSpec(shape, lambda i: tuple(0 for _ in shape))


def column_norm(values):
    center = jnp.mean(values, axis=0, keepdims=True)
    centred = values - center
    spread = jnp.mean(centred * centred, axis=0, keepdims=True)
    inverse = lax.rsqrt(spread + norm_eps)
    return centred * inverse, inverse


def column_norm_back(grad, unit, inverse, gain):
    scaled = grad * gain
    inner = (
        scaled
        - jnp.mean(scaled, axis=0, keepdims=True)
        - unit * jnp.mean(scaled * unit, axis=0, keepdims=True)
    )
    return inner * inverse


def fold_lanes(values):
    width = values.shape[1]
    total = values[:, :128]
    for start in range(128, width, 128):
        total = total + values[:, start : start + 128]
    return total


def pick_piece(step, table_ref, sources, target_ref):
    if len(sources) == 1:
        target_ref[...] = sources[0][...]
        return
    keep, own, *got = sources
    rows = target_ref.shape[0]
    prompt = table_ref[IS_PROMPT] == 1
    which = ((step == 0), (step == 1) & jnp.logical_not(prompt), (step == 1) & prompt)
    for chosen, ref in zip(which + ((step == 2), (step == 3)), (keep, own, *got)):

        @pl.when(chosen)
        def _():
            target_ref[...] = ref[:rows, :]


def store_piece(step, targets, value):
    if len(targets) == 1:
        targets[0][...] = value
        return
    for k, ref in enumerate(targets):

        @pl.when(step == k)
        def _():
            ref[...] = value


def piece_specs(pieces):
    if len(pieces) == 1:
        return [pl.BlockSpec((TILE, pieces[0].shape[1]), lambda i, t: (i, 0))]
    return [pl.BlockSpec(x.shape, lambda i, t: (0, 0)) for x in pieces]


def pack_kernel(table_ref, *refs):
    rows_ref, *refs = refs
    index = refs.pop(0) if len(refs) > 4 else None
    for k, ref in enumerate(refs):
        span = pl.ds(pl.multiple_of(table_ref[PIECES + k] * PART, PART), PART)
        ref[:PART, :] = rows_ref[span, :]
        if index is not None:
            chosen = index[:, span].astype(f32)
            blank = jnp.zeros((16 - index.shape[0], PART), f32)
            ref[PART:, :] = jnp.concatenate(
                [jnp.concatenate([chosen, blank], axis=0)] * (ref.shape[1] // PART), axis=1
            ).astype(bf16)


def pack_call(table, rows, index=None):
    count, width = rows.shape
    out = (count // 4 + (0 if index is None else 16), width)
    inputs = (rows,) if index is None else (rows, index)
    return pl.pallas_call(
        pack_kernel,
        grid_spec=pltpu.PrefetchScalarGridSpec(
            num_scalar_prefetch=1,
            grid=(1,),
            in_specs=[pl.BlockSpec(x.shape, lambda i, t: (0, 0)) for x in inputs],
            out_specs=[pl.BlockSpec(out, lambda i, t: (0, 0))] * 4,
        ),
        out_shape=[jax.ShapeDtypeStruct(out, bf16)] * 4,
        compiler_params=params(),
        cost_estimate=cost(2),
        name="pack",
    )(table, *inputs)


def unpack_kernel(table_ref, keep_ref, own_ref, *refs):
    *got, out_ref = refs
    prompt = table_ref[IS_PROMPT] == 1
    place_of = lambda k: pl.ds(pl.multiple_of(table_ref[PIECES + k] * PART, PART), PART)
    out_ref[place_of(0), :] = keep_ref[...]
    out_ref[place_of(2), :] = got[1][...]
    out_ref[place_of(3), :] = got[2][...]

    @pl.when(prompt)
    def _():
        out_ref[place_of(1), :] = got[0][...]

    @pl.when(jnp.logical_not(prompt))
    def _():
        out_ref[place_of(1), :] = own_ref[...]


def unpack_call(table, pieces):
    rows, width = pieces[0].shape
    return pl.pallas_call(
        unpack_kernel,
        grid_spec=pltpu.PrefetchScalarGridSpec(
            num_scalar_prefetch=1,
            grid=(1,),
            in_specs=[pl.BlockSpec((rows, width), lambda i, t: (0, 0))] * 5,
            out_specs=pl.BlockSpec((4 * rows, width), lambda i, t: (0, 0)),
        ),
        out_shape=jax.ShapeDtypeStruct((4 * rows, width), bf16),
        compiler_params=params(),
        cost_estimate=cost(0),
        name="unpack",
    )(table, *pieces)


def first_kernel(pieces, table_ref, *refs):
    sources = refs[:pieces]
    gain_ref, shift_ref, kv_weight_ref = refs[pieces : pieces + 3]
    refs = refs[pieces + 3 :]
    step = pl.program_id(0)
    first_ref = refs[0]
    tokens_ref = refs[-1]
    pick_piece(step, table_ref, sources, tokens_ref)
    unit, _ = column_norm(tokens_ref[...].astype(f32).T)
    first = (unit * gain_ref[...] + shift_ref[...]).astype(bf16)
    first_ref[...] = first
    kv = dot_tn(kv_weight_ref[...], first).T.astype(bf16)
    if pieces == 1:
        refs[1][...] = kv
        return
    shared_ref, own_ref, index_ref, flat_ref, _ = refs[1:]
    flat_ref[...] = tokens_ref[...]
    topk, rows = index_ref.shape
    keep, own, *got = sources
    prompt = table_ref[IS_PROMPT] == 1
    which = ((step == 0), (step == 1) & jnp.logical_not(prompt), (step == 1) & prompt)
    for chosen, ref in zip(which + ((step == 2), (step == 3)), (keep, own, *got)):

        @pl.when(chosen)
        def _():
            index_ref[...] = ref[PART:, :rows][:topk, :].astype(f32).astype(jnp.int32)

    for slot, half in ((LOW_SLOT, 0), (HIGH_SLOT, 1)):

        @pl.when(step == table_ref[slot])
        def _():
            shared_ref[half * PART : (half + 1) * PART, :] = kv

    for half in range(2):

        @pl.when(step == table_ref[OWN_SLOT] + half)
        def _():
            own_ref[half * PART : (half + 1) * PART, :] = kv


def first_call(table, sources, count, topk, gain, shift, kv_weight):
    width, pair = kv_weight.shape
    keep = lambda shape: pl.BlockSpec(shape, lambda i, t: (0, 0))
    shape = jax.ShapeDtypeStruct
    split = len(sources) > 1
    outs = [(pl.BlockSpec((width, TILE), lambda i, t: (0, i)), shape((width, count), bf16))]
    rows = lambda n: pl.BlockSpec((TILE, n), lambda i, t: (i, 0))
    if split:
        outs += [
            (keep((2 * PART, pair)), shape((2 * PART, pair), bf16)),
            (keep((2 * PART, pair)), shape((2 * PART, pair), bf16)),
            (pl.BlockSpec((topk, TILE), lambda i, t: (0, i)), shape((topk, count), jnp.int32)),
            (rows(width), shape((count, width), bf16)),
        ]
    else:
        outs += [(rows(pair), shape((count, pair), bf16))]
    return pl.pallas_call(
        functools.partial(first_kernel, len(sources)),
        grid_spec=pltpu.PrefetchScalarGridSpec(
            num_scalar_prefetch=1,
            grid=(count // TILE,),
            in_specs=piece_specs(sources)
            + [keep((width, 1)), keep((width, 1)), keep((width, pair))],
            out_specs=[x for x, _ in outs],
            scratch_shapes=[pltpu.VMEM((TILE, width), bf16)],
        ),
        out_shape=[x for _, x in outs],
        compiler_params=params(),
        cost_estimate=cost(5),
        name="first_norm",
    )(table, *sources, gain, shift, kv_weight)


def join_rows(shard, own_ref, other_ref, all_ref, start=0):
    half = own_ref.shape[0]
    all_ref[pl.ds(pl.multiple_of(shard * half, half), half), :] = own_ref[...]
    rows = pl.ds(pl.multiple_of((1 - shard) * half, half), half)
    all_ref[rows, :] = other_ref[start : start + half, :]


def query_kernel(
    table_ref, first_ref, own_ref, other_ref, router_ref, index_ref,
    qt_ref, q_ref, gate_ref, query_weight_ref,
):
    topk = index_ref.shape[0]

    @pl.when(pl.program_id(0) == 0)
    def _():
        join_rows(table_ref[SHARD], own_ref, other_ref, query_weight_ref)

    head = qt_ref.shape[1]
    experts = query_weight_ref.shape[1] // head
    first = first_ref[...]
    projected = dot_tn(query_weight_ref[...], first)
    logits = dot_tn(router_ref[...], first)
    index = index_ref[...]
    picked = jnp.zeros(index.shape, f32)
    for expert in range(experts):
        picked = jnp.where(index == expert, logits[expert : expert + 1, :], picked)
    picked = jnp.exp(picked - jnp.max(picked, axis=0, keepdims=True))
    gate_ref[...] = picked / jnp.sum(picked, axis=0, keepdims=True)
    for part in range(TILE // ROWS):
        lanes = slice(part * ROWS, (part + 1) * ROWS)
        for j in range(topk):
            row = index[j : j + 1, lanes]
            chosen = jnp.zeros((head, ROWS), f32)
            for expert in range(experts):
                chosen = jnp.where(
                    row == expert, projected[expert * head : (expert + 1) * head, lanes], chosen
                )
            qt_ref[part, :, j * ROWS : (j + 1) * ROWS] = chosen.astype(bf16)
            q_ref[part, j * ROWS : (j + 1) * ROWS, :] = chosen.T.astype(bf16)


def query_call(table, first, own, other, router, index, head):
    width, count = first.shape
    topk = index.shape[0]
    tiles = count // ROWS
    per = TILE // ROWS
    keep = lambda shape: pl.BlockSpec(shape, lambda i, s: (0, 0))
    return pl.pallas_call(
        query_kernel,
        grid_spec=pltpu.PrefetchScalarGridSpec(
            num_scalar_prefetch=1,
            grid=(count // TILE,),
            in_specs=[
                pl.BlockSpec((width, TILE), lambda i, s: (0, i)),
                keep(own.shape),
                keep(other.shape),
                keep(router.shape),
                pl.BlockSpec((topk, TILE), lambda i, s: (0, i)),
            ],
            out_specs=[
                pl.BlockSpec((per, head, topk * ROWS), lambda i, s: (i, 0, 0)),
                pl.BlockSpec((per, topk * ROWS, head), lambda i, s: (i, 0, 0)),
                pl.BlockSpec((topk, TILE), lambda i, s: (0, i)),
            ],
            scratch_shapes=[pltpu.VMEM((width, own.shape[1]), bf16)],
        ),
        out_shape=[
            jax.ShapeDtypeStruct((tiles, head, topk * ROWS), bf16),
            jax.ShapeDtypeStruct((tiles, topk * ROWS, head), bf16),
            jax.ShapeDtypeStruct((topk, count), f32),
        ],
        compiler_params=params(),
        cost_estimate=cost(10),
        name="queries",
    )(table, first, own, other, router, index)


def tile_ranges(base):
    prompt = base < PROMPT
    begin = jnp.where(prompt, base // FULL * FULL, PROMPT)
    position = jnp.where(prompt, begin, PROMPT + (base - PROMPT) // CLEN * CLEN)
    parts = (base + ROWS - position + PART - 1) // PART
    return begin // FULL, begin, position, parts


def allowed_mask(position, base, width):
    key_pos = position + lax.broadcasted_iota(jnp.int32, (PART, width), 0)
    query_pos = base + lax.rem(lax.broadcasted_iota(jnp.int32, (PART, width), 1), ROWS)
    return key_pos <= query_pos


def for_slots(refs, table_ref, start, visit):
    slot = 0
    for ref in refs:
        for row in range(0, ref.shape[0], PART):
            place_of = pl.multiple_of(table_ref[start + slot] * PART, PART)
            visit(ref, row, pl.ds(place_of, PART))
            slot += 1


def attend_kernel(start, buffers, table_ref, *refs):
    sources = refs[:buffers]
    qt_ref = refs[buffers]
    out_ref, factor_ref, probs_ref = refs[buffers + 1 : buffers + 4]
    refs = refs[buffers + 4 :]
    kv_ref, vt_ref, knorm_ref, acc_ref, max_ref = refs[:5]
    full_ref, part_ref, twice_ref, full_sem, part_sem, twice_sem, done_ref = refs[5:]
    tile = pl.program_id(0)
    head, width = qt_ref.shape[1:]
    factor = LOG2E * head ** (-0.5)

    @pl.when(tile == 0)
    def _():
        knorm_ref[0] = 0.0
        for kind in range(3):
            done_ref[kind] = 0

        def turn(ref, row, span):
            rows = ref[row : row + PART, :]
            kv_ref[span, :] = rows
            both = rows.T
            vt_ref[:head, span] = both[head:, :]
            vt_ref[head:, span] = jnp.ones((vt_ref.shape[0] - head, PART), bf16)
            keys = both[:head, :].astype(f32)
            most = jnp.max(jnp.sum(keys * keys, axis=0, keepdims=True))
            knorm_ref[0] = jnp.maximum(knorm_ref[0], most)

        for_slots(sources, table_ref, start, turn)

    base = table_ref[BASES + tile]
    steps, begin, position, parts = tile_ranges(base)
    query = qt_ref[0].astype(f32)
    qnorm = jnp.max(jnp.sum(query * query, axis=0, keepdims=True))
    narrow = qnorm * knorm_ref[0] * (factor * factor) < 60.0 * 60.0
    acc_ref[...] = jnp.zeros(acc_ref.shape, f32)
    max_ref[...] = jnp.zeros(max_ref.shape, f32)

    def writer(kind, buffer_ref, sem, span):
        count = done_ref[kind]
        slot = lax.rem(count, 2)
        copy = pltpu.make_async_copy(
            buffer_ref.at[slot], probs_ref.at[tile, span, :], sem.at[slot]
        )
        done_ref[kind] = count + 1

        @pl.when(count >= 2)
        def _():
            copy.wait()

        def write(probs):
            buffer_ref[slot] = probs
            copy.start()

        return write

    def span_of(offset, size):
        return pl.ds(pl.multiple_of(offset, size), size)

    def scores_of(span):
        return dot(kv_ref[span, :head], qt_ref[0]) * factor

    @pl.when(narrow)
    def _():
        def whole_step(kind, buffer_ref, sem, offset, size):
            span = pl.ds(pl.multiple_of(offset, FULL), size)
            write = writer(kind, buffer_ref, sem, span)
            probs = jnp.exp2(scores_of(span)).astype(bf16)
            write(probs)
            acc_ref[...] += dot(vt_ref[:, span], probs)

        def step(i, carry):
            whole_step(2, twice_ref, twice_sem, i * 2 * FULL, 2 * FULL)
            return carry

        @pl.when(lax.rem(steps, 2) == 1)
        def _():
            whole_step(0, full_ref, full_sem, (steps - 1) * FULL, FULL)

        def part(i, carry):
            span = span_of(begin + i * PART, PART)
            write = writer(1, part_ref, part_sem, span)
            mask = allowed_mask(position + i * PART, base, width)
            probs = jnp.exp2(jnp.where(mask, scores_of(span), mask_fill)).astype(bf16)
            write(probs)
            acc_ref[...] += dot(vt_ref[:, span], probs)
            return carry

        lax.fori_loop(0, steps // 2, step, 0)
        lax.fori_loop(0, parts, part, 0)
        factor_ref[0] = 1.0 / acc_ref[head : head + 1, :]

    @pl.when(jnp.logical_not(narrow))
    def _():
        max_ref[...] = jnp.full(max_ref.shape, mask_fill, f32)
        count = steps * (FULL // PART) + parts

        def masked(i):
            before = i < steps * (FULL // PART)
            offset = i * PART
            span = span_of(offset, PART)
            shifted = jnp.where(before, -(1 << 24), position + offset - begin)
            mask = allowed_mask(shifted, base, width)
            return span, mask, jnp.where(mask, scores_of(span), mask_fill)

        def part(i, carry):
            span, mask, scores = masked(i)
            old = max_ref[...]
            new = jnp.maximum(old, jnp.max(scores, axis=0, keepdims=True))
            probs = jnp.where(mask, jnp.exp2(scores - new), 0.0).astype(bf16)
            acc_ref[...] = acc_ref[...] * jnp.exp2(old - new) + dot(vt_ref[:, span], probs)
            max_ref[...] = new
            return carry

        lax.fori_loop(0, count, part, 0)
        max_ref[...] = max_ref[...] + jnp.log2(acc_ref[head : head + 1, :])

        def again(i, carry):
            span, mask, scores = masked(i)
            write = writer(1, part_ref, part_sem, span)
            write(jnp.where(mask, jnp.exp2(scores - max_ref[...]), 0.0).astype(bf16))
            return carry

        lax.fori_loop(0, count, again, 0)
        factor_ref[0] = jnp.ones(max_ref.shape, f32)

    out_ref[0] = acc_ref[:head, :] / acc_ref[head : head + 1, :]

    @pl.when(tile == pl.num_programs(0) - 1)
    def _():
        kinds = ((full_ref, full_sem), (part_ref, part_sem), (twice_ref, twice_sem))
        for kind, (buffer_ref, sem) in enumerate(kinds):
            for slot in range(2):

                @pl.when(done_ref[kind] > slot)
                def _():
                    rows = pl.ds(0, buffer_ref.shape[1])
                    pltpu.make_async_copy(
                        buffer_ref.at[slot], probs_ref.at[0, rows, :], sem.at[slot]
                    ).wait()


def attend_call(start, sources, table, qt):
    tiles, head, width = qt.shape
    total_keys = sum(x.shape[0] for x in sources)
    pair = sources[0].shape[1]
    one = lambda shape: pl.BlockSpec((1,) + shape, lambda i, t: (i, 0, 0))
    keep = lambda x: pl.BlockSpec(x.shape, lambda i, t: (0, 0))
    return pl.pallas_call(
        functools.partial(attend_kernel, start, len(sources)),
        grid_spec=pltpu.PrefetchScalarGridSpec(
            num_scalar_prefetch=1,
            grid=(tiles,),
            in_specs=[keep(x) for x in sources] + [one((head, width))],
            out_specs=[one((head, width)), one((1, width)), pl.BlockSpec(memory_space=pl.ANY)],
            scratch_shapes=[
                pltpu.VMEM((total_keys, pair), bf16),
                pltpu.VMEM((head + 16, total_keys), bf16),
                pltpu.SMEM((1,), f32),
                pltpu.VMEM((head + 16, width), f32),
                pltpu.VMEM((1, width), f32),
                pltpu.VMEM((2, FULL, width), bf16),
                pltpu.VMEM((2, PART, width), bf16),
                pltpu.VMEM((2, 2 * FULL, width), bf16),
                pltpu.SemaphoreType.DMA((2,)),
                pltpu.SemaphoreType.DMA((2,)),
                pltpu.SemaphoreType.DMA((2,)),
                pltpu.SMEM((3,), jnp.int32),
            ],
        ),
        out_shape=[
            jax.ShapeDtypeStruct((tiles, head, width), f32),
            jax.ShapeDtypeStruct((tiles, 1, width), f32),
            jax.ShapeDtypeStruct((tiles, total_keys, width), bf16),
        ],
        compiler_params=params(),
        cost_estimate=cost(64),
        name="attend",
    )(table, *sources, qt)


def attend_back_kernel(start, buffers, table_ref, *refs):
    sources = refs[:buffers]
    q_ref, dot_ref, do_ref, delta_ref, probs_ref = refs[buffers : buffers + 5]
    refs = refs[buffers + 5 :]
    dq_ref = refs[0]
    outs = refs[1 : 1 + buffers]
    refs = refs[1 + buffers :]
    kv_ref, kt_ref, dkv_ref, rows_ref, full_ref, part_ref, full_sem, part_sem, done_ref = refs
    tile = pl.program_id(0)
    tiles = pl.num_programs(0)
    width, head = q_ref.shape[1:]
    scale = head ** (-0.5)

    @pl.when(tile == 0)
    def _():
        done_ref[0] = 0
        rows_ref[...] = jnp.zeros(rows_ref.shape, bf16)

        def turn(ref, row, span):
            rows = ref[row : row + PART, :]
            kv_ref[span, :] = rows
            kt_ref[:, span] = rows.T[:head, :]
            dkv_ref[span, :] = jnp.zeros((PART, 2 * head), f32)

        for_slots(sources, table_ref, start, turn)

    def steps_of(which):
        return tile_ranges(table_ref[BASES + jnp.clip(which, 0, tiles - 1)])[0]

    steps, begin, _, parts = tile_ranges(table_ref[BASES + tile])

    def full_copy(which, i, slot):
        rows = pl.ds(pl.multiple_of(i * FULL, FULL), FULL)
        return pltpu.make_async_copy(
            probs_ref.at[which, rows, :], full_ref.at[slot], full_sem.at[slot]
        )

    def part_copy(i):
        slot = lax.rem(i, 2)
        rows = pl.ds(pl.multiple_of(begin + i * PART, PART), PART)
        return pltpu.make_async_copy(
            probs_ref.at[tile, rows, :], part_ref.at[slot], part_sem.at[slot]
        )

    done = done_ref[0]

    @pl.when((steps > 0) & ((tile == 0) | (steps_of(tile - 1) == 0)))
    def _():
        full_copy(tile, 0, lax.rem(done, 2)).start()

    for i in range(2):

        @pl.when(i < parts)
        def _():
            part_copy(i).start()

    dq_ref[...] = jnp.zeros(dq_ref.shape, f32)
    rows_ref[:width, :head] = q_ref[0]
    rows_ref[width:, head:] = do_ref[0]

    def block(offset, size, probs):
        span = pl.ds(pl.multiple_of(offset, size), size)
        prob_grad = dot(kv_ref[span, head:], dot_ref[0])
        score_grad = (probs.astype(f32) * (prob_grad - delta_ref[0])).astype(bf16)
        dq_ref[0] += dot(kt_ref[:, span], score_grad)
        dkv_ref[span, :] += dot(jnp.concatenate([score_grad, probs], axis=1), rows_ref[...])

    def step(i, carry):
        slot = lax.rem(done + i, 2)

        @pl.when(i + 1 < steps)
        def _():
            full_copy(tile, i + 1, 1 - slot).start()

        @pl.when((i + 1 == steps) & (tile + 1 < tiles) & (steps_of(tile + 1) > 0))
        def _():
            full_copy(tile + 1, 0, 1 - slot).start()

        full_copy(tile, i, slot).wait()
        block(i * FULL, FULL, full_ref[slot])
        return carry

    def part(i, carry):
        part_copy(i).wait()
        block(begin + i * PART, PART, part_ref[lax.rem(i, 2)])

        @pl.when(i + 2 < parts)
        def _():
            part_copy(i + 2).start()

        return carry

    lax.fori_loop(0, steps, step, 0)
    lax.fori_loop(0, parts, part, 0)
    done_ref[0] = done + steps
    dq_ref[...] = dq_ref[...] * scale

    @pl.when(tile == tiles - 1)
    def _():
        lane = lax.broadcasted_iota(jnp.int32, (PART, 2 * head), 1)
        both = jnp.where(lane < head, scale, 1.0)

        def finish(ref, row, span):
            ref[row : row + PART, :] = (dkv_ref[span, :] * both).astype(ref.dtype)

        for_slots(outs, table_ref, start, finish)


def attend_back_call(start, sources, kinds, table, q, grad_t, grad, delta, probs):
    tiles, width, head = q.shape
    total_keys = sum(x.shape[0] for x in sources)
    pair = sources[0].shape[1]
    one = lambda shape: pl.BlockSpec((1,) + shape, lambda i, t: (i, 0, 0))
    keep = lambda x: pl.BlockSpec(x.shape, lambda i, t: (0, 0))
    return pl.pallas_call(
        functools.partial(attend_back_kernel, start, len(sources)),
        grid_spec=pltpu.PrefetchScalarGridSpec(
            num_scalar_prefetch=1,
            grid=(tiles,),
            in_specs=[keep(x) for x in sources]
            + [
                one((width, head)),
                one((head, width)),
                one((width, head)),
                one((1, width)),
                pl.BlockSpec(memory_space=pl.ANY),
            ],
            out_specs=[one((head, width))] + [keep(x) for x in sources],
            scratch_shapes=[
                pltpu.VMEM((total_keys, pair), bf16),
                pltpu.VMEM((head, total_keys), bf16),
                pltpu.VMEM((total_keys, pair), f32),
                pltpu.VMEM((2 * width, pair), bf16),
                pltpu.VMEM((2, FULL, width), bf16),
                pltpu.VMEM((2, PART, width), bf16),
                pltpu.SemaphoreType.DMA((2,)),
                pltpu.SemaphoreType.DMA((2,)),
                pltpu.SMEM((1,), jnp.int32),
            ],
        ),
        out_shape=[jax.ShapeDtypeStruct((tiles, head, width), f32)]
        + [jax.ShapeDtypeStruct(x.shape, kind) for x, kind in zip(sources, kinds)],
        compiler_params=params(),
        cost_estimate=cost(0),
        name="attend_back",
    )(table, *sources, q, grad_t, grad, delta, probs)


def place(index, pieces, expert):
    total = jnp.zeros(pieces[0].shape, f32)
    for j, piece in enumerate(pieces):
        total = jnp.where(index[j : j + 1, :] == expert, piece, total)
    return total


def middle_kernel(pieces, table_ref, *refs):
    sources = refs[:pieces]
    refs = refs[pieces:]
    outs = 4 if pieces > 1 else 1
    layer_out_refs = refs[MIDDLE_INPUTS : MIDDLE_INPUTS + outs]
    refs = refs[:MIDDLE_INPUTS] + refs[MIDDLE_INPUTS + outs :]
    middle_body(table_ref, sources, layer_out_refs, *refs)


MIDDLE_INPUTS = 14


def middle_body(
    table_ref,
    sources,
    layer_out_refs,
    tokens_ref,
    index_ref,
    gate_ref,
    attended_ref,
    factor_ref,
    output_own_ref,
    down_own_ref,
    both_other_ref,
    up_own_ref,
    up_other_ref,
    gain_ref,
    shift_ref,
    up_bias_ref,
    down_bias_ref,
    middle_grad_ref,
    grad_t_ref,
    grad_rows_ref,
    delta_ref,
    logit_grad_ref,
    output_weight_grad_ref,
    up_weight_grad_ref,
    down_weight_grad_ref,
    gain_grad_ref,
    shift_grad_ref,
    up_bias_grad_ref,
    down_bias_grad_ref,
    grad_ref,
    output_weight_ref,
    up_weight_ref,
    down_weight_ref,
    spread_ref,
    chosen_ref,
    dwo_ref,
    dup_ref,
    ddown_ref,
):
    step = pl.program_id(0)
    topk = index_ref.shape[0]
    head = attended_ref.shape[1]
    experts = output_weight_ref.shape[0] // head
    per = TILE // ROWS

    @pl.when(step == 0)
    def _():
        shard = table_ref[SHARD]
        join_rows(shard, output_own_ref, both_other_ref, output_weight_ref)
        join_rows(shard, down_own_ref, both_other_ref, down_weight_ref, output_own_ref.shape[0])
        join_rows(shard, up_own_ref, up_other_ref, up_weight_ref)
        for ref in (
            dwo_ref,
            dup_ref,
            ddown_ref,
            gain_grad_ref,
            shift_grad_ref,
            up_bias_grad_ref,
            down_bias_grad_ref,
        ):
            ref[...] = jnp.zeros(ref.shape, ref.dtype)

    pick_piece(step, table_ref, sources, grad_ref)
    index = index_ref[...]
    gate = gate_ref[...]
    for part in range(per):
        lanes = slice(part * ROWS, (part + 1) * ROWS)
        pieces = [
            attended_ref[part, :, j * ROWS : (j + 1) * ROWS] * gate[j : j + 1, lanes]
            for j in range(topk)
        ]
        for expert in range(experts):
            spread_ref[expert * head : (expert + 1) * head, lanes] = place(
                index[:, lanes], pieces, expert
            ).astype(bf16)

    middle = tokens_ref[...].astype(f32).T + dot_tn(output_weight_ref[...], spread_ref[...])
    unit, inverse = column_norm(middle)
    second = (unit * gain_ref[...] + shift_ref[...]).astype(bf16)
    pre = dot_tn(up_weight_ref[...], second) + up_bias_ref[...]
    coeff = math.sqrt(2.0 / math.pi)
    square = pre * pre
    wave = jnp.tanh(coeff * pre * (1.0 + 0.044715 * square))
    half = 0.5 * (1.0 + wave)
    hidden = (pre * half).astype(bf16)
    slope = half + 0.5 * pre * (1.0 - wave * wave) * (coeff * (1.0 + 3 * 0.044715 * square))
    result = middle + dot_tn(down_weight_ref[...], hidden) + down_bias_ref[...]
    store_piece(step, layer_out_refs, result.T.astype(bf16))

    grad_rows = grad_ref[...]
    grad_wide = grad_rows.astype(f32)
    grad_t = grad_wide.T
    ddown_ref[...] += dot(hidden, grad_rows)
    down_bias_grad_ref[...] += jnp.sum(grad_wide, axis=0, keepdims=True)
    pre_grad = (dot(down_weight_ref[...], grad_t.astype(bf16)) * slope).astype(bf16)
    dup_ref[...] += dot_nt(second, pre_grad)
    up_bias_grad_ref[...] += fold_lanes(pre_grad.astype(f32))
    second_grad = dot(up_weight_ref[...], pre_grad)
    gain_grad_ref[...] += fold_lanes(second_grad * unit)
    shift_grad_ref[...] += fold_lanes(second_grad)
    middle_grad = grad_t + column_norm_back(second_grad, unit, inverse, gain_ref[...])
    middle_grad_ref[...] = middle_grad
    middle_low = middle_grad.astype(bf16)
    dwo_ref[...] += dot_nt(spread_ref[...], middle_low)
    chosen_ref[...] = dot(output_weight_ref[...], middle_low)

    for part in range(per):
        lanes = slice(part * ROWS, (part + 1) * ROWS)
        picks = []
        for j in range(topk):
            span = slice(j * ROWS, (j + 1) * ROWS)
            row = index[j : j + 1, lanes]
            chosen = jnp.zeros((head, ROWS), f32)
            for expert in range(experts):
                chosen = jnp.where(
                    row == expert, chosen_ref[expert * head : (expert + 1) * head, lanes], chosen
                )
            attended = attended_ref[part, :, span]
            picks.append(jnp.sum(chosen * attended, axis=0, keepdims=True))
            back = (chosen * gate[j : j + 1, lanes]).astype(bf16).astype(f32)
            back = (back * factor_ref[part, :, span]).astype(bf16)
            grad_t_ref[part, :, span] = back
            back = back.astype(f32)
            grad_rows_ref[part, span, :] = back.T.astype(bf16)
            delta_ref[part, :, span] = jnp.sum(back * attended, axis=0, keepdims=True)
        gates = [gate[j : j + 1, lanes] for j in range(topk)]
        mean = sum(g * p for g, p in zip(gates, picks))
        rows = [g * (p - mean) for g, p in zip(gates, picks)]
        numbers = lax.broadcasted_iota(jnp.int32, (logit_grad_ref.shape[0], ROWS), 0)
        logit = jnp.zeros(numbers.shape, f32)
        for j in range(topk):
            logit = jnp.where(index[j : j + 1, lanes] == numbers, rows[j], logit)
        logit_grad_ref[:, lanes] = logit.astype(bf16)

    @pl.when(step == pl.num_programs(0) - 1)
    def _():
        output_weight_grad_ref[...] = dwo_ref[...].astype(bf16)
        up_weight_grad_ref[...] = dup_ref[...].astype(bf16)
        down_weight_grad_ref[...] = ddown_ref[...].astype(bf16)


def middle_call(
    table, sources, tokens, index, gate, attended, factor, weights,
    gain, shift, up_bias, down_bias, padded,
):
    count, width = tokens.shape
    topk = index.shape[0]
    tiles, head, wide = attended.shape
    per = TILE // ROWS
    spread = 2 * weights[0].shape[0]
    hidden = 2 * weights[1].shape[0]
    keep = lambda shape: pl.BlockSpec(shape, lambda i, s: tuple(0 for _ in shape))
    rows = pl.BlockSpec((TILE, width), lambda i, s: (i, 0))
    columns = lambda n: pl.BlockSpec((n, TILE), lambda i, s: (0, i))
    tile = lambda shape: pl.BlockSpec((per,) + shape, lambda i, s: (i, 0, 0))
    shape = jax.ShapeDtypeStruct
    if len(sources) > 1:
        outs = [(keep((TILE, width)), shape((TILE, width), bf16))] * 4
    else:
        outs = [(rows, shape((count, width), bf16))]
    outs += [
        (columns(width), shape((width, count), f32)),
        (tile((head, wide)), shape((tiles, head, wide), bf16)),
        (tile((wide, head)), shape((tiles, wide, head), bf16)),
        (tile((1, wide)), shape((tiles, 1, wide), f32)),
        (columns(padded), shape((padded, count), bf16)),
        (keep((spread, width)), shape((spread, width), bf16)),
        (keep((width, hidden)), shape((width, hidden), bf16)),
        (keep((hidden, width)), shape((hidden, width), bf16)),
        (keep((width, 128)), shape((width, 128), f32)),
        (keep((width, 128)), shape((width, 128), f32)),
        (keep((hidden, 128)), shape((hidden, 128), f32)),
        (keep((1, width)), shape((1, width), f32)),
    ]
    return pl.pallas_call(
        functools.partial(middle_kernel, len(sources)),
        grid_spec=pltpu.PrefetchScalarGridSpec(
            num_scalar_prefetch=1,
            grid=(count // TILE,),
            in_specs=piece_specs(sources)
            + [rows, columns(topk), columns(topk), tile((head, wide)), tile((1, wide))]
            + [keep(w.shape) for w in weights]
            + [keep((width, 1)), keep((width, 1)), keep((hidden, 1)), keep((width, 1))],
            out_specs=[x for x, _ in outs],
            scratch_shapes=[
                pltpu.VMEM((TILE, width), bf16),
                pltpu.VMEM((spread, width), bf16),
                pltpu.VMEM((width, hidden), bf16),
                pltpu.VMEM((hidden, width), bf16),
                pltpu.VMEM((spread, TILE), bf16),
                pltpu.VMEM((spread, TILE), f32),
                pltpu.VMEM((spread, width), f32),
                pltpu.VMEM((width, hidden), f32),
                pltpu.VMEM((hidden, width), f32),
            ],
        ),
        out_shape=[x for _, x in outs],
        compiler_params=params(),
        cost_estimate=cost(44),
        name="middle",
    )(table, *sources, tokens, index, gate, attended, factor, *weights,
      gain, shift, up_bias, down_bias)


def query_back_kernel(
    table_ref,
    first_ref,
    index_ref,
    dq_ref,
    own_ref,
    other_ref,
    logit_grad_ref,
    router_ref,
    partial_ref,
    keep_ref,
    send_ref,
    router_grad_ref,
    query_weight_ref,
    placed_ref,
    dwq_ref,
    dr_ref,
):
    step = pl.program_id(0)
    topk = index_ref.shape[0]
    head = dq_ref.shape[1]
    experts = query_weight_ref.shape[1] // head

    @pl.when(step == 0)
    def _():
        join_rows(table_ref[SHARD], own_ref, other_ref, query_weight_ref)
        dwq_ref[...] = jnp.zeros(dwq_ref.shape, f32)
        dr_ref[...] = jnp.zeros(dr_ref.shape, f32)

    index = index_ref[...]
    for part in range(TILE // ROWS):
        lanes = slice(part * ROWS, (part + 1) * ROWS)
        pieces = [dq_ref[part, :, j * ROWS : (j + 1) * ROWS] for j in range(topk)]
        for expert in range(experts):
            placed_ref[expert * head : (expert + 1) * head, lanes] = place(
                index[:, lanes], pieces, expert
            ).astype(bf16)
    first = first_ref[...]
    dwq_ref[...] += dot_nt(first, placed_ref[...])
    dr_ref[...] += dot_nt(first, logit_grad_ref[...])
    partial_ref[...] = dot(query_weight_ref[...], placed_ref[...]) + dot(
        router_ref[...], logit_grad_ref[...]
    )

    @pl.when(step == pl.num_programs(0) - 1)
    def _():
        router_grad_ref[...] = dr_ref[...]
        size = keep_ref.shape[2]
        shard, core, side = table_ref[SHARD], table_ref[CORE], table_ref[SIDE]
        for target, half in ((keep_ref, shard), (send_ref, 1 - shard)):
            for i, last in enumerate((core, 1 - core)):
                for j, part in enumerate((side, 1 - side)):
                    at = ((half * 2 + last) * 2 + part) * size
                    rows = pl.ds(pl.multiple_of(at, size), size)
                    target[i, j] = dwq_ref[rows, :].astype(bf16)


def query_back_call(table, first, index, dq, own, other, logit_grad, router):
    width, count = first.shape
    topk = index.shape[0]
    tiles, head, wide = dq.shape
    padded = router.shape[1]
    spread = own.shape[1]
    keep = lambda shape: pl.BlockSpec(shape, lambda i, s: tuple(0 for _ in shape))
    columns = lambda n: pl.BlockSpec((n, TILE), lambda i, s: (0, i))
    shape = jax.ShapeDtypeStruct
    quarters = (2, 2, width // 8, spread)
    return pl.pallas_call(
        query_back_kernel,
        grid_spec=pltpu.PrefetchScalarGridSpec(
            num_scalar_prefetch=1,
            grid=(count // TILE,),
            in_specs=[
                columns(width),
                columns(topk),
                pl.BlockSpec((TILE // ROWS, head, wide), lambda i, s: (i, 0, 0)),
                keep(own.shape),
                keep(other.shape),
                columns(padded),
                keep(router.shape),
            ],
            out_specs=[columns(width), keep(quarters), keep(quarters), keep(router.shape)],
            scratch_shapes=[
                pltpu.VMEM((width, spread), bf16),
                pltpu.VMEM((spread, TILE), bf16),
                pltpu.VMEM((width, spread), f32),
                pltpu.VMEM(router.shape, f32),
            ],
        ),
        out_shape=[
            shape((width, count), f32),
            shape(quarters, bf16),
            shape(quarters, bf16),
            shape(router.shape, f32),
        ],
        compiler_params=params(),
        cost_estimate=cost(0),
        name="query_back",
    )(table, first, index, dq, own, other, logit_grad, router)


def first_back_kernel(pieces, table_ref, *refs):
    tokens_ref, first_ref, partial_ref, middle_grad_ref = refs[:4]
    sources = refs[4 : 4 + pieces]
    kv_weight_ref, gain_ref, rest_ref = refs[4 + pieces : 7 + pieces]
    refs = refs[7 + pieces :]
    outs = 4 if pieces > 1 else 1
    tokens_grad_refs = refs[:outs]
    keep_ref, send_ref, total_ref, gain_grad_ref, shift_grad_ref, dkv_ref = refs[outs:]
    step = pl.program_id(0)
    pair = kv_weight_ref.shape[1]

    @pl.when(step == 0)
    def _():
        total_ref[:, :pair] = jnp.zeros((total_ref.shape[0], pair), f32)
        for ref in (gain_grad_ref, shift_grad_ref):
            ref[...] = jnp.zeros(ref.shape, ref.dtype)

    unit, inverse = column_norm(tokens_ref[...].astype(f32).T)
    if pieces == 1:
        dkv_ref[...] = sources[0][...]
    else:
        low_ref, high_ref, own_ref = sources
        own = table_ref[OWN_SLOT]
        for chosen, ref, half in (
            (table_ref[LOW_SLOT], low_ref, 0),
            (table_ref[HIGH_SLOT], high_ref, 0),
            (own, own_ref, 0),
            (own + 1, own_ref, 1),
        ):

            @pl.when(step == chosen)
            def _():
                dkv_ref[...] = ref[half * PART : (half + 1) * PART, :]

    dkv = dkv_ref[...]
    total_ref[:, :pair] += dot(first_ref[...], dkv)
    first_grad = partial_ref[...] + dot_nt(kv_weight_ref[...], dkv)
    gain_grad_ref[...] += fold_lanes(first_grad * unit)
    shift_grad_ref[...] += fold_lanes(first_grad)
    total = middle_grad_ref[...] + column_norm_back(first_grad, unit, inverse, gain_ref[...])
    store_piece(step, tokens_grad_refs, total.T.astype(bf16))

    @pl.when(step == pl.num_programs(0) - 1)
    def _():
        lane = lax.broadcasted_iota(jnp.int32, rest_ref.shape, 1)
        gains = jnp.sum(gain_grad_ref[...], axis=1, keepdims=True)
        shifts = jnp.sum(shift_grad_ref[...], axis=1, keepdims=True)
        rest = jnp.where(lane == 0, gains, jnp.where(lane == 1, shifts, rest_ref[...]))
        total_ref[:, pair:] = rest
        size = keep_ref.shape[1]
        shard, core = table_ref[SHARD], table_ref[CORE]
        for target, last in ((keep_ref, core), (send_ref, 1 - core)):
            for i, half in enumerate((shard, 1 - shard)):
                rows = pl.ds(pl.multiple_of((half * 2 + last) * size, size), size)
                target[i] = total_ref[rows, :].astype(bf16)


def first_back_call(table, tokens, first, partial, middle_grad, dkv, kv_weight, gain, rest):
    count, width = tokens.shape
    pair = kv_weight.shape[1]
    wide = pair + rest.shape[1]
    columns = lambda n: pl.BlockSpec((n, TILE), lambda i, t: (0, i))
    rows = lambda n: pl.BlockSpec((TILE, n), lambda i, t: (i, 0))
    keep = lambda shape: pl.BlockSpec(shape, lambda i, t: tuple(0 for _ in shape))
    shape = jax.ShapeDtypeStruct
    quarters = (2, width // 4, wide)
    if len(dkv) > 1:
        outs = [(keep((TILE, width)), shape((TILE, width), bf16))] * 4
    else:
        outs = [(rows(width), shape((count, width), bf16))]
    outs += [(keep(quarters), shape(quarters, bf16))] * 2
    return pl.pallas_call(
        functools.partial(first_back_kernel, len(dkv)),
        grid_spec=pltpu.PrefetchScalarGridSpec(
            num_scalar_prefetch=1,
            grid=(count // TILE,),
            in_specs=[rows(width), columns(width), columns(width), columns(width)]
            + piece_specs(dkv)
            + [keep(kv_weight.shape), keep((width, 1)), keep(rest.shape)],
            out_specs=[x for x, _ in outs],
            scratch_shapes=[
                pltpu.VMEM((width, wide), f32),
                pltpu.VMEM((width, 128), f32),
                pltpu.VMEM((width, 128), f32),
                pltpu.VMEM((TILE, pair), bf16),
            ],
        ),
        out_shape=[x for _, x in outs],
        compiler_params=params(),
        cost_estimate=cost(7),
        name="first_back",
    )(table, tokens, first, partial, middle_grad, *dkv, kv_weight, gain, rest)


def after(value, *others):
    return lax.optimization_barrier((value,) + others)[0]


def other_half(value):
    return lax.ppermute(value, "shard", [(0, 1), (1, 0)])


def join(value, other):
    low = lax.axis_index("shard") == 0
    return jnp.concatenate([jnp.where(low, value, other), jnp.where(low, other, value)], axis=0)


def swap(value, mask):
    count = lax.axis_size("ctx")
    return lax.ppermute(value, "ctx", [(i, i ^ mask) for i in range(count)])


def bit_masks(count):
    return [1 << k for k in reversed(range(count.bit_length() - 1))]


def key_orders(count):
    masks = bit_masks(count)
    return masks, masks[:1] + masks[1:-1][::-1] + masks[-1:]


def slots_of(masks):
    return [sum(m for k, m in enumerate(masks) if j >> k & 1) for j in range(1 << len(masks))]


def gather_keys(shared):
    low_order, high_order = key_orders(lax.axis_size("ctx"))
    got = swap(shared, low_order[0])
    low = jnp.concatenate([shared[:PART], got[:PART]], axis=0)
    high = jnp.concatenate([shared[PART:], got[PART:]], axis=0)
    for low_mask, high_mask in zip(low_order[1:-1], high_order[1:-1]):
        low_got, high_got = swap(low, low_mask), swap(high, high_mask)
        low = jnp.concatenate([low, low_got], axis=0)
        high = jnp.concatenate([high, high_got], axis=0)
    return (low, swap(low, low_order[-1])), (high, swap(high, high_order[-1]))


def add_low(a, b):
    return (a.astype(f32) + b.astype(f32)).astype(bf16)


def step_down(total, mask):
    half = total.shape[0] // 2
    return total[:half], swap(total[half:].astype(bf16), mask)


def double(total, mask):
    other = swap(total, mask)
    low = (lax.axis_index("ctx") // mask) % 2 == 0
    return jnp.concatenate([jnp.where(low, total, other), jnp.where(low, other, total)], axis=0)


def home_plan(count, block):
    half = count // 2
    if block != 4 * PART or block * half != PROMPT or block != CLEN or half % 2:
        return None
    sends = [None] * count
    hops = [[], [], []]
    for a in range(half // 2):
        b = half - 1 - a
        p, q = a + half, b + half
        sends[a], sends[b] = (0, 1, 2, 3), (2, 3, 0, 1)
        sends[p] = sends[q] = (0, 3, 1, 2)
        hops[0] += [(a, b), (b, a)]
        hops[1] += [(a, p), (p, a), (b, q), (q, b)]
        hops[2] += [(a, q), (b, p), (p, a), (q, b)]
    places = [[(i, sends[i][0]), (i, sends[i][1]), None, None] for i in range(count)]
    for k, hop in enumerate(hops):
        for source, target in hop:
            places[target][k + 1] = (source, sends[source][k + 1])
    return sends, hops, places


def plan_rows(plan, count):
    sends, _, places = plan
    lower, prompt = HALF // PART, PROMPT // PART
    where = [[source * 4 + quarter for source, quarter in row] for row in places]
    low_slot = [next(k for k in range(4) if row[k] < lower) for row in where]
    high_slot = [next(k for k in range(4) if lower <= row[k] < prompt) for row in where]
    own_slot = [2 if i < count // 2 else 0 for i in range(count)]
    own_at = [[row[k] % 4, row[k + 1] % 4] for row, k in zip(where, own_slot)]
    low_slots, high_slots = (slots_of(masks) for masks in key_orders(count))
    rows = []
    for i in range(count):
        row = list(sends[i]) + [int(i < count // 2), low_slot[i], high_slot[i], own_slot[i]]
        row += [0, i % 2, i // 2 % 2]
        row += [x * PART + r for x in where[i] for r in range(0, PART, ROWS)]
        row += [where[i ^ m][low_slot[i ^ m]] for m in low_slots]
        row += [where[i ^ m][high_slot[i ^ m]] for m in high_slots]
        row += [prompt + x for x in own_at[i] + own_at[i ^ (count // 2)]]
        rows.append(row)
    return rows


def send_pieces(pieces, plan):
    got = [lax.ppermute(piece, "ctx", hop) for piece, hop in zip(pieces[1:], plan[1])]
    return pieces[0], pieces[1], *got


def send_back(pieces, plan):
    hops = [[(t, s) for s, t in hop] for hop in plan[1]]
    got = [lax.ppermute(piece, "ctx", hop) for piece, hop in zip(pieces[1:], hops)]
    return pieces[0], pieces[1], *got


def per_device(
    tokens,
    expert_index,
    first_gain,
    first_shift,
    router_weight,
    query_weight,
    key_weight,
    value_weight,
    output_weight,
    second_gain,
    second_shift,
    up_weight,
    up_bias,
    down_weight,
    down_bias,
    out_grad,
):
    groups, block, width = tokens.shape
    assert groups == 1 and lax.axis_size("shard") == 2
    count = lax.axis_size("ctx")
    me = lax.axis_index("ctx")
    shard = lax.axis_index("shard")
    experts = router_weight.shape[1]
    topk = expert_index.shape[-1]
    head = key_weight.shape[1]
    pair = 2 * head
    padded = 32
    tiles = block // ROWS
    key_table = BASES + tiles
    plan = home_plan(count, block)
    if plan:
        table = jnp.array(plan_rows(plan, count), jnp.int32)[me]
        table = table + shard * (jnp.arange(table.shape[0], dtype=jnp.int32) == SHARD)
        packed = pack_call(table, tokens[0], expert_index[0].T)
        sources = send_pieces(packed, plan)
        key_weight, packed = lax.optimization_barrier((key_weight, packed))
    else:
        base = me * block
        numbers = [0, 0, 0, 0, 0, 0, 0, 0, shard, me % 2, me // 2 % 2]
        table = jnp.concatenate(
            [
                jnp.stack([jnp.int32(x) for x in numbers]),
                base + jnp.arange(tiles, dtype=jnp.int32) * ROWS,
                jnp.arange((PROMPT + CLEN) // PART, dtype=jnp.int32),
            ]
        )
        sources = (tokens[0],)

    spare = jnp.zeros((key_weight.shape[0], padded - experts), bf16)
    vectors = [first_gain, first_shift, second_gain, second_shift, down_bias]
    half_width = width // 2
    small = jnp.concatenate(
        [key_weight, value_weight, router_weight, spare]
        + [v[:, None] for v in vectors]
        + [up_bias.reshape(half_width, -1)],
        axis=1,
    )
    small = join(small, other_half(small))
    query_other = other_half(after(query_weight, small))
    kv_weight = small[:, :pair]
    router = small[:, pair : pair + padded]
    at = pair + padded
    columns = [small[:, at + i : at + i + 1].astype(f32) for i in range(len(vectors))]
    gain_one, shift_one, gain_two, shift_two, down_bias_all = columns
    up_bias_all = small[:, at + len(vectors) :].reshape(-1, 1).astype(f32)

    both_weights = jnp.concatenate([output_weight, down_weight], axis=0)
    early_work = (both_weights, router, up_bias_all, *columns)
    if plan:
        grads = pack_call(after(table, small), out_grad[0])
        early_work += tuple(grads)
    table, early_work = lax.optimization_barrier((table, early_work))
    both_weights, router, up_bias_all, *rest = early_work
    gain_one, shift_one, gain_two, shift_two, down_bias_all = rest[: len(vectors)]
    grads = rest[len(vectors) :]
    first_out = first_call(table, sources, block, topk, gain_one, shift_one, kv_weight)
    if plan:
        first, shared, own, index, flat = first_out
        low_keys, high_keys = gather_keys(shared)
        partner = swap(own, count // 2)
        high_keys += (own, partner)
    else:
        first, kv = first_out
        flat = tokens[0]
        index = expert_index[0].T
        gathered = lax.all_gather(kv, "ctx", axis=0, tiled=True)
        segment = jnp.maximum(base, PROMPT) // CLEN * CLEN
        own = lax.dynamic_slice_in_dim(gathered, segment, CLEN, 0)
        quarter = HALF // 2
        low_keys = (gathered[:quarter], gathered[quarter:HALF])
        high_keys = (
            gathered[HALF : HALF + quarter], gathered[HALF + quarter : PROMPT],
            own[: CLEN // 2], own[CLEN // 2 :],
        )

    qt, q, gate = query_call(table, first, query_weight, query_other, router, index, head)
    both_other = other_half(after(both_weights, query_other))
    weights = (
        output_weight, down_weight, both_other, up_weight, other_half(after(up_weight, query_other))
    )
    if plan:
        grads = send_pieces(after(tuple(grads), *low_keys, *high_keys), plan)
    else:
        grads = (out_grad[0],)
    keys = low_keys + high_keys
    attended, factor, probs = attend_call(key_table, keys, table, qt)
    outs = 4 if plan else 1
    middle = middle_call(
        table, grads, flat, index, gate, attended, factor, weights,
        gain_two, shift_two, up_bias_all, down_bias_all, padded,
    )
    layer_out = middle[:outs]
    (
        middle_grad, grad_t, grad_rows, delta, logit_grad,
        output_weight_grad, up_weight_grad, down_weight_grad,
        second_gain_grad, second_shift_grad, up_bias_grad, down_bias_grad,
    ) = middle[outs:]

    early = lax.psum((output_weight_grad, up_weight_grad, down_weight_grad), ("ctx", "shard"))
    if plan:
        layer_out = send_back(layer_out, plan)
    kinds = (f32, bf16, f32, bf16, f32, bf16) if plan else (bf16,) * 6
    dq, *key_grads = attend_back_call(
        key_table, keys, kinds, table, q, grad_t, grad_rows, delta, probs
    )
    dq, key_grads, layer_out = lax.optimization_barrier((dq, key_grads, layer_out))
    if plan:
        low_near, low_far, high_near, high_far, own_near, own_far = key_grads
        low_got, high_got = swap(low_far, 1), swap(high_far, 1)
    partial, keep, send, router_grad = query_back_call(
        table, first, index, dq, query_weight, query_other, logit_grad, router
    )
    sums = (second_gain_grad, second_shift_grad, down_bias_grad, up_bias_grad)
    router_grad, layer_out, *sums = lax.optimization_barrier((router_grad, layer_out, *sums))
    second_gain_grad, second_shift_grad, down_bias_grad, up_bias_grad = sums
    layer_out = unpack_call(table, layer_out) if plan else layer_out[0]
    rest = jnp.concatenate(
        [
            jnp.zeros((width, 2), f32),
            jnp.sum(second_gain_grad, axis=1)[:, None],
            jnp.sum(second_shift_grad, axis=1)[:, None],
            down_bias_grad[0][:, None],
            jnp.sum(up_bias_grad, axis=1).reshape(width, -1),
        ],
        axis=1,
    )
    bias_columns = rest.shape[1] - 5
    rest = jnp.pad(rest, ((0, 0), (0, padded - rest.shape[1])))
    rest = jnp.concatenate([rest, router_grad, jnp.zeros((width, 128 - 2 * padded), f32)], axis=1)
    total = add_low(keep, other_half(send))
    if plan:
        low_order, high_order = key_orders(count)
        low_keep, low_got = step_down(low_near + low_got.astype(f32), low_order[2])
        high_keep, high_got = step_down(high_near + high_got.astype(f32), high_order[2])
        total, rest, layer_out, *early = lax.optimization_barrier(
            (total, rest, layer_out, *early)
        )
        query_got = swap(total[1], 1)
    if plan:
        low_got, high_got, total, own_far = lax.optimization_barrier(
            (low_got, high_got, total, own_far)
        )
        own_got = swap(own_far, count // 2)
        low_keep, low_got = step_down(low_keep + low_got.astype(f32), low_order[1])
        high_keep, high_got = step_down(high_keep + high_got.astype(f32), high_order[1])
        low_got, high_got, query_got = lax.optimization_barrier((low_got, high_got, query_got))
        total = add_low(total[0], query_got)
        query_got = swap(total[1], 2)
        low_sum = low_keep + low_got.astype(f32)
        high_sum = high_keep + high_got.astype(f32)
        both = jnp.concatenate([low_sum[PART:], high_sum[PART:]], axis=0).astype(bf16)
        both = swap(both, low_order[0])
        both, query_got = lax.optimization_barrier((both, query_got))
        dkv = (
            add_low(low_sum[:PART], both[:PART]),
            add_low(high_sum[:PART], both[PART:]),
            add_low(own_near, own_got),
        )
    else:
        rows = count * block - PROMPT
        dall = jnp.concatenate(key_grads[:4] + [jnp.zeros((rows, pair), bf16)])
        own_grad = jnp.concatenate(key_grads[4:])
        own_grad = jnp.where(base >= PROMPT, own_grad, jnp.zeros_like(own_grad))
        dall = lax.dynamic_update_slice_in_dim(dall, own_grad, segment, 0)
        dkv = (lax.psum_scatter(dall, "ctx", scatter_dimension=0, tiled=True),)
        total = add_low(total[0], swap(total[1], 1))
        query_got = swap(total[1], 2)
    total = add_low(total[0], query_got)
    query_got = swap(total, 4)
    done = first_back_call(
        table, flat, first, partial, middle_grad, dkv, kv_weight, gain_one, rest
    )
    tokens_grad = done[:outs]
    (keep, send), early, query_got = lax.optimization_barrier((done[outs:], early, query_got))
    if plan:
        tokens_grad = send_back(tokens_grad, plan)
    total = add_low(total, query_got)
    small_sum = add_low(keep, swap(send, 1))
    total = add_low(total, swap(total, 8))
    small_sum = add_low(small_sum[0], other_half(small_sum[1]))
    small_sum = add_low(small_sum, swap(small_sum, 2))
    for mask in bit_masks(count)[:-4][::-1]:
        total = add_low(total, swap(total, mask))
        small_sum = add_low(small_sum, swap(small_sum, mask))
    small_sum = add_low(small_sum, swap(small_sum, 4))
    small_sum = add_low(small_sum, swap(small_sum, 8))
    total = double(total, 2)
    early = [
        lax.dynamic_slice_in_dim(x, shard * (x.shape[0] // 2), x.shape[0] // 2, 0).astype(f32)
        for x in early
    ]
    query_weight_grad = double(total, 1).astype(f32)
    small_grad = double(small_sum, 1).astype(f32)
    tokens_grad = unpack_call(table, tokens_grad) if plan else tokens_grad[0]
    output_weight_grad, up_weight_grad, down_weight_grad = early
    return (
        layer_out[None],
        tokens_grad[None],
        small_grad[:, pair],
        small_grad[:, pair + 1],
        small_grad[:, pair + padded : pair + padded + experts],
        query_weight_grad,
        small_grad[:, :head],
        small_grad[:, head:pair],
        output_weight_grad,
        small_grad[:, pair + 2],
        small_grad[:, pair + 3],
        up_weight_grad,
        small_grad[:, pair + 5 : pair + 5 + bias_columns].reshape(-1),
        down_weight_grad,
        small_grad[:, pair + 4],
    )


def solution(mesh):
    split = P("shard", "ctx", None)
    vector = P("shard")
    matrix = P("shard", None)
    in_specs = (
        split, split, vector, vector, matrix, matrix, matrix, matrix, matrix,
        vector, vector, matrix, vector, matrix, vector, split,
    )
    out_specs = (
        split, split, vector, vector, matrix, matrix, matrix, matrix, matrix,
        vector, vector, matrix, vector, matrix, vector,
    )
    return jax.shard_map(
        per_device, mesh=mesh, in_specs=in_specs, out_specs=out_specs, check_vma=False
    )
```

```python
import functools
import math

import jax
import jax.numpy as jnp
from jax import lax
from jax.experimental import pallas as pl
from jax.experimental.pallas import tpu as pltpu
from jax.sharding import PartitionSpec as P

PROMPT = 8192
CLEN = 1024
ROWS = 128
TILE = 256
FULL = 1024
PART = 256
HALF = PROMPT // 2
VMEM = 60 << 20

PIECES, IS_PROMPT, LOW_SLOT, HIGH_SLOT, OWN_SLOT, SHARD, CORE, SIDE, BASES = 0, 4, 5, 6, 7, 8, 9, 10, 11
norm_eps = 1e-05
mask_fill = -1e30
LOG2E = math.log2(math.e)
bf16 = jnp.bfloat16
f32 = jnp.float32


def dot(a, b):
    return lax.dot_general(a, b, (((1,), (0,)), ((), ())), preferred_element_type=f32)


def dot_tn(a, b):
    return lax.dot_general(a, b, (((0,), (0,)), ((), ())), preferred_element_type=f32)


def dot_nt(a, b):
    return lax.dot_general(a, b, (((1,), (1,)), ((), ())), preferred_element_type=f32)


def params(**kw):
    return pltpu.CompilerParams(vmem_limit_bytes=VMEM, **kw)


def cost(us):
    return pl.CostEstimate(flops=int(us * 1.15e9), transcendentals=0, bytes_accessed=0)


def whole(shape):
    return pl.BlockSpec(shape, lambda i: tuple(0 for _ in shape))


def column_norm(values):
    center = jnp.mean(values, axis=0, keepdims=True)
    centred = values - center
    spread = jnp.mean(centred * centred, axis=0, keepdims=True)
    inverse = lax.rsqrt(spread + norm_eps)
    return centred * inverse, inverse


def column_norm_back(grad, unit, inverse, gain):
    scaled = grad * gain
    inner = (
        scaled
        - jnp.mean(scaled, axis=0, keepdims=True)
        - unit * jnp.mean(scaled * unit, axis=0, keepdims=True)
    )
    return inner * inverse


def fold_lanes(values):
    width = values.shape[1]
    total = values[:, :128]
    for start in range(128, width, 128):
        total = total + values[:, start : start + 128]
    return total


def pick_piece(step, table_ref, sources, target_ref):
    if len(sources) == 1:
        target_ref[...] = sources[0][...]
        return
    keep, own, *got = sources
    rows = target_ref.shape[0]
    prompt = table_ref[IS_PROMPT] == 1
    which = ((step == 0), (step == 1) & jnp.logical_not(prompt), (step == 1) & prompt)
    for chosen, ref in zip(which + ((step == 2), (step == 3)), (keep, own, *got)):

        @pl.when(chosen)
        def _():
            target_ref[...] = ref[:rows, :]


def store_piece(step, targets, value):
    if len(targets) == 1:
        targets[0][...] = value
        return
    for k, ref in enumerate(targets):

        @pl.when(step == k)
        def _():
            ref[...] = value


def piece_specs(pieces):
    if len(pieces) == 1:
        return [pl.BlockSpec((TILE, pieces[0].shape[1]), lambda i, t: (i, 0))]
    return [pl.BlockSpec(x.shape, lambda i, t: (0, 0)) for x in pieces]


def pack_kernel(table_ref, *refs):
    rows_ref, *refs = refs
    index = refs.pop(0) if len(refs) > 4 else None
    for k, ref in enumerate(refs):
        span = pl.ds(pl.multiple_of(table_ref[PIECES + k] * PART, PART), PART)
        ref[:PART, :] = rows_ref[span, :]
        if index is not None:
            chosen = index[:, span].astype(f32)
            blank = jnp.zeros((16 - index.shape[0], PART), f32)
            ref[PART:, :] = jnp.concatenate(
                [jnp.concatenate([chosen, blank], axis=0)] * (ref.shape[1] // PART), axis=1
            ).astype(bf16)


def pack_call(table, rows, index=None):
    count, width = rows.shape
    out = (count // 4 + (0 if index is None else 16), width)
    inputs = (rows,) if index is None else (rows, index)
    return pl.pallas_call(
        pack_kernel,
        grid_spec=pltpu.PrefetchScalarGridSpec(
            num_scalar_prefetch=1,
            grid=(1,),
            in_specs=[pl.BlockSpec(x.shape, lambda i, t: (0, 0)) for x in inputs],
            out_specs=[pl.BlockSpec(out, lambda i, t: (0, 0))] * 4,
        ),
        out_shape=[jax.ShapeDtypeStruct(out, bf16)] * 4,
        compiler_params=params(),
        cost_estimate=cost(2),
        name="pack",
    )(table, *inputs)


def unpack_kernel(table_ref, keep_ref, own_ref, *refs):
    *got, out_ref = refs
    prompt = table_ref[IS_PROMPT] == 1
    place_of = lambda k: pl.ds(pl.multiple_of(table_ref[PIECES + k] * PART, PART), PART)
    out_ref[place_of(0), :] = keep_ref[...]
    out_ref[place_of(2), :] = got[1][...]
    out_ref[place_of(3), :] = got[2][...]

    @pl.when(prompt)
    def _():
        out_ref[place_of(1), :] = got[0][...]

    @pl.when(jnp.logical_not(prompt))
    def _():
        out_ref[place_of(1), :] = own_ref[...]


def unpack_call(table, pieces):
    rows, width = pieces[0].shape
    return pl.pallas_call(
        unpack_kernel,
        grid_spec=pltpu.PrefetchScalarGridSpec(
            num_scalar_prefetch=1,
            grid=(1,),
            in_specs=[pl.BlockSpec((rows, width), lambda i, t: (0, 0))] * 5,
            out_specs=pl.BlockSpec((4 * rows, width), lambda i, t: (0, 0)),
        ),
        out_shape=jax.ShapeDtypeStruct((4 * rows, width), bf16),
        compiler_params=params(),
        cost_estimate=cost(0),
        name="unpack",
    )(table, *pieces)


def first_kernel(pieces, table_ref, *refs):
    sources = refs[:pieces]
    gain_ref, shift_ref, kv_weight_ref = refs[pieces : pieces + 3]
    refs = refs[pieces + 3 :]
    step = pl.program_id(0)
    first_ref = refs[0]
    tokens_ref = refs[-1]
    pick_piece(step, table_ref, sources, tokens_ref)
    unit, _ = column_norm(tokens_ref[...].astype(f32).T)
    first = (unit * gain_ref[...] + shift_ref[...]).astype(bf16)
    first_ref[...] = first
    kv = dot_tn(kv_weight_ref[...], first).T.astype(bf16)
    if pieces == 1:
        refs[1][...] = kv
        return
    shared_ref, own_ref, index_ref, flat_ref, _ = refs[1:]
    flat_ref[...] = tokens_ref[...]
    topk, rows = index_ref.shape
    keep, own, *got = sources
    prompt = table_ref[IS_PROMPT] == 1
    which = ((step == 0), (step == 1) & jnp.logical_not(prompt), (step == 1) & prompt)
    for chosen, ref in zip(which + ((step == 2), (step == 3)), (keep, own, *got)):

        @pl.when(chosen)
        def _():
            index_ref[...] = ref[PART:, :rows][:topk, :].astype(f32).astype(jnp.int32)

    for slot, half in ((LOW_SLOT, 0), (HIGH_SLOT, 1)):

        @pl.when(step == table_ref[slot])
        def _():
            shared_ref[half * PART : (half + 1) * PART, :] = kv

    for half in range(2):

        @pl.when(step == table_ref[OWN_SLOT] + half)
        def _():
            own_ref[half * PART : (half + 1) * PART, :] = kv


def first_call(table, sources, count, topk, gain, shift, kv_weight):
    width, pair = kv_weight.shape
    keep = lambda shape: pl.BlockSpec(shape, lambda i, t: (0, 0))
    shape = jax.ShapeDtypeStruct
    split = len(sources) > 1
    outs = [(pl.BlockSpec((width, TILE), lambda i, t: (0, i)), shape((width, count), bf16))]
    rows = lambda n: pl.BlockSpec((TILE, n), lambda i, t: (i, 0))
    if split:
        outs += [
            (keep((2 * PART, pair)), shape((2 * PART, pair), bf16)),
            (keep((2 * PART, pair)), shape((2 * PART, pair), bf16)),
            (pl.BlockSpec((topk, TILE), lambda i, t: (0, i)), shape((topk, count), jnp.int32)),
            (rows(width), shape((count, width), bf16)),
        ]
    else:
        outs += [(rows(pair), shape((count, pair), bf16))]
    return pl.pallas_call(
        functools.partial(first_kernel, len(sources)),
        grid_spec=pltpu.PrefetchScalarGridSpec(
            num_scalar_prefetch=1,
            grid=(count // TILE,),
            in_specs=piece_specs(sources)
            + [keep((width, 1)), keep((width, 1)), keep((width, pair))],
            out_specs=[x for x, _ in outs],
            scratch_shapes=[pltpu.VMEM((TILE, width), bf16)],
        ),
        out_shape=[x for _, x in outs],
        compiler_params=params(),
        cost_estimate=cost(5),
        name="first_norm",
    )(table, *sources, gain, shift, kv_weight)


def join_rows(shard, own_ref, other_ref, all_ref, start=0):
    half = own_ref.shape[0]
    all_ref[pl.ds(pl.multiple_of(shard * half, half), half), :] = own_ref[...]
    rows = pl.ds(pl.multiple_of((1 - shard) * half, half), half)
    all_ref[rows, :] = other_ref[start : start + half, :]


def query_kernel(
    table_ref, first_ref, own_ref, other_ref, router_ref, index_ref,
    qt_ref, q_ref, gate_ref, query_weight_ref,
):
    topk = index_ref.shape[0]

    @pl.when(pl.program_id(0) == 0)
    def _():
        join_rows(table_ref[SHARD], own_ref, other_ref, query_weight_ref)

    head = qt_ref.shape[1]
    experts = query_weight_ref.shape[1] // head
    first = first_ref[...]
    projected = dot_tn(query_weight_ref[...], first)
    logits = dot_tn(router_ref[...], first)
    index = index_ref[...]
    picked = jnp.zeros(index.shape, f32)
    for expert in range(experts):
        picked = jnp.where(index == expert, logits[expert : expert + 1, :], picked)
    picked = jnp.exp(picked - jnp.max(picked, axis=0, keepdims=True))
    gate_ref[...] = picked / jnp.sum(picked, axis=0, keepdims=True)
    for part in range(TILE // ROWS):
        lanes = slice(part * ROWS, (part + 1) * ROWS)
        for j in range(topk):
            row = index[j : j + 1, lanes]
            chosen = jnp.zeros((head, ROWS), f32)
            for expert in range(experts):
                chosen = jnp.where(
                    row == expert, projected[expert * head : (expert + 1) * head, lanes], chosen
                )
            qt_ref[part, :, j * ROWS : (j + 1) * ROWS] = chosen.astype(bf16)
            q_ref[part, j * ROWS : (j + 1) * ROWS, :] = chosen.T.astype(bf16)


def query_call(table, first, own, other, router, index, head):
    width, count = first.shape
    topk = index.shape[0]
    tiles = count // ROWS
    per = TILE // ROWS
    keep = lambda shape: pl.BlockSpec(shape, lambda i, s: (0, 0))
    return pl.pallas_call(
        query_kernel,
        grid_spec=pltpu.PrefetchScalarGridSpec(
            num_scalar_prefetch=1,
            grid=(count // TILE,),
            in_specs=[
                pl.BlockSpec((width, TILE), lambda i, s: (0, i)),
                keep(own.shape),
                keep(other.shape),
                keep(router.shape),
                pl.BlockSpec((topk, TILE), lambda i, s: (0, i)),
            ],
            out_specs=[
                pl.BlockSpec((per, head, topk * ROWS), lambda i, s: (i, 0, 0)),
                pl.BlockSpec((per, topk * ROWS, head), lambda i, s: (i, 0, 0)),
                pl.BlockSpec((topk, TILE), lambda i, s: (0, i)),
            ],
            scratch_shapes=[pltpu.VMEM((width, own.shape[1]), bf16)],
        ),
        out_shape=[
            jax.ShapeDtypeStruct((tiles, head, topk * ROWS), bf16),
            jax.ShapeDtypeStruct((tiles, topk * ROWS, head), bf16),
            jax.ShapeDtypeStruct((topk, count), f32),
        ],
        compiler_params=params(),
        cost_estimate=cost(10),
        name="queries",
    )(table, first, own, other, router, index)


def tile_ranges(base):
    prompt = base < PROMPT
    begin = jnp.where(prompt, base // FULL * FULL, PROMPT)
    position = jnp.where(prompt, begin, PROMPT + (base - PROMPT) // CLEN * CLEN)
    parts = (base + ROWS - position + PART - 1) // PART
    return begin // FULL, begin, position, parts


def allowed_mask(position, base, width):
    key_pos = position + lax.broadcasted_iota(jnp.int32, (PART, width), 0)
    query_pos = base + lax.rem(lax.broadcasted_iota(jnp.int32, (PART, width), 1), ROWS)
    return key_pos <= query_pos


def for_slots(refs, table_ref, start, visit):
    slot = 0
    for ref in refs:
        for row in range(0, ref.shape[0], PART):
            place_of = pl.multiple_of(table_ref[start + slot] * PART, PART)
            visit(ref, row, pl.ds(place_of, PART))
            slot += 1


def attend_kernel(start, buffers, table_ref, *refs):
    sources = refs[:buffers]
    qt_ref = refs[buffers]
    out_ref, factor_ref, probs_ref = refs[buffers + 1 : buffers + 4]
    refs = refs[buffers + 4 :]
    kv_ref, vt_ref, knorm_ref, acc_ref, max_ref, full_ref, part_ref, full_sem, part_sem, done_ref = refs
    tile = pl.program_id(0)
    head, width = qt_ref.shape[1:]
    factor = LOG2E * head ** (-0.5)

    @pl.when(tile == 0)
    def _():
        knorm_ref[0] = 0.0
        done_ref[0] = 0
        done_ref[1] = 0

        def turn(ref, row, span):
            rows = ref[row : row + PART, :]
            kv_ref[span, :] = rows
            both = rows.T
            vt_ref[:head, span] = both[head:, :]
            vt_ref[head:, span] = jnp.ones((vt_ref.shape[0] - head, PART), bf16)
            keys = both[:head, :].astype(f32)
            most = jnp.max(jnp.sum(keys * keys, axis=0, keepdims=True))
            knorm_ref[0] = jnp.maximum(knorm_ref[0], most)

        for_slots(sources, table_ref, start, turn)

    base = table_ref[BASES + tile]
    steps, begin, position, parts = tile_ranges(base)
    query = qt_ref[0].astype(f32)
    qnorm = jnp.max(jnp.sum(query * query, axis=0, keepdims=True))
    narrow = qnorm * knorm_ref[0] * (factor * factor) < 60.0 * 60.0
    acc_ref[...] = jnp.zeros(acc_ref.shape, f32)
    max_ref[...] = jnp.zeros(max_ref.shape, f32)

    def writer(kind, buffer_ref, sem, span):
        count = done_ref[kind]
        slot = lax.rem(count, 2)
        copy = pltpu.make_async_copy(
            buffer_ref.at[slot], probs_ref.at[tile, span, :], sem.at[slot]
        )
        done_ref[kind] = count + 1

        @pl.when(count >= 2)
        def _():
            copy.wait()

        def write(probs):
            buffer_ref[slot] = probs
            copy.start()

        return write

    def span_of(offset, size):
        return pl.ds(pl.multiple_of(offset, size), size)

    def scores_of(span):
        return dot(kv_ref[span, :head], qt_ref[0]) * factor

    @pl.when(narrow)
    def _():
        def step(i, carry):
            span = span_of(i * FULL, FULL)
            write = writer(0, full_ref, full_sem, span)
            probs = jnp.exp2(scores_of(span)).astype(bf16)
            write(probs)
            acc_ref[...] += dot(vt_ref[:, span], probs)
            return carry

        def part(i, carry):
            span = span_of(begin + i * PART, PART)
            write = writer(1, part_ref, part_sem, span)
            mask = allowed_mask(position + i * PART, base, width)
            probs = jnp.exp2(jnp.where(mask, scores_of(span), mask_fill)).astype(bf16)
            write(probs)
            acc_ref[...] += dot(vt_ref[:, span], probs)
            return carry

        lax.fori_loop(0, steps, step, 0)
        lax.fori_loop(0, parts, part, 0)
        factor_ref[0] = 1.0 / acc_ref[head : head + 1, :]

    @pl.when(jnp.logical_not(narrow))
    def _():
        max_ref[...] = jnp.full(max_ref.shape, mask_fill, f32)
        count = steps * (FULL // PART) + parts

        def masked(i):
            before = i < steps * (FULL // PART)
            offset = i * PART
            span = span_of(offset, PART)
            shifted = jnp.where(before, -(1 << 24), position + offset - begin)
            mask = allowed_mask(shifted, base, width)
            return span, mask, jnp.where(mask, scores_of(span), mask_fill)

        def part(i, carry):
            span, mask, scores = masked(i)
            old = max_ref[...]
            new = jnp.maximum(old, jnp.max(scores, axis=0, keepdims=True))
            probs = jnp.where(mask, jnp.exp2(scores - new), 0.0).astype(bf16)
            acc_ref[...] = acc_ref[...] * jnp.exp2(old - new) + dot(vt_ref[:, span], probs)
            max_ref[...] = new
            return carry

        lax.fori_loop(0, count, part, 0)
        max_ref[...] = max_ref[...] + jnp.log2(acc_ref[head : head + 1, :])

        def again(i, carry):
            span, mask, scores = masked(i)
            write = writer(1, part_ref, part_sem, span)
            write(jnp.where(mask, jnp.exp2(scores - max_ref[...]), 0.0).astype(bf16))
            return carry

        lax.fori_loop(0, count, again, 0)
        factor_ref[0] = jnp.ones(max_ref.shape, f32)

    out_ref[0] = acc_ref[:head, :] / acc_ref[head : head + 1, :]

    @pl.when(tile == pl.num_programs(0) - 1)
    def _():
        for kind, buffer_ref, sem in ((0, full_ref, full_sem), (1, part_ref, part_sem)):
            for slot in range(2):

                @pl.when(done_ref[kind] > slot)
                def _():
                    rows = pl.ds(0, buffer_ref.shape[1])
                    pltpu.make_async_copy(
                        buffer_ref.at[slot], probs_ref.at[0, rows, :], sem.at[slot]
                    ).wait()


def attend_call(start, sources, table, qt):
    tiles, head, width = qt.shape
    total_keys = sum(x.shape[0] for x in sources)
    pair = sources[0].shape[1]
    one = lambda shape: pl.BlockSpec((1,) + shape, lambda i, t: (i, 0, 0))
    keep = lambda x: pl.BlockSpec(x.shape, lambda i, t: (0, 0))
    return pl.pallas_call(
        functools.partial(attend_kernel, start, len(sources)),
        grid_spec=pltpu.PrefetchScalarGridSpec(
            num_scalar_prefetch=1,
            grid=(tiles,),
            in_specs=[keep(x) for x in sources] + [one((head, width))],
            out_specs=[one((head, width)), one((1, width)), pl.BlockSpec(memory_space=pl.ANY)],
            scratch_shapes=[
                pltpu.VMEM((total_keys, pair), bf16),
                pltpu.VMEM((head + 16, total_keys), bf16),
                pltpu.SMEM((1,), f32),
                pltpu.VMEM((head + 16, width), f32),
                pltpu.VMEM((1, width), f32),
                pltpu.VMEM((2, FULL, width), bf16),
                pltpu.VMEM((2, PART, width), bf16),
                pltpu.SemaphoreType.DMA((2,)),
                pltpu.SemaphoreType.DMA((2,)),
                pltpu.SMEM((2,), jnp.int32),
            ],
        ),
        out_shape=[
            jax.ShapeDtypeStruct((tiles, head, width), f32),
            jax.ShapeDtypeStruct((tiles, 1, width), f32),
            jax.ShapeDtypeStruct((tiles, total_keys, width), bf16),
        ],
        compiler_params=params(),
        cost_estimate=cost(64),
        name="attend",
    )(table, *sources, qt)


def attend_back_kernel(start, buffers, table_ref, *refs):
    sources = refs[:buffers]
    q_ref, dot_ref, do_ref, delta_ref, probs_ref = refs[buffers : buffers + 5]
    refs = refs[buffers + 5 :]
    dq_ref = refs[0]
    outs = refs[1 : 1 + buffers]
    refs = refs[1 + buffers :]
    kv_ref, kt_ref, dkv_ref, rows_ref, full_ref, part_ref, full_sem, part_sem, done_ref = refs
    tile = pl.program_id(0)
    tiles = pl.num_programs(0)
    width, head = q_ref.shape[1:]
    scale = head ** (-0.5)

    @pl.when(tile == 0)
    def _():
        done_ref[0] = 0
        rows_ref[...] = jnp.zeros(rows_ref.shape, bf16)

        def turn(ref, row, span):
            rows = ref[row : row + PART, :]
            kv_ref[span, :] = rows
            kt_ref[:, span] = rows.T[:head, :]
            dkv_ref[span, :] = jnp.zeros((PART, 2 * head), f32)

        for_slots(sources, table_ref, start, turn)

    def steps_of(which):
        return tile_ranges(table_ref[BASES + jnp.clip(which, 0, tiles - 1)])[0]

    steps, begin, _, parts = tile_ranges(table_ref[BASES + tile])

    def full_copy(which, i, slot):
        rows = pl.ds(pl.multiple_of(i * FULL, FULL), FULL)
        return pltpu.make_async_copy(
            probs_ref.at[which, rows, :], full_ref.at[slot], full_sem.at[slot]
        )

    def part_copy(i):
        slot = lax.rem(i, 2)
        rows = pl.ds(pl.multiple_of(begin + i * PART, PART), PART)
        return pltpu.make_async_copy(
            probs_ref.at[tile, rows, :], part_ref.at[slot], part_sem.at[slot]
        )

    done = done_ref[0]

    @pl.when((steps > 0) & ((tile == 0) | (steps_of(tile - 1) == 0)))
    def _():
        full_copy(tile, 0, lax.rem(done, 2)).start()

    for i in range(2):

        @pl.when(i < parts)
        def _():
            part_copy(i).start()

    dq_ref[...] = jnp.zeros(dq_ref.shape, f32)
    rows_ref[:width, :head] = q_ref[0]
    rows_ref[width:, head:] = do_ref[0]

    def block(offset, size, probs):
        span = pl.ds(pl.multiple_of(offset, size), size)
        prob_grad = dot(kv_ref[span, head:], dot_ref[0])
        score_grad = (probs.astype(f32) * (prob_grad - delta_ref[0])).astype(bf16)
        dq_ref[0] += dot(kt_ref[:, span], score_grad)
        dkv_ref[span, :] += dot(jnp.concatenate([score_grad, probs], axis=1), rows_ref[...])

    def step(i, carry):
        slot = lax.rem(done + i, 2)

        @pl.when(i + 1 < steps)
        def _():
            full_copy(tile, i + 1, 1 - slot).start()

        @pl.when((i + 1 == steps) & (tile + 1 < tiles) & (steps_of(tile + 1) > 0))
        def _():
            full_copy(tile + 1, 0, 1 - slot).start()

        full_copy(tile, i, slot).wait()
        block(i * FULL, FULL, full_ref[slot])
        return carry

    def part(i, carry):
        part_copy(i).wait()
        block(begin + i * PART, PART, part_ref[lax.rem(i, 2)])

        @pl.when(i + 2 < parts)
        def _():
            part_copy(i + 2).start()

        return carry

    lax.fori_loop(0, steps, step, 0)
    lax.fori_loop(0, parts, part, 0)
    done_ref[0] = done + steps
    dq_ref[...] = dq_ref[...] * scale

    @pl.when(tile == tiles - 1)
    def _():
        lane = lax.broadcasted_iota(jnp.int32, (PART, 2 * head), 1)
        both = jnp.where(lane < head, scale, 1.0)

        def finish(ref, row, span):
            ref[row : row + PART, :] = (dkv_ref[span, :] * both).astype(ref.dtype)

        for_slots(outs, table_ref, start, finish)


def attend_back_call(start, sources, kinds, table, q, grad_t, grad, delta, probs):
    tiles, width, head = q.shape
    total_keys = sum(x.shape[0] for x in sources)
    pair = sources[0].shape[1]
    one = lambda shape: pl.BlockSpec((1,) + shape, lambda i, t: (i, 0, 0))
    keep = lambda x: pl.BlockSpec(x.shape, lambda i, t: (0, 0))
    return pl.pallas_call(
        functools.partial(attend_back_kernel, start, len(sources)),
        grid_spec=pltpu.PrefetchScalarGridSpec(
            num_scalar_prefetch=1,
            grid=(tiles,),
            in_specs=[keep(x) for x in sources]
            + [
                one((width, head)),
                one((head, width)),
                one((width, head)),
                one((1, width)),
                pl.BlockSpec(memory_space=pl.ANY),
            ],
            out_specs=[one((head, width))] + [keep(x) for x in sources],
            scratch_shapes=[
                pltpu.VMEM((total_keys, pair), bf16),
                pltpu.VMEM((head, total_keys), bf16),
                pltpu.VMEM((total_keys, pair), f32),
                pltpu.VMEM((2 * width, pair), bf16),
                pltpu.VMEM((2, FULL, width), bf16),
                pltpu.VMEM((2, PART, width), bf16),
                pltpu.SemaphoreType.DMA((2,)),
                pltpu.SemaphoreType.DMA((2,)),
                pltpu.SMEM((1,), jnp.int32),
            ],
        ),
        out_shape=[jax.ShapeDtypeStruct((tiles, head, width), f32)]
        + [jax.ShapeDtypeStruct(x.shape, kind) for x, kind in zip(sources, kinds)],
        compiler_params=params(),
        cost_estimate=cost(0),
        name="attend_back",
    )(table, *sources, q, grad_t, grad, delta, probs)


def place(index, pieces, expert):
    total = jnp.zeros(pieces[0].shape, f32)
    for j, piece in enumerate(pieces):
        total = jnp.where(index[j : j + 1, :] == expert, piece, total)
    return total


def middle_kernel(pieces, table_ref, *refs):
    sources = refs[:pieces]
    refs = refs[pieces:]
    outs = 4 if pieces > 1 else 1
    layer_out_refs = refs[MIDDLE_INPUTS : MIDDLE_INPUTS + outs]
    refs = refs[:MIDDLE_INPUTS] + refs[MIDDLE_INPUTS + outs :]
    middle_body(table_ref, sources, layer_out_refs, *refs)


MIDDLE_INPUTS = 14


def middle_body(
    table_ref,
    sources,
    layer_out_refs,
    tokens_ref,
    index_ref,
    gate_ref,
    attended_ref,
    factor_ref,
    output_own_ref,
    down_own_ref,
    both_other_ref,
    up_own_ref,
    up_other_ref,
    gain_ref,
    shift_ref,
    up_bias_ref,
    down_bias_ref,
    middle_grad_ref,
    grad_t_ref,
    grad_rows_ref,
    delta_ref,
    logit_grad_ref,
    output_weight_grad_ref,
    up_weight_grad_ref,
    down_weight_grad_ref,
    gain_grad_ref,
    shift_grad_ref,
    up_bias_grad_ref,
    down_bias_grad_ref,
    grad_ref,
    output_weight_ref,
    up_weight_ref,
    down_weight_ref,
    spread_ref,
    chosen_ref,
    dwo_ref,
    dup_ref,
    ddown_ref,
):
    step = pl.program_id(0)
    topk = index_ref.shape[0]
    head = attended_ref.shape[1]
    experts = output_weight_ref.shape[0] // head
    per = TILE // ROWS

    @pl.when(step == 0)
    def _():
        shard = table_ref[SHARD]
        join_rows(shard, output_own_ref, both_other_ref, output_weight_ref)
        join_rows(shard, down_own_ref, both_other_ref, down_weight_ref, output_own_ref.shape[0])
        join_rows(shard, up_own_ref, up_other_ref, up_weight_ref)
        for ref in (
            dwo_ref,
            dup_ref,
            ddown_ref,
            gain_grad_ref,
            shift_grad_ref,
            up_bias_grad_ref,
            down_bias_grad_ref,
        ):
            ref[...] = jnp.zeros(ref.shape, ref.dtype)

    pick_piece(step, table_ref, sources, grad_ref)
    index = index_ref[...]
    gate = gate_ref[...]
    for part in range(per):
        lanes = slice(part * ROWS, (part + 1) * ROWS)
        pieces = [
            attended_ref[part, :, j * ROWS : (j + 1) * ROWS] * gate[j : j + 1, lanes]
            for j in range(topk)
        ]
        for expert in range(experts):
            spread_ref[expert * head : (expert + 1) * head, lanes] = place(
                index[:, lanes], pieces, expert
            ).astype(bf16)

    middle = tokens_ref[...].astype(f32).T + dot_tn(output_weight_ref[...], spread_ref[...])
    unit, inverse = column_norm(middle)
    second = (unit * gain_ref[...] + shift_ref[...]).astype(bf16)
    pre = dot_tn(up_weight_ref[...], second) + up_bias_ref[...]
    coeff = math.sqrt(2.0 / math.pi)
    square = pre * pre
    wave = jnp.tanh(coeff * pre * (1.0 + 0.044715 * square))
    half = 0.5 * (1.0 + wave)
    hidden = (pre * half).astype(bf16)
    slope = half + 0.5 * pre * (1.0 - wave * wave) * (coeff * (1.0 + 3 * 0.044715 * square))
    result = middle + dot_tn(down_weight_ref[...], hidden) + down_bias_ref[...]
    store_piece(step, layer_out_refs, result.T.astype(bf16))

    grad_rows = grad_ref[...]
    grad_wide = grad_rows.astype(f32)
    grad_t = grad_wide.T
    ddown_ref[...] += dot(hidden, grad_rows)
    down_bias_grad_ref[...] += jnp.sum(grad_wide, axis=0, keepdims=True)
    pre_grad = (dot(down_weight_ref[...], grad_t.astype(bf16)) * slope).astype(bf16)
    dup_ref[...] += dot_nt(second, pre_grad)
    up_bias_grad_ref[...] += fold_lanes(pre_grad.astype(f32))
    second_grad = dot(up_weight_ref[...], pre_grad)
    gain_grad_ref[...] += fold_lanes(second_grad * unit)
    shift_grad_ref[...] += fold_lanes(second_grad)
    middle_grad = grad_t + column_norm_back(second_grad, unit, inverse, gain_ref[...])
    middle_grad_ref[...] = middle_grad
    middle_low = middle_grad.astype(bf16)
    dwo_ref[...] += dot_nt(spread_ref[...], middle_low)
    chosen_ref[...] = dot(output_weight_ref[...], middle_low)

    for part in range(per):
        lanes = slice(part * ROWS, (part + 1) * ROWS)
        picks = []
        for j in range(topk):
            span = slice(j * ROWS, (j + 1) * ROWS)
            row = index[j : j + 1, lanes]
            chosen = jnp.zeros((head, ROWS), f32)
            for expert in range(experts):
                chosen = jnp.where(
                    row == expert, chosen_ref[expert * head : (expert + 1) * head, lanes], chosen
                )
            attended = attended_ref[part, :, span]
            picks.append(jnp.sum(chosen * attended, axis=0, keepdims=True))
            back = (chosen * gate[j : j + 1, lanes]).astype(bf16).astype(f32)
            back = (back * factor_ref[part, :, span]).astype(bf16)
            grad_t_ref[part, :, span] = back
            back = back.astype(f32)
            grad_rows_ref[part, span, :] = back.T.astype(bf16)
            delta_ref[part, :, span] = jnp.sum(back * attended, axis=0, keepdims=True)
        gates = [gate[j : j + 1, lanes] for j in range(topk)]
        mean = sum(g * p for g, p in zip(gates, picks))
        rows = [g * (p - mean) for g, p in zip(gates, picks)]
        spare = logit_grad_ref.shape[0] - experts
        logit = [place(index[:, lanes], rows, expert) for expert in range(experts)]
        logit.append(jnp.zeros((spare, ROWS), f32))
        logit_grad_ref[:, lanes] = jnp.concatenate(logit, axis=0).astype(bf16)

    @pl.when(step == pl.num_programs(0) - 1)
    def _():
        output_weight_grad_ref[...] = dwo_ref[...].astype(bf16)
        up_weight_grad_ref[...] = dup_ref[...].astype(bf16)
        down_weight_grad_ref[...] = ddown_ref[...].astype(bf16)


def middle_call(
    table, sources, tokens, index, gate, attended, factor, weights,
    gain, shift, up_bias, down_bias, padded,
):
    count, width = tokens.shape
    topk = index.shape[0]
    tiles, head, wide = attended.shape
    per = TILE // ROWS
    spread = 2 * weights[0].shape[0]
    hidden = 2 * weights[1].shape[0]
    keep = lambda shape: pl.BlockSpec(shape, lambda i, s: tuple(0 for _ in shape))
    rows = pl.BlockSpec((TILE, width), lambda i, s: (i, 0))
    columns = lambda n: pl.BlockSpec((n, TILE), lambda i, s: (0, i))
    tile = lambda shape: pl.BlockSpec((per,) + shape, lambda i, s: (i, 0, 0))
    shape = jax.ShapeDtypeStruct
    if len(sources) > 1:
        outs = [(keep((TILE, width)), shape((TILE, width), bf16))] * 4
    else:
        outs = [(rows, shape((count, width), bf16))]
    outs += [
        (columns(width), shape((width, count), f32)),
        (tile((head, wide)), shape((tiles, head, wide), bf16)),
        (tile((wide, head)), shape((tiles, wide, head), bf16)),
        (tile((1, wide)), shape((tiles, 1, wide), f32)),
        (columns(padded), shape((padded, count), bf16)),
        (keep((spread, width)), shape((spread, width), bf16)),
        (keep((width, hidden)), shape((width, hidden), bf16)),
        (keep((hidden, width)), shape((hidden, width), bf16)),
        (keep((width, 128)), shape((width, 128), f32)),
        (keep((width, 128)), shape((width, 128), f32)),
        (keep((hidden, 128)), shape((hidden, 128), f32)),
        (keep((1, width)), shape((1, width), f32)),
    ]
    return pl.pallas_call(
        functools.partial(middle_kernel, len(sources)),
        grid_spec=pltpu.PrefetchScalarGridSpec(
            num_scalar_prefetch=1,
            grid=(count // TILE,),
            in_specs=piece_specs(sources)
            + [rows, columns(topk), columns(topk), tile((head, wide)), tile((1, wide))]
            + [keep(w.shape) for w in weights]
            + [keep((width, 1)), keep((width, 1)), keep((hidden, 1)), keep((width, 1))],
            out_specs=[x for x, _ in outs],
            scratch_shapes=[
                pltpu.VMEM((TILE, width), bf16),
                pltpu.VMEM((spread, width), bf16),
                pltpu.VMEM((width, hidden), bf16),
                pltpu.VMEM((hidden, width), bf16),
                pltpu.VMEM((spread, TILE), bf16),
                pltpu.VMEM((spread, TILE), f32),
                pltpu.VMEM((spread, width), f32),
                pltpu.VMEM((width, hidden), f32),
                pltpu.VMEM((hidden, width), f32),
            ],
        ),
        out_shape=[x for _, x in outs],
        compiler_params=params(),
        cost_estimate=cost(44),
        name="middle",
    )(table, *sources, tokens, index, gate, attended, factor, *weights,
      gain, shift, up_bias, down_bias)


def query_back_kernel(
    table_ref,
    first_ref,
    index_ref,
    dq_ref,
    own_ref,
    other_ref,
    logit_grad_ref,
    router_ref,
    partial_ref,
    keep_ref,
    send_ref,
    router_grad_ref,
    query_weight_ref,
    placed_ref,
    dwq_ref,
    dr_ref,
):
    step = pl.program_id(0)
    topk = index_ref.shape[0]
    head = dq_ref.shape[1]
    experts = query_weight_ref.shape[1] // head

    @pl.when(step == 0)
    def _():
        join_rows(table_ref[SHARD], own_ref, other_ref, query_weight_ref)
        dwq_ref[...] = jnp.zeros(dwq_ref.shape, f32)
        dr_ref[...] = jnp.zeros(dr_ref.shape, f32)

    index = index_ref[...]
    for part in range(TILE // ROWS):
        lanes = slice(part * ROWS, (part + 1) * ROWS)
        pieces = [dq_ref[part, :, j * ROWS : (j + 1) * ROWS] for j in range(topk)]
        for expert in range(experts):
            placed_ref[expert * head : (expert + 1) * head, lanes] = place(
                index[:, lanes], pieces, expert
            ).astype(bf16)
    first = first_ref[...]
    dwq_ref[...] += dot_nt(first, placed_ref[...])
    dr_ref[...] += dot_nt(first, logit_grad_ref[...])
    partial_ref[...] = dot(query_weight_ref[...], placed_ref[...]) + dot(
        router_ref[...], logit_grad_ref[...]
    )

    @pl.when(step == pl.num_programs(0) - 1)
    def _():
        router_grad_ref[...] = dr_ref[...]
        size = keep_ref.shape[2]
        shard, core, side = table_ref[SHARD], table_ref[CORE], table_ref[SIDE]
        for target, half in ((keep_ref, shard), (send_ref, 1 - shard)):
            for i, last in enumerate((core, 1 - core)):
                for j, part in enumerate((side, 1 - side)):
                    at = ((half * 2 + last) * 2 + part) * size
                    rows = pl.ds(pl.multiple_of(at, size), size)
                    target[i, j] = dwq_ref[rows, :].astype(bf16)


def query_back_call(table, first, index, dq, own, other, logit_grad, router):
    width, count = first.shape
    topk = index.shape[0]
    tiles, head, wide = dq.shape
    padded = router.shape[1]
    spread = own.shape[1]
    keep = lambda shape: pl.BlockSpec(shape, lambda i, s: tuple(0 for _ in shape))
    columns = lambda n: pl.BlockSpec((n, TILE), lambda i, s: (0, i))
    shape = jax.ShapeDtypeStruct
    quarters = (2, 2, width // 8, spread)
    return pl.pallas_call(
        query_back_kernel,
        grid_spec=pltpu.PrefetchScalarGridSpec(
            num_scalar_prefetch=1,
            grid=(count // TILE,),
            in_specs=[
                columns(width),
                columns(topk),
                pl.BlockSpec((TILE // ROWS, head, wide), lambda i, s: (i, 0, 0)),
                keep(own.shape),
                keep(other.shape),
                columns(padded),
                keep(router.shape),
            ],
            out_specs=[columns(width), keep(quarters), keep(quarters), keep(router.shape)],
            scratch_shapes=[
                pltpu.VMEM((width, spread), bf16),
                pltpu.VMEM((spread, TILE), bf16),
                pltpu.VMEM((width, spread), f32),
                pltpu.VMEM(router.shape, f32),
            ],
        ),
        out_shape=[
            shape((width, count), f32),
            shape(quarters, bf16),
            shape(quarters, bf16),
            shape(router.shape, f32),
        ],
        compiler_params=params(),
        cost_estimate=cost(0),
        name="query_back",
    )(table, first, index, dq, own, other, logit_grad, router)


def first_back_kernel(pieces, table_ref, *refs):
    tokens_ref, first_ref, partial_ref, middle_grad_ref = refs[:4]
    sources = refs[4 : 4 + pieces]
    kv_weight_ref, gain_ref, rest_ref = refs[4 + pieces : 7 + pieces]
    refs = refs[7 + pieces :]
    outs = 4 if pieces > 1 else 1
    tokens_grad_refs = refs[:outs]
    keep_ref, send_ref, total_ref, gain_grad_ref, shift_grad_ref, dkv_ref = refs[outs:]
    step = pl.program_id(0)
    pair = kv_weight_ref.shape[1]

    @pl.when(step == 0)
    def _():
        total_ref[:, :pair] = jnp.zeros((total_ref.shape[0], pair), f32)
        for ref in (gain_grad_ref, shift_grad_ref):
            ref[...] = jnp.zeros(ref.shape, ref.dtype)

    unit, inverse = column_norm(tokens_ref[...].astype(f32).T)
    if pieces == 1:
        dkv_ref[...] = sources[0][...]
    else:
        low_ref, high_ref, own_ref = sources
        own = table_ref[OWN_SLOT]
        for chosen, ref, half in (
            (table_ref[LOW_SLOT], low_ref, 0),
            (table_ref[HIGH_SLOT], high_ref, 0),
            (own, own_ref, 0),
            (own + 1, own_ref, 1),
        ):

            @pl.when(step == chosen)
            def _():
                dkv_ref[...] = ref[half * PART : (half + 1) * PART, :]

    dkv = dkv_ref[...]
    total_ref[:, :pair] += dot(first_ref[...], dkv)
    first_grad = partial_ref[...] + dot_nt(kv_weight_ref[...], dkv)
    gain_grad_ref[...] += fold_lanes(first_grad * unit)
    shift_grad_ref[...] += fold_lanes(first_grad)
    total = middle_grad_ref[...] + column_norm_back(first_grad, unit, inverse, gain_ref[...])
    store_piece(step, tokens_grad_refs, total.T.astype(bf16))

    @pl.when(step == pl.num_programs(0) - 1)
    def _():
        lane = lax.broadcasted_iota(jnp.int32, rest_ref.shape, 1)
        gains = jnp.sum(gain_grad_ref[...], axis=1, keepdims=True)
        shifts = jnp.sum(shift_grad_ref[...], axis=1, keepdims=True)
        rest = jnp.where(lane == 0, gains, jnp.where(lane == 1, shifts, rest_ref[...]))
        total_ref[:, pair:] = rest
        size = keep_ref.shape[1]
        shard, core = table_ref[SHARD], table_ref[CORE]
        for target, last in ((keep_ref, core), (send_ref, 1 - core)):
            for i, half in enumerate((shard, 1 - shard)):
                rows = pl.ds(pl.multiple_of((half * 2 + last) * size, size), size)
                target[i] = total_ref[rows, :].astype(bf16)


def first_back_call(table, tokens, first, partial, middle_grad, dkv, kv_weight, gain, rest):
    count, width = tokens.shape
    pair = kv_weight.shape[1]
    wide = pair + rest.shape[1]
    columns = lambda n: pl.BlockSpec((n, TILE), lambda i, t: (0, i))
    rows = lambda n: pl.BlockSpec((TILE, n), lambda i, t: (i, 0))
    keep = lambda shape: pl.BlockSpec(shape, lambda i, t: tuple(0 for _ in shape))
    shape = jax.ShapeDtypeStruct
    quarters = (2, width // 4, wide)
    if len(dkv) > 1:
        outs = [(keep((TILE, width)), shape((TILE, width), bf16))] * 4
    else:
        outs = [(rows(width), shape((count, width), bf16))]
    outs += [(keep(quarters), shape(quarters, bf16))] * 2
    return pl.pallas_call(
        functools.partial(first_back_kernel, len(dkv)),
        grid_spec=pltpu.PrefetchScalarGridSpec(
            num_scalar_prefetch=1,
            grid=(count // TILE,),
            in_specs=[rows(width), columns(width), columns(width), columns(width)]
            + piece_specs(dkv)
            + [keep(kv_weight.shape), keep((width, 1)), keep(rest.shape)],
            out_specs=[x for x, _ in outs],
            scratch_shapes=[
                pltpu.VMEM((width, wide), f32),
                pltpu.VMEM((width, 128), f32),
                pltpu.VMEM((width, 128), f32),
                pltpu.VMEM((TILE, pair), bf16),
            ],
        ),
        out_shape=[x for _, x in outs],
        compiler_params=params(),
        cost_estimate=cost(7),
        name="first_back",
    )(table, tokens, first, partial, middle_grad, *dkv, kv_weight, gain, rest)


def after(value, *others):
    return lax.optimization_barrier((value,) + others)[0]


def other_half(value):
    return lax.ppermute(value, "shard", [(0, 1), (1, 0)])


def join(value, other):
    low = lax.axis_index("shard") == 0
    return jnp.concatenate([jnp.where(low, value, other), jnp.where(low, other, value)], axis=0)


def swap(value, mask):
    count = lax.axis_size("ctx")
    return lax.ppermute(value, "ctx", [(i, i ^ mask) for i in range(count)])


def bit_masks(count):
    return [1 << k for k in reversed(range(count.bit_length() - 1))]


def key_orders(count):
    masks = bit_masks(count)
    return masks, masks[:1] + masks[1:-1][::-1] + masks[-1:]


def slots_of(masks):
    return [sum(m for k, m in enumerate(masks) if j >> k & 1) for j in range(1 << len(masks))]


def gather_keys(shared):
    low_order, high_order = key_orders(lax.axis_size("ctx"))
    got = swap(shared, low_order[0])
    low = jnp.concatenate([shared[:PART], got[:PART]], axis=0)
    high = jnp.concatenate([shared[PART:], got[PART:]], axis=0)
    for low_mask, high_mask in zip(low_order[1:-1], high_order[1:-1]):
        low_got, high_got = swap(low, low_mask), swap(high, high_mask)
        low = jnp.concatenate([low, low_got], axis=0)
        high = jnp.concatenate([high, high_got], axis=0)
    return (low, swap(low, low_order[-1])), (high, swap(high, high_order[-1]))


def add_low(a, b):
    return (a.astype(f32) + b.astype(f32)).astype(bf16)


def step_down(total, mask):
    half = total.shape[0] // 2
    return total[:half], swap(total[half:].astype(bf16), mask)


def double(total, mask):
    other = swap(total, mask)
    low = (lax.axis_index("ctx") // mask) % 2 == 0
    return jnp.concatenate([jnp.where(low, total, other), jnp.where(low, other, total)], axis=0)


def home_plan(count, block):
    half = count // 2
    if block != 4 * PART or block * half != PROMPT or block != CLEN or half % 2:
        return None
    sends = [None] * count
    hops = [[], [], []]
    for a in range(half // 2):
        b = half - 1 - a
        p, q = a + half, b + half
        sends[a], sends[b] = (0, 1, 2, 3), (2, 3, 0, 1)
        sends[p] = sends[q] = (0, 3, 1, 2)
        hops[0] += [(a, b), (b, a)]
        hops[1] += [(a, p), (p, a), (b, q), (q, b)]
        hops[2] += [(a, q), (b, p), (p, a), (q, b)]
    places = [[(i, sends[i][0]), (i, sends[i][1]), None, None] for i in range(count)]
    for k, hop in enumerate(hops):
        for source, target in hop:
            places[target][k + 1] = (source, sends[source][k + 1])
    return sends, hops, places


def plan_rows(plan, count):
    sends, _, places = plan
    lower, prompt = HALF // PART, PROMPT // PART
    where = [[source * 4 + quarter for source, quarter in row] for row in places]
    low_slot = [next(k for k in range(4) if row[k] < lower) for row in where]
    high_slot = [next(k for k in range(4) if lower <= row[k] < prompt) for row in where]
    own_slot = [2 if i < count // 2 else 0 for i in range(count)]
    own_at = [[row[k] % 4, row[k + 1] % 4] for row, k in zip(where, own_slot)]
    low_slots, high_slots = (slots_of(masks) for masks in key_orders(count))
    rows = []
    for i in range(count):
        row = list(sends[i]) + [int(i < count // 2), low_slot[i], high_slot[i], own_slot[i]]
        row += [0, i % 2, i // 2 % 2]
        row += [x * PART + r for x in where[i] for r in range(0, PART, ROWS)]
        row += [where[i ^ m][low_slot[i ^ m]] for m in low_slots]
        row += [where[i ^ m][high_slot[i ^ m]] for m in high_slots]
        row += [prompt + x for x in own_at[i] + own_at[i ^ (count // 2)]]
        rows.append(row)
    return rows


def send_pieces(pieces, plan):
    got = [lax.ppermute(piece, "ctx", hop) for piece, hop in zip(pieces[1:], plan[1])]
    return pieces[0], pieces[1], *got


def send_back(pieces, plan):
    hops = [[(t, s) for s, t in hop] for hop in plan[1]]
    got = [lax.ppermute(piece, "ctx", hop) for piece, hop in zip(pieces[1:], hops)]
    return pieces[0], pieces[1], *got


def per_device(
    tokens,
    expert_index,
    first_gain,
    first_shift,
    router_weight,
    query_weight,
    key_weight,
    value_weight,
    output_weight,
    second_gain,
    second_shift,
    up_weight,
    up_bias,
    down_weight,
    down_bias,
    out_grad,
):
    groups, block, width = tokens.shape
    assert groups == 1 and lax.axis_size("shard") == 2
    count = lax.axis_size("ctx")
    me = lax.axis_index("ctx")
    shard = lax.axis_index("shard")
    experts = router_weight.shape[1]
    topk = expert_index.shape[-1]
    head = key_weight.shape[1]
    pair = 2 * head
    padded = 32
    tiles = block // ROWS
    key_table = BASES + tiles
    plan = home_plan(count, block)
    if plan:
        table = jnp.array(plan_rows(plan, count), jnp.int32)[me]
        table = table + shard * (jnp.arange(table.shape[0], dtype=jnp.int32) == SHARD)
        packed = pack_call(table, tokens[0], expert_index[0].T)
        sources = send_pieces(packed, plan)
        key_weight, packed = lax.optimization_barrier((key_weight, packed))
    else:
        base = me * block
        numbers = [0, 0, 0, 0, 0, 0, 0, 0, shard, me % 2, me // 2 % 2]
        table = jnp.concatenate(
            [
                jnp.stack([jnp.int32(x) for x in numbers]),
                base + jnp.arange(tiles, dtype=jnp.int32) * ROWS,
                jnp.arange((PROMPT + CLEN) // PART, dtype=jnp.int32),
            ]
        )
        sources = (tokens[0],)

    spare = jnp.zeros((key_weight.shape[0], padded - experts), bf16)
    vectors = [first_gain, first_shift, second_gain, second_shift, down_bias]
    half_width = width // 2
    small = jnp.concatenate(
        [key_weight, value_weight, router_weight, spare]
        + [v[:, None] for v in vectors]
        + [up_bias.reshape(half_width, -1)],
        axis=1,
    )
    small = join(small, other_half(small))
    query_other = other_half(after(query_weight, small))
    kv_weight = small[:, :pair]
    router = small[:, pair : pair + padded]
    at = pair + padded
    columns = [small[:, at + i : at + i + 1].astype(f32) for i in range(len(vectors))]
    gain_one, shift_one, gain_two, shift_two, down_bias_all = columns
    up_bias_all = small[:, at + len(vectors) :].reshape(-1, 1).astype(f32)

    both_weights = jnp.concatenate([output_weight, down_weight], axis=0)
    early_work = (both_weights, router, up_bias_all, *columns)
    if plan:
        grads = pack_call(after(table, small), out_grad[0])
        early_work += tuple(grads)
    table, early_work = lax.optimization_barrier((table, early_work))
    both_weights, router, up_bias_all, *rest = early_work
    gain_one, shift_one, gain_two, shift_two, down_bias_all = rest[: len(vectors)]
    grads = rest[len(vectors) :]
    first_out = first_call(table, sources, block, topk, gain_one, shift_one, kv_weight)
    if plan:
        first, shared, own, index, flat = first_out
        low_keys, high_keys = gather_keys(shared)
        partner = swap(own, count // 2)
        high_keys += (own, partner)
    else:
        first, kv = first_out
        flat = tokens[0]
        index = expert_index[0].T
        gathered = lax.all_gather(kv, "ctx", axis=0, tiled=True)
        segment = jnp.maximum(base, PROMPT) // CLEN * CLEN
        own = lax.dynamic_slice_in_dim(gathered, segment, CLEN, 0)
        quarter = HALF // 2
        low_keys = (gathered[:quarter], gathered[quarter:HALF])
        high_keys = (
            gathered[HALF : HALF + quarter], gathered[HALF + quarter : PROMPT],
            own[: CLEN // 2], own[CLEN // 2 :],
        )

    qt, q, gate = query_call(table, first, query_weight, query_other, router, index, head)
    both_other = other_half(after(both_weights, query_other))
    weights = (
        output_weight, down_weight, both_other, up_weight, other_half(after(up_weight, query_other))
    )
    if plan:
        grads = send_pieces(after(tuple(grads), *low_keys, *high_keys), plan)
    else:
        grads = (out_grad[0],)
    keys = low_keys + high_keys
    attended, factor, probs = attend_call(key_table, keys, table, qt)
    outs = 4 if plan else 1
    middle = middle_call(
        table, grads, flat, index, gate, attended, factor, weights,
        gain_two, shift_two, up_bias_all, down_bias_all, padded,
    )
    layer_out = middle[:outs]
    (
        middle_grad, grad_t, grad_rows, delta, logit_grad,
        output_weight_grad, up_weight_grad, down_weight_grad,
        second_gain_grad, second_shift_grad, up_bias_grad, down_bias_grad,
    ) = middle[outs:]

    early = lax.psum((output_weight_grad, up_weight_grad, down_weight_grad), ("ctx", "shard"))
    if plan:
        layer_out = send_back(layer_out, plan)
    kinds = (f32, bf16, f32, bf16, f32, bf16) if plan else (bf16,) * 6
    dq, *key_grads = attend_back_call(
        key_table, keys, kinds, table, q, grad_t, grad_rows, delta, probs
    )
    dq, key_grads, layer_out = lax.optimization_barrier((dq, key_grads, layer_out))
    if plan:
        low_near, low_far, high_near, high_far, own_near, own_far = key_grads
        low_got, high_got = swap(low_far, 1), swap(high_far, 1)
    partial, keep, send, router_grad = query_back_call(
        table, first, index, dq, query_weight, query_other, logit_grad, router
    )
    sums = (second_gain_grad, second_shift_grad, down_bias_grad, up_bias_grad)
    router_grad, layer_out, *sums = lax.optimization_barrier((router_grad, layer_out, *sums))
    second_gain_grad, second_shift_grad, down_bias_grad, up_bias_grad = sums
    layer_out = unpack_call(table, layer_out) if plan else layer_out[0]
    rest = jnp.concatenate(
        [
            jnp.zeros((width, 2), f32),
            jnp.sum(second_gain_grad, axis=1)[:, None],
            jnp.sum(second_shift_grad, axis=1)[:, None],
            down_bias_grad[0][:, None],
            jnp.sum(up_bias_grad, axis=1).reshape(width, -1),
        ],
        axis=1,
    )
    bias_columns = rest.shape[1] - 5
    rest = jnp.pad(rest, ((0, 0), (0, padded - rest.shape[1])))
    rest = jnp.concatenate([rest, router_grad, jnp.zeros((width, 128 - 2 * padded), f32)], axis=1)
    total = add_low(keep, other_half(send))
    if plan:
        low_order, high_order = key_orders(count)
        low_keep, low_got = step_down(low_near + low_got.astype(f32), low_order[2])
        high_keep, high_got = step_down(high_near + high_got.astype(f32), high_order[2])
        total, rest, layer_out, *early = lax.optimization_barrier(
            (total, rest, layer_out, *early)
        )
        query_got = swap(total[1], 1)
    if plan:
        low_got, high_got, total, own_far = lax.optimization_barrier(
            (low_got, high_got, total, own_far)
        )
        own_got = swap(own_far, count // 2)
        low_keep, low_got = step_down(low_keep + low_got.astype(f32), low_order[1])
        high_keep, high_got = step_down(high_keep + high_got.astype(f32), high_order[1])
        low_got, high_got, query_got = lax.optimization_barrier((low_got, high_got, query_got))
        total = add_low(total[0], query_got)
        query_got = swap(total[1], 2)
        low_sum = low_keep + low_got.astype(f32)
        high_sum = high_keep + high_got.astype(f32)
        both = jnp.concatenate([low_sum[PART:], high_sum[PART:]], axis=0).astype(bf16)
        both = swap(both, low_order[0])
        both, query_got = lax.optimization_barrier((both, query_got))
        dkv = (
            add_low(low_sum[:PART], both[:PART]),
            add_low(high_sum[:PART], both[PART:]),
            add_low(own_near, own_got),
        )
    else:
        rows = count * block - PROMPT
        dall = jnp.concatenate(key_grads[:4] + [jnp.zeros((rows, pair), bf16)])
        own_grad = jnp.concatenate(key_grads[4:])
        own_grad = jnp.where(base >= PROMPT, own_grad, jnp.zeros_like(own_grad))
        dall = lax.dynamic_update_slice_in_dim(dall, own_grad, segment, 0)
        dkv = (lax.psum_scatter(dall, "ctx", scatter_dimension=0, tiled=True),)
        total = add_low(total[0], swap(total[1], 1))
        query_got = swap(total[1], 2)
    total = add_low(total[0], query_got)
    query_got = swap(total, 4)
    done = first_back_call(
        table, flat, first, partial, middle_grad, dkv, kv_weight, gain_one, rest
    )
    tokens_grad = done[:outs]
    (keep, send), early, query_got = lax.optimization_barrier((done[outs:], early, query_got))
    if plan:
        tokens_grad = send_back(tokens_grad, plan)
    total = add_low(total, query_got)
    small_sum = add_low(keep, swap(send, 1))
    total = add_low(total, swap(total, 8))
    small_sum = add_low(small_sum[0], other_half(small_sum[1]))
    small_sum = add_low(small_sum, swap(small_sum, 2))
    for mask in bit_masks(count)[:-4][::-1]:
        total = add_low(total, swap(total, mask))
        small_sum = add_low(small_sum, swap(small_sum, mask))
    small_sum = add_low(small_sum, swap(small_sum, 4))
    small_sum = add_low(small_sum, swap(small_sum, 8))
    total = double(total, 2)
    early = [
        lax.dynamic_slice_in_dim(x, shard * (x.shape[0] // 2), x.shape[0] // 2, 0).astype(f32)
        for x in early
    ]
    query_weight_grad = double(total, 1).astype(f32)
    small_grad = double(small_sum, 1).astype(f32)
    tokens_grad = unpack_call(table, tokens_grad) if plan else tokens_grad[0]
    output_weight_grad, up_weight_grad, down_weight_grad = early
    return (
        layer_out[None],
        tokens_grad[None],
        small_grad[:, pair],
        small_grad[:, pair + 1],
        small_grad[:, pair + padded : pair + padded + experts],
        query_weight_grad,
        small_grad[:, :head],
        small_grad[:, head:pair],
        output_weight_grad,
        small_grad[:, pair + 2],
        small_grad[:, pair + 3],
        up_weight_grad,
        small_grad[:, pair + 5 : pair + 5 + bias_columns].reshape(-1),
        down_weight_grad,
        small_grad[:, pair + 4],
    )


def solution(mesh):
    split = P("shard", "ctx", None)
    vector = P("shard")
    matrix = P("shard", None)
    in_specs = (
        split, split, vector, vector, matrix, matrix, matrix, matrix, matrix,
        vector, vector, matrix, vector, matrix, vector, split,
    )
    out_specs = (
        split, split, vector, vector, matrix, matrix, matrix, matrix, matrix,
        vector, vector, matrix, vector, matrix, vector,
    )
    return jax.shard_map(
        per_device, mesh=mesh, in_specs=in_specs, out_specs=out_specs, check_vma=False
    )
```
